128 devices in a mesh: dp: 2 (over core), gx: 8 (over y, z_lo), gy: 8 (over x, z_hi).
Axes of the slice: x: 4, y: 4, z: 4 (z_hi: 2, z_lo: 2; z = z_hi * 2 + z_lo), core: 2. Of those that a mesh axis runs over, the one named last changes fastest.
Arguments:
- state_now: bfloat16 [2, 8, 32, 192, 128], P('dp', None, 'gx', 'gy'), may hold values from -6 to 6
- enc_pre: bfloat16 [2, 32, 32, 192, 128], P('dp', None, 'gx', 'gy'), may hold values from -8 to 8
- mid_pre: bfloat16 [2, 64, 16, 96, 64], P('dp', None, 'gx', 'gy'), may hold values from -8 to 8
- dec_pre: bfloat16 [2, 32, 32, 192, 128], P('dp', None, 'gx', 'gy'), may hold values from -8 to 8
- cotangent: bfloat16 [2, 8, 32, 192, 128], P('dp', None, 'gx', 'gy'), may hold values from -6 to 6
- enc_kernel: bfloat16 [32, 8, 3, 3, 3], replicated, may hold values from -0.4375 to 0.4375
- mid_kernel: bfloat16 [64, 32, 3, 3, 3], replicated, may hold values from -0.21875 to 0.21875
- dec_kernel: bfloat16 [32, 96, 3, 3, 3], replicated, may hold values from -0.125 to 0.125
- out_kernel: bfloat16 [8, 32], replicated, may hold values from -1 to 1
Outputs:
- state_grad: bfloat16 [2, 8, 32, 192, 128], P('dp', None, 'gx', 'gy')
- enc_grad: float32 [32, 8, 3, 3, 3], replicated
- mid_grad: float32 [64, 32, 3, 3, 3], replicated
- dec_grad: float32 [32, 96, 3, 3, 3], replicated
- out_grad: float32 [8, 32], replicated
The draws below stay inside these ranges and needn't reach their ends.
All inputs are finite; a program needn't handle non-finite values.
Results may differ from the reference program's by a relative error of at most 0.0069.
Values may be sent and summed in bfloat16 or wider, within the bound.
No kernel may reach another device: no remote copies, remote signals or barrier semaphores. Data moves between devices by JAX's collectives and lax.ppermute only.
A program may use at most 128 MiB of HBM per device.

```python
import math
import jax
import jax.numpy as jnp
from jax import lax

IN = 8
C0 = 32
C1 = 64
Z = 128
BATCH = 2
NX = 32
NY = 192


def levels(own_key, shape, cuts, smallest, top_value):
    loudness = 1.0
    for position, parts in cuts:
        steps = jax.random.uniform(jax.random.fold_in(jax.random.fold_in(own_key, 6), position), (parts,), jnp.float32, smallest / len(cuts), top_value / len(cuts))
        loudness = loudness * jnp.repeat(jnp.exp(steps), shape[position] // parts).reshape((-1,) + (1,) * (len(shape) - 1 - position))
    return loudness


def scatter_about(key, shape, deviation, reach, pieces=(), kind=jnp.bfloat16):
    entries = jax.random.normal(key, shape, jnp.float32) * deviation
    if len(pieces) > 0:
        entries = levels(key, shape, pieces, -0.22, 0.18) * entries
    return jnp.clip(entries, min=-reach, max=reach).astype(kind)


def setup_inputs(seed: int = 0) -> dict:
    streams_of = jax.random.split(jax.random.key(seed), 10)
    state_now = scatter_about(streams_of[0], (BATCH, IN, NX, NY, Z), 1.0, 6.0, ((0, 2), (2, 8), (3, 8)))
    enc_pre = scatter_about(streams_of[1], (BATCH, C0, NX, NY, Z), 1.5, 8.0, ((0, 2), (2, 8), (3, 8)))
    mid_pre = scatter_about(streams_of[2], (BATCH, C1, NX // 2, NY // 2, Z // 2), 1.5, 8.0, ((0, 2), (2, 8), (3, 8)))
    dec_pre = scatter_about(streams_of[3], (BATCH, C0, NX, NY, Z), 1.5, 8.0, ((0, 2), (2, 8), (3, 8)))
    cotangent = scatter_about(streams_of[4], (BATCH, IN, NX, NY, Z), 1.0, 6.0, ((0, 2), (2, 8), (3, 8)))
    enc_kernel = scatter_about(streams_of[5], (C0, IN, 3, 3, 3), (27 * IN) ** -0.5, 0.4375)
    mid_kernel = scatter_about(streams_of[6], (C1, C0, 3, 3, 3), (27 * C0) ** -0.5, 0.21875)
    dec_kernel = scatter_about(streams_of[7], (C0, C1 + C0, 3, 3, 3), (27 * (C1 + C0)) ** -0.5, 0.125)
    out_kernel = scatter_about(streams_of[8], (IN, C0), C0 ** -0.5, 1.0)
    return dict(state_now=state_now, enc_pre=enc_pre, mid_pre=mid_pre, dec_pre=dec_pre, cotangent=cotangent, enc_kernel=enc_kernel, mid_kernel=mid_kernel, dec_kernel=dec_kernel, out_kernel=out_kernel)


def apply_conv(values, kernel, pads):
    return lax.conv_general_dilated(values, kernel, (1, 1, 1), pads, dimension_numbers=('NCDHW', 'OIDHW', 'NCDHW'), preferred_element_type=jnp.float32)

def kernel_grad(values, delta, pads):
    return lax.conv_general_dilated(values, delta, (1, 1, 1), pads, dimension_numbers=('CNDHW', 'IODHW', 'CNDHW'), preferred_element_type=jnp.float32)

def flip_kernel(kernel):
    return jnp.transpose(jnp.flip(kernel, (2, 3, 4)), (1, 0, 2, 3, 4))

def silu_slope(values):
    sig = jax.nn.sigmoid(values)
    return sig * (1.0 + values * (1.0 - sig))

def block_sum(values):
    shape = values.shape
    split = values.reshape(shape[0], shape[1], shape[2] // 2, 2, shape[3] // 2, 2, shape[4] // 2, 2)
    return lax.optimization_barrier(jnp.sum(split, axis=(3, 5, 7)))

def upsample(values):
    return jnp.repeat(jnp.repeat(jnp.repeat(values, 2, axis=2), 2, axis=3), 2, axis=4)

def reference(state_now, enc_pre, mid_pre, dec_pre, cotangent, enc_kernel, mid_kernel, dec_kernel, out_kernel):
    all_pad = ((1, 1), (1, 1), (1, 1))
    enc_wide = enc_pre.astype(jnp.float32)
    mid_wide = mid_pre.astype(jnp.float32)
    dec_wide = dec_pre.astype(jnp.float32)
    hidden_enc = jax.nn.silu(enc_wide).astype(jnp.bfloat16)
    pooled = (block_sum(hidden_enc.astype(jnp.float32)) * 0.125).astype(jnp.bfloat16)
    hidden_mid = jax.nn.silu(mid_wide).astype(jnp.bfloat16)
    joined = jnp.concatenate([upsample(hidden_mid), hidden_enc], axis=1)
    decoded = jax.nn.silu(dec_wide).astype(jnp.bfloat16)
    grad_scale = 1.0 / math.sqrt(BATCH * NX * NY * Z)
    out_grad = jnp.einsum('boxyz,bcxyz->oc', cotangent.astype(jnp.float32), decoded.astype(jnp.float32))
    dec_back = jnp.einsum('oc,boxyz->bcxyz', out_kernel.astype(jnp.float32), cotangent.astype(jnp.float32))
    dec_delta = (dec_back * silu_slope(dec_wide)).astype(jnp.bfloat16)
    dec_grad = kernel_grad(joined, dec_delta, all_pad)
    joined_back = apply_conv(dec_delta, flip_kernel(dec_kernel), all_pad)
    wide_mid = joined_back.shape[1] - enc_pre.shape[1]
    mid_delta = (block_sum(joined_back[:, :wide_mid]) * silu_slope(mid_wide)).astype(jnp.bfloat16)
    mid_grad = kernel_grad(pooled, mid_delta, all_pad)
    pool_back = apply_conv(mid_delta, flip_kernel(mid_kernel), all_pad)
    enc_delta = ((joined_back[:, wide_mid:] + upsample(pool_back) * 0.125) * silu_slope(enc_wide)).astype(jnp.bfloat16)
    enc_grad = kernel_grad(state_now, enc_delta, all_pad)
    state_grad = (cotangent.astype(jnp.float32) + apply_conv(enc_delta, flip_kernel(enc_kernel), all_pad)).astype(jnp.bfloat16)
    return (state_grad, enc_grad * grad_scale, mid_grad * grad_scale, dec_grad * grad_scale, out_grad * grad_scale)
```

```python
import functools
import math

import jax
import jax.numpy as jnp
import numpy as np
from jax import lax
from jax.experimental import pallas as pl
from jax.experimental.pallas import tpu as pltpu
from jax.sharding import PartitionSpec as P

F32 = jnp.float32
BF16 = jnp.bfloat16


VMEM = pl.BlockSpec(memory_space=pltpu.VMEM)
HBM = pl.BlockSpec(memory_space=pltpu.HBM)


def call(body, outs, scratch, args, flops, limit, far=0, far_outs=0):
    return pl.pallas_call(
        body,
        out_shape=outs,
        in_specs=[HBM] * far + [VMEM] * (len(args) - far),
        out_specs=[HBM] * far_outs + [VMEM] * (len(outs) - far_outs),
        scratch_shapes=scratch,
        compiler_params=pltpu.CompilerParams(vmem_limit_bytes=limit << 20),
        cost_estimate=pl.CostEstimate(flops=flops, bytes_accessed=4 << 20, transcendentals=0),
    )(*args)


def fetch(pairs, sems):
    copies = [pltpu.make_async_copy(src, dst, sems.at[i]) for i, (src, dst) in enumerate(pairs)]
    for copy in copies:
        copy.start()
    return [copy.wait for copy in copies]


def sds(shape, dtype):
    return jax.ShapeDtypeStruct(shape, dtype)


def dot(a, b):
    return lax.dot_general(a, b, (((1,), (0,)), ((), ())), preferred_element_type=F32)


def dot_tn(a, b):
    return lax.dot_general(a, b, (((0,), (0,)), ((), ())), preferred_element_type=F32)


def dot_nt(a, b):
    return lax.dot_general(a, b, (((1,), (1,)), ((), ())), preferred_element_type=F32)


def sigmoid(v):
    return 0.5 + 0.5 * jnp.tanh(0.5 * v)


def slope(v, s):
    return s * (1.0 + v * (1.0 - s))


def lane_ids(shape):
    return lax.broadcasted_iota(jnp.int32, shape, len(shape) - 1)


def shifts(v, period):
    lane = jnp.bitwise_and(lane_ids(v.shape), period - 1)
    axis = v.ndim - 1
    size = v.shape[-1]
    back = jnp.where(lane == period - 1, 0.0, pltpu.roll(v, size - 1, axis))
    ahead = jnp.where(lane == 0, 0.0, pltpu.roll(v, 1, axis))
    return back, v, ahead


def delta_plane(dec, cot, head):
    pre = jnp.swapaxes(dec.astype(F32), 0, 1)
    cot = jnp.swapaxes(cot.astype(F32), 0, 1)
    cot_lanes = jnp.concatenate([cot[y] for y in range(24)], axis=1).astype(BF16)
    back = dot_tn(head, cot_lanes)
    back = jnp.stack([back[:, y * 128 : y * 128 + 128] for y in range(24)], axis=0)
    s = sigmoid(pre)
    return (back * slope(pre, s)).astype(BF16), cot_lanes, pre * s


def face_body(dec_far, cot_far, head_far, low_far, high_far, dec_ref, cot_ref, head_ref, delta_ref, sems, out_sems):
    planes = (0, 3)
    pairs = [(head_far, head_ref)]
    for i, x in enumerate(planes):
        pairs += [(cot_far.at[:, x], cot_ref.at[i]), (dec_far.at[:, x], dec_ref.at[i])]
    waits = fetch(pairs, sems)
    waits[0]()
    writes = []
    for i, far in enumerate((low_far, high_far)):
        waits[2 * i + 1]()
        waits[2 * i + 2]()
        delta_ref[i] = delta_plane(dec_ref[i], cot_ref[i], head_ref[...])[0]
        writes += fetch([(delta_ref.at[i], far)], out_sems.at[i])
    for wait in writes:
        wait()


def forward_body(
    dec_ref, cot_ref, head_ref, enc_ref, state_ref, mid_ref, pool_ref,
    delta_ref, head_grad_ref, hid_ref, slope_ref, pooled_ref, hmid_ref, mslope_ref, st_ref, ylo_ref, yhi_ref, xlo_ref, xhi_ref,
):
    total = jnp.zeros((8, 32), F32)
    for x in range(4):
        delta, cot_lanes, decoded = delta_plane(dec_ref[:, x], cot_ref[:, x], head_ref[...])
        if x in (1, 2):
            delta_ref[x - 1] = delta
        decoded = jnp.concatenate([decoded[y] for y in range(24)], axis=1).astype(BF16)
        total = total + dot_nt(cot_lanes, decoded)
    head_grad_ref[...] = total
    low_rows, high_rows = [], []
    for x in range(4):
        pre = jnp.swapaxes(enc_ref[:, x].astype(F32), 0, 1)
        s = sigmoid(pre)
        hid_ref[x] = (pre * s).astype(BF16)
        slope_ref[x] = slope(pre, s)
        state = jnp.swapaxes(state_ref[:, x].astype(F32), 0, 1)
        st_ref[x] = state
        low_rows.append(state[0])
        high_rows.append(state[23])
    ylo_ref[64:96, :] = jnp.concatenate(low_rows, axis=0).astype(BF16)
    yhi_ref[64:96, :] = jnp.concatenate(high_rows, axis=0).astype(BF16)
    tilts = {}
    for bx in range(2):
        for m in range(6):
            acc = None
            for ex in range(2):
                for ey in range(2):
                    pair = jnp.concatenate(
                        [hid_ref[2 * bx + ex, 4 * m + ey], hid_ref[2 * bx + ex, 4 * m + 2 + ey]], axis=1
                    )
                    part = dot(pair, pool_ref[:, 128:256])
                    acc = part if acc is None else acc + part
            pooled = (acc * 0.125).astype(BF16)
            pooled_ref[bx, m] = pooled
            side_ref = xlo_ref if bx == 0 else xhi_ref
            side_ref[m * 32 : m * 32 + 32, :] = pooled
            pre = mid_ref[bx, m].astype(F32)
            s = sigmoid(pre)
            hmid_ref[bx, m] = (pre * s).astype(BF16)
            tilts[bx, m] = slope(pre, s)
            mslope_ref[bx, m] = tilts[bx, m]
    lower = lane_ids((64, 128)) < 64
    ylo_ref[0:64, :] = jnp.where(lower, tilts[0, 0], pltpu.roll(tilts[1, 0], 64, 1)).astype(BF16)
    yhi_ref[0:64, :] = jnp.where(lower, pltpu.roll(tilts[0, 5], 64, 1), tilts[1, 5]).astype(BF16)


def window_sums(rows_of, pool, put):
    got = dot(
        jnp.concatenate([jnp.concatenate([rows_of(x, j) for j in range(4)], axis=0) for x in range(6)], axis=0), pool
    )
    sums = []
    for x in range(6):
        at = [got[x * 128 + j * 32 : x * 128 + j * 32 + 32] for j in range(4)]
        sums.append([at[j] + at[j + 1] for j in (2, 1, 0)])
    for bx in range(2):
        for a, kx in enumerate((-1, 0, 1)):
            for b in range(3):
                both = (sums[2 * bx - kx + 1][b] + sums[2 * bx - kx + 2][b]).astype(BF16)
                for c in range(3):
                    put(bx, ((a * 3 + b) * 3 + c) * 32, both[:, c * 128 : c * 128 + 128])


def stack_of(row):
    return jnp.concatenate(
        [jnp.concatenate([row(x + 1 - kx) for x in range(4)], axis=1) for kx in (-1, 0, 1)], axis=0
    )


def skip_weights(w_ref):
    parts = [
        jnp.concatenate([w_ref[a, b].astype(F32).reshape(96, 96)[:, 64:96] for b in range(3)], axis=1)
        for a in range(3)
    ]
    return jnp.concatenate(parts, axis=0).T.astype(BF16)


def inner_body(xlo_ref, low_ref, delta_ref, high_ref, xhi_ref, pool_ref, w_ref, wmid_ref, acc_ref, wide_ref, win_ref, up_ref, wskip_ref, wm_ref):
    def put(x, v):
        parts = shifts(v.astype(F32).reshape(768, 128), 128)
        for a in range(3):
            wide_ref[x, :, a * 32 : a * 32 + 32, :] = parts[a].astype(BF16).reshape(24, 32, 128)

    for x, v in enumerate((xlo_ref[...], low_ref[...], delta_ref[0], delta_ref[1], high_ref[...], xhi_ref[...])):
        put(x, v)
    wskip_ref[...] = skip_weights(w_ref)
    acc_ref[...] = jnp.zeros(acc_ref.shape, F32)

    def step(i, carry):
        y = 4 * i
        out = dot(
            wskip_ref[...],
            jnp.concatenate([stack_of(lambda x, j=j: wide_ref[x, y + j]) for j in range(4)], axis=1),
        )
        for x in range(4):
            for r in range(6):
                parts = [
                    out[b * 32 : b * 32 + 32, ((r - b) * 4 + x) * 128 : ((r - b) * 4 + x) * 128 + 128]
                    for b in range(3)
                    if 0 <= r - b < 4
                ]
                acc_ref[x, y + r] += sum(parts[1:], parts[0])
        return carry

    lax.fori_loop(0, 6, step, 0)
    for m in range(1, 5):

        def rows_of(x, j):
            return jnp.concatenate(
                [wide_ref[x, 4 * m + j - 1, 32:64, :], wide_ref[x, 4 * m + j + 1, 32:64, :]], axis=1
            )

        def put_window(bx, row, v):
            lane = (bx * 4 + m - 1) * 128
            win_ref[row : row + 32, lane : lane + 128] = v

        window_sums(rows_of, pool_ref[...], put_window)
    w = w_ref[...].reshape(864, 96)
    up_ref[...] = dot_tn(w, win_ref[...])[:64]
    for a in range(3):
        for b in range(3):
            at = (a * 3 + b) * 32
            parts = [wmid_ref[a, b, c].astype(F32) for c in range(3)]
            wm_ref[at : at + 32, :] = jnp.concatenate(parts, axis=1).astype(BF16)


def outer_body(
    got_lo_ref, got_hi_ref, wide_ref, up_ref, mslope_ref, st_ref, pool_lo_ref, pool_hi_ref, pool_ref, w_ref, wskip_ref, wm_ref,
    edge_ref, rim_ref, win_ref, mid_ref, back_ref, face_lo_ref, face_hi_ref,
    total_ref,
):
    wskip = wskip_ref[...]

    def row(x, y):
        if y < 0:
            at = (x * 3 + y + 3) * 32
            return got_lo_ref[at : at + 32, :]
        if y > 23:
            at = (x * 3 + y - 24) * 32
            return got_hi_ref[at : at + 32, :]
        return wide_ref[x, y, 32:64, :]

    for x in range(6):
        v = jnp.concatenate([row(x, -1), row(x, 24)], axis=0).astype(F32)
        parts = shifts(v, 128)
        for a in range(3):
            rim_ref[x, :, a * 32 : a * 32 + 32, :] = parts[a].astype(BF16).reshape(2, 32, 128)
    outs = [dot(wskip, stack_of(lambda x, r=r: rim_ref[x, r])) for r in range(2)]
    for x in range(4):
        at = slice(x * 128, x * 128 + 128)
        edge_ref[x, 0] = outs[0][64:96, at]
        edge_ref[x, 1] = outs[1][0:32, at]

    for i, (left, right) in enumerate(((-1, 1), (19, 21), (23, -3))):

        def rows_of(x, j):
            return jnp.concatenate([row(x, left + j), row(x, right + j)], axis=1)

        def put_window(bx, r, v):
            lane = (bx * 3 + i) * 128
            win_ref[r : r + 32, lane : lane + 128] = v

        window_sums(rows_of, pool_ref[...], put_window)
    rim_up = dot_tn(w_ref[...].reshape(864, 96), win_ref[...])[:64]

    upper = lane_ids((64, 128)) >= 64
    before = got_lo_ref[576:640, :].astype(F32)
    after = got_hi_ref[576:640, :].astype(F32)
    rim_tilt = (
        jnp.where(upper, pltpu.roll(before, 64, 1), after),
        jnp.where(upper, before, pltpu.roll(after, 64, 1)),
    )
    for bx in range(2):
        for m in range(7):
            if 1 <= m <= 4:
                lane = (bx * 4 + m - 1) * 128
                v = up_ref[:, lane : lane + 128]
            else:
                lane = (bx * 3 + (0, 5, 6).index(m)) * 128
                v = rim_up[:, lane : lane + 128]
            tilt = rim_tilt[bx] if m == 6 else mslope_ref[bx, m]
            delta = (v * tilt).astype(BF16).astype(F32)
            lane = (bx * 7 + m) * 128
            for a, part in enumerate(shifts(delta, 64)):
                mid_ref[a * 64 : a * 64 + 64, lane : lane + 128] = part.astype(BF16)

    out = dot(wm_ref[...], mid_ref[...])
    total_ref[...] = jnp.zeros(total_ref.shape, F32)
    upper = lane_ids((32, 128)) >= 64
    for bx in range(2):
        for m in range(7):
            col = (bx * 7 + m) * 128
            for a in range(3):
                parts = [out[(a * 3 + b) * 32 : (a * 3 + b) * 32 + 32, col : col + 128] for b in range(3)]
                down = pltpu.roll(parts[0], 64, 1)
                up = pltpu.roll(parts[2], 64, 1)
                total_ref[bx + a, (m + 6) % 7] += jnp.where(upper, down, 0.0)
                total_ref[bx + a, m] += parts[1] + jnp.where(upper, up, down)
                total_ref[bx + a, (m + 1) % 7] += jnp.where(upper, 0.0, up)
    back_ref[...] = total_ref[1:3, 0:6]
    before = got_lo_ref[640:672, :].astype(F32)
    after = got_hi_ref[640:672, :].astype(F32)
    for x, face_ref, side_ref in ((0, face_lo_ref, pool_lo_ref), (3, face_hi_ref, pool_hi_ref)):
        face_ref[0:192, :] = total_ref[x, 0:6].astype(BF16).reshape(192, 128)
        face_ref[192:384, :] = side_ref[...]
        rows = (before[x * 8 : x * 8 + 8], st_ref[x].reshape(192, 128), after[x * 8 : x * 8 + 8])
        face_ref[384:592, :] = jnp.concatenate(rows, axis=0).astype(BF16)


def hidden_rows(hid_ref, ys):
    def tap(x, y):
        return hid_ref[x, y + 2]

    return jnp.concatenate(
        [jnp.concatenate([tap(x, y + b - 1) for y in ys for x in range(4)], axis=1) for b in range(3)], axis=0
    )


def pooled_taps(blocks):
    blocks = blocks + [jnp.zeros((32, 128), F32)]
    lower = lane_ids((32, 128)) < 64
    turned = [pltpu.roll(v, 64, 1) for v in blocks]
    taps = (
        [jnp.where(lower, turned[(m + 6) % 7], turned[m]) for m in range(7)],
        blocks,
        [jnp.where(lower, turned[m], turned[(m + 1) % 7]) for m in range(7)],
    )
    return jnp.concatenate([jnp.concatenate(v, axis=1) for v in taps], axis=0).astype(BF16)


def dec_grad_body(
    wide_ref, rim_ref, hid_ref, win_ref, rim_win_ref, hmid_ref, head_ref, pooled_ref, mid_ref,
    rows_ref, gmid_ref, hpad_ref, skip_ref,
):
    blank = jnp.zeros((2, 32, 128), BF16)
    for x in range(4):
        hpad_ref[x, 0:2] = blank
        hpad_ref[x, 26:28] = blank
        hpad_ref[x, 2:26] = hid_ref[x]
    rims = jnp.concatenate([stack_of(lambda x, r=r: rim_ref[x, r]) for r in (0, 1)], axis=1)
    skip_ref[...] = dot_nt(rims, hidden_rows(hpad_ref, (-1, 24)))

    def step(i, carry):
        y = 4 * i
        rows = jnp.concatenate([stack_of(lambda x, j=j: wide_ref[x, y + j]) for j in range(4)], axis=1)
        skip_ref[...] += dot_nt(rows, hidden_rows(hpad_ref, [y + j for j in range(4)]))
        return carry

    lax.fori_loop(0, 6, step, 0)
    rows_ref[0:288, :] = jnp.concatenate([skip_ref[...], jnp.zeros((288, 32), F32)], axis=1).astype(BF16)

    def side(bx, m):
        if 1 <= m <= 4:
            at = (bx * 4 + m - 1) * 128
            return win_ref[:, at : at + 128]
        at = (bx * 3 + (0 if m == 0 else 1)) * 128
        return rim_win_ref[:, at : at + 128]

    order = [(bx, m) for bx in range(2) for m in range(6)]
    windows = jnp.concatenate([side(bx, m) for bx, m in order], axis=1)
    hmid = jnp.concatenate([hmid_ref[bx, m] for bx, m in order], axis=1)
    lift = dot_nt(windows, hmid)
    rows_ref[288:720, :] = jnp.concatenate([lift[0:432], lift[432:864]], axis=1).astype(BF16)
    rows_ref[720:736, :] = jnp.concatenate(
        [jnp.concatenate([head_ref[...], jnp.zeros((8, 96), F32)], axis=1), jnp.zeros((8, 128), F32)], axis=0
    ).astype(BF16)
    taps = [pooled_taps([pooled_ref[bx, m].astype(F32) for m in range(6)]) for bx in range(2)]
    first, second = mid_ref[:, 0:896], mid_ref[:, 896:1792]
    gmid_ref[0:96, :] = dot_nt(taps[0], second)
    gmid_ref[96:192, :] = dot_nt(taps[0], first) + dot_nt(taps[1], second)
    gmid_ref[192:288, :] = dot_nt(taps[1], first)


def encoder_body(
    acc_ref, edge_ref, back_ref, rim_lo_ref, rim_hi_ref, got_lo_ref, got_hi_ref, slope_ref, w_ref, up_ref,
    mid_ref, gmid_ref, st_ref, dec_ref,
    rows_far, own_ref, face_lo_ref, face_hi_ref, edge_lo_ref, edge_hi_ref,
    enc_ref, total_ref, we_ref, rows_ref, sext_ref, sum_ref, sems,
):
    writes = fetch([(dec_ref, rows_far.at[0:736])], sems.at[0])

    def beyond(ref):
        side = ref[192:384, :].astype(F32)
        return pooled_taps([side[m * 32 : m * 32 + 32] for m in range(6)])

    gmid = jnp.concatenate(
        [
            gmid_ref[0:96, :] + dot_nt(beyond(got_lo_ref), mid_ref[:, 0:896]),
            gmid_ref[96:192, :],
            gmid_ref[192:288, :] + dot_nt(beyond(got_hi_ref), mid_ref[:, 896:1792]),
        ],
        axis=0,
    )
    rows_ref[0:288, :] = gmid[:, :128].astype(BF16)
    rows_ref[288:432, :] = jnp.concatenate([gmid[:144, 128:], gmid[144:, 128:]], axis=1).astype(BF16)
    writes += fetch([(rows_ref.at[0:432], rows_far.at[736:1168])], sems.at[1])

    sext_ref[1:5, 1:25] = st_ref[...]
    sext_ref[0] = got_lo_ref[384:592, :].astype(F32).reshape(26, 8, 128)
    sext_ref[5] = got_hi_ref[384:592, :].astype(F32).reshape(26, 8, 128)
    before = rim_lo_ref[640:672, :].astype(F32)
    after = rim_hi_ref[640:672, :].astype(F32)
    for x in range(4):
        sext_ref[x + 1, 0] = before[x * 8 : x * 8 + 8]
        sext_ref[x + 1, 25] = after[x * 8 : x * 8 + 8]

    for bx in range(2):
        for m in range(6):
            whole = back_ref[bx, m]
            whole = whole + (got_lo_ref if bx == 0 else got_hi_ref)[m * 32 : m * 32 + 32, :].astype(F32)
            whole = whole * 0.125
            high = whole.astype(BF16)
            low = (whole - high.astype(F32)).astype(BF16)
            wide = dot(jnp.concatenate([high, low], axis=1), up_ref[...])
            for half in range(2):
                fine = wide[:, half * 128 : half * 128 + 128]
                for ey in range(2):
                    y = 4 * m + 2 * half + ey
                    for ex in range(2):
                        x = 2 * bx + ex
                        sum_in = acc_ref[x, y + 1] + fine
                        if y in (0, 23):
                            sum_in = sum_in + edge_ref[x, (0, 23).index(y)]
                        delta = (sum_in * slope_ref[x, y]).astype(BF16).astype(F32)
                        lane = (y * 4 + x) * 128
                        for c, part in enumerate(shifts(delta, 128)):
                            enc_ref[c * 32 : c * 32 + 32, lane : lane + 128] = part.astype(BF16)

    for a in range(3):
        for b in range(3):
            at = (a * 3 + b) * 8
            we_ref[at : at + 8, :] = jnp.concatenate([w_ref[a, b, c].astype(F32) for c in range(3)], axis=1)
    w = we_ref[...].astype(BF16)
    total_ref[...] = jnp.zeros(total_ref.shape, F32)
    sum_ref[...] = jnp.zeros(sum_ref.shape, F32)

    def step(i, carry):
        y = 4 * i
        delta = enc_ref[:, pl.ds(pl.multiple_of(y * 512, 2048), 2048)]
        state = jnp.concatenate(
            [
                jnp.concatenate([sext_ref[x + a, y + j + b] for j in range(4) for x in range(4)], axis=1)
                for a in range(3)
                for b in range(3)
            ],
            axis=0,
        ).astype(BF16)
        sum_ref[...] += dot_nt(state, delta)
        out = dot(w, delta)
        for x in range(6):
            for r in range(6):
                parts = []
                for a in range(3):
                    for b in range(3):
                        j, own = r - b, x - a
                        if 0 <= j < 4 and 0 <= own < 4:
                            row, lane = (a * 3 + b) * 8, (j * 4 + own) * 128
                            parts.append(out[row : row + 8, lane : lane + 128])
                total_ref[x, y + r] += sum(parts[1:], parts[0])
        return carry

    lax.fori_loop(0, 6, step, 0)
    genc = jnp.concatenate([sum_ref[...], jnp.zeros((72, 32), F32)], axis=1)
    rows_ref[432:544, :] = jnp.concatenate([genc, jnp.zeros((40, 128), F32)], axis=0).astype(BF16)
    writes += fetch([(rows_ref.at[432:544], rows_far.at[1168:1280])], sems.at[2])
    own_ref[...] = total_ref[1:5, 1:25]
    face_lo_ref[...] = total_ref[0].reshape(208, 128).astype(BF16)
    face_hi_ref[...] = total_ref[5].reshape(208, 128).astype(BF16)
    edge_lo_ref[...] = total_ref[1:5, 0]
    edge_hi_ref[...] = total_ref[1:5, 25]
    for wait in writes:
        wait()


def corner_body(edge_lo_ref, edge_hi_ref, lo_ref, hi_ref, col_lo_ref, col_hi_ref):
    before = lo_ref[...].astype(F32)
    after = hi_ref[...].astype(F32)
    for edge_ref, at, col_ref in ((edge_lo_ref, 0, col_lo_ref), (edge_hi_ref, 200, col_hi_ref)):
        rows = [edge_ref[0] + before[at : at + 8], edge_ref[1], edge_ref[2], edge_ref[3] + after[at : at + 8]]
        col_ref[...] = jnp.concatenate(rows, axis=0).astype(BF16)


def final_body(cot_ref, own_ref, lo_ref, hi_ref, ylo_ref, yhi_ref, grad_ref):
    before = ylo_ref[...].astype(F32)
    after = yhi_ref[...].astype(F32)
    for x in range(4):
        total = own_ref[x]
        if x in (0, 3):
            side = (lo_ref if x == 0 else hi_ref)[...].astype(F32)
            total = total + side[8:200].reshape(24, 8, 128)
        at = slice(x * 8, x * 8 + 8)
        ends = [before[at][None], jnp.zeros((22, 8, 128), F32), after[at][None]]
        total = total + jnp.concatenate(ends, axis=0)
        grad_ref[:, x] = (cot_ref[:, x].astype(F32) + jnp.swapaxes(total, 0, 1)).astype(BF16)


def share_body(pieces_far, out_far, pieces_ref, copies_ref, sems, out_sems):
    count = pieces_ref.shape[0]
    part = count // 4
    spans = [pl.ds(i * part, part) for i in range(4)]
    waits = fetch([(pieces_far.at[span], pieces_ref.at[span]) for span in spans], sems)
    total = jnp.zeros(pieces_ref.shape[1:], F32)
    for i, wait in enumerate(waits):
        wait()
        for j in range(part):
            total = total + pieces_ref[i * part + j].astype(F32)
    total = total.astype(BF16)
    part = copies_ref.shape[0]
    for j in range(part):
        copies_ref[j] = total
    for wait in fetch([(copies_ref, out_far.at[pl.ds(i * part, part)]) for i in range(count // part)], out_sems):
        wait()


def unpack_body(scale, rows_ref, enc_ref, mid_ref, dec_ref, head_ref):
    def rows(at, count):
        return rows_ref[at : at + count, :].astype(F32) * scale

    skip = [rows(i * 32, 32) for i in range(9)]
    head_ref[...] = rows(720, 16)[:8, :32]
    mid_rest = [rows(1024 + i * 48, 48) for i in range(3)]
    mid_rest = jnp.concatenate(mid_rest, axis=0)
    mid_rest = jnp.concatenate([mid_rest[:, :64], mid_rest[:, 64:]], axis=0)
    enc = rows(1168, 80)
    lift = rows(288, 432)
    lift = jnp.concatenate([lift[:, :64], lift[:, 64:]], axis=0)
    for a in range(3):
        for b in range(3):
            tap = a * 3 + b
            pair = rows(736 + tap * 32, 32)
            mid_ref[a, b, 0] = pair[:, :64]
            mid_ref[a, b, 1] = pair[:, 64:]
            mid_ref[a, b, 2] = mid_rest[tap * 32 : tap * 32 + 32]
            for c in range(3):
                enc_ref[a, b, c] = enc[tap * 8 : tap * 8 + 8, c * 32 : c * 32 + 32]
                at = (tap * 3 + c) * 32
                dec_ref[a, b, c] = jnp.concatenate(
                    [lift[at : at + 32], skip[a * 3 + c][:, b * 32 : b * 32 + 32]], axis=1
                )


def pool_matrix():
    table = np.zeros((256, 3, 128), np.float32)
    for c, k in enumerate((-1, 0, 1)):
        for half in range(2):
            for q in range(64):
                for e in range(2):
                    z = 2 * q + e - k
                    if 0 <= z < 128:
                        table[half * 128 + z, c, half * 64 + q] = 1.0
    return jnp.asarray(table.reshape(256, 384), BF16)


def up_matrix():
    table = np.zeros((2, 128, 256), np.float32)
    for half in range(2):
        for z in range(128):
            table[:, half * 64 + z // 2, half * 128 + z] = 1.0
    return jnp.asarray(table.reshape(256, 256), BF16)


def both_ways(low, high, axis):
    ends = lax.axis_size(axis) - 1
    from_before = lax.ppermute(high, axis, [(i, i + 1) for i in range(ends)])
    from_after = lax.ppermute(low, axis, [(i + 1, i) for i in range(ends)])
    return from_before, from_after


def on_device(
    state_now, enc_pre, mid_pre, dec_pre, cotangent, enc_kernel, mid_kernel, dec_kernel, out_kernel
):
    state_now, enc_pre, mid_pre, dec_pre, cotangent = (
        v[0] for v in (state_now, enc_pre, mid_pre, dec_pre, cotangent)
    )
    cells = state_now[0].size * lax.axis_size("gx") * lax.axis_size("gy") * lax.axis_size("dp")
    grad_scale = 1.0 / math.sqrt(cells)
    pool = pool_matrix()
    dec_w = dec_kernel.transpose(2, 3, 4, 0, 1)
    mid_w = mid_kernel.transpose(2, 3, 4, 1, 0)
    enc_w = enc_kernel.transpose(2, 3, 4, 1, 0)

    plane = sds((24, 32, 128), BF16)
    delta_lo, delta_hi = call(
        face_body,
        [plane, plane],
        [
            pltpu.VMEM((2, 32, 24, 128), BF16),
            pltpu.VMEM((2, 8, 24, 128), BF16),
            pltpu.VMEM((8, 32), BF16),
            pltpu.VMEM((2, 24, 32, 128), BF16),
            pltpu.SemaphoreType.DMA((5,)),
            pltpu.SemaphoreType.DMA((2, 1)),
        ],
        (dec_pre, cotangent, out_kernel),
        200 << 20, 56, far=3, far_outs=2,
    )
    xlo, xhi = both_ways(delta_lo, delta_hi, "gx")
    mid_blocks = mid_pre.reshape(64, 2, 6, 2, 64).transpose(1, 2, 0, 3, 4).reshape(2, 6, 64, 128)
    (
        delta, head_grad, hidden, enc_slope, pooled, hidden_mid, mid_slope, state,
        tail_lo, tail_hi, pool_lo, pool_hi,
    ) = call(
        forward_body,
        [
            sds((2, 24, 32, 128), BF16),
            sds((8, 32), F32),
            sds((4, 24, 32, 128), BF16),
            sds((4, 24, 32, 128), F32),
            sds((2, 6, 32, 128), BF16),
            sds((2, 6, 64, 128), BF16),
            sds((2, 6, 64, 128), F32),
            sds((4, 24, 8, 128), F32),
            sds((96, 128), BF16),
            sds((96, 128), BF16),
            sds((192, 128), BF16),
            sds((192, 128), BF16),
        ],
        [],
        (dec_pre, cotangent, out_kernel, enc_pre, state_now, mid_blocks, pool),
        600 << 20, 16,
    )

    def column(at, tail):
        rows = (xlo[at], delta_lo[at], delta[0, at], delta[1, at], delta_hi[at], xhi[at], tail)
        return jnp.concatenate([v.reshape(-1, 128) for v in rows])

    ylo, yhi = both_ways(column(slice(0, 3), tail_lo), column(slice(21, 24), tail_hi), "gy")
    acc, wide, win, up, wskip, wmid = call(
        inner_body,
        [
            sds((4, 26, 32, 128), F32),
            sds((6, 24, 96, 128), BF16),
            sds((864, 1024), BF16),
            sds((64, 1024), F32),
            sds((96, 288), BF16),
            sds((288, 192), BF16),
        ],
        [],
        (xlo, delta_lo, delta, delta_hi, xhi, pool, dec_w, mid_w),
        3 << 30, 24,
    )
    edge, rim_wide, rim_win, mid_wide, back, face_lo, face_hi = call(
        outer_body,
        [
            sds((4, 2, 32, 128), F32),
            sds((6, 2, 96, 128), BF16),
            sds((864, 768), BF16),
            sds((192, 1792), BF16),
            sds((2, 6, 32, 128), F32),
            sds((592, 128), BF16),
            sds((592, 128), BF16),
        ],
        [pltpu.VMEM((4, 7, 32, 128), F32)],
        (ylo, yhi, wide, up, mid_slope, state, pool_lo, pool_hi, pool, dec_w, wskip, wmid),
        1 << 30, 24,
    )
    got_lo, got_hi = both_ways(face_lo, face_hi, "gx")
    dec_rows, mid_grad = call(
        dec_grad_body,
        [sds((736, 128), BF16), sds((288, 192), F32)],
        [pltpu.VMEM((4, 28, 32, 128), BF16), pltpu.VMEM((288, 96), F32)],
        (wide, rim_wide, hidden, win, rim_win, hidden_mid, head_grad, pooled, mid_wide),
        3 << 30, 20,
    )
    dec_rows, mid_grad, got_lo, got_hi = lax.optimization_barrier((dec_rows, mid_grad, got_lo, got_hi))
    rows, own, face_lo, face_hi, edge_lo, edge_hi = call(
        encoder_body,
        [
            sds((1280, 128), BF16),
            sds((4, 24, 8, 128), F32),
            sds((208, 128), BF16),
            sds((208, 128), BF16),
            sds((4, 8, 128), F32),
            sds((4, 8, 128), F32),
        ],
        [
            pltpu.VMEM((96, 24 * 512), BF16),
            pltpu.VMEM((6, 26, 8, 128), F32),
            pltpu.VMEM((72, 96), F32),
            pltpu.VMEM((544, 128), BF16),
            pltpu.VMEM((6, 26, 8, 128), F32),
            pltpu.VMEM((72, 96), F32),
            pltpu.SemaphoreType.DMA((3, 1)),
        ],
        (
            acc, edge, back, ylo, yhi, got_lo, got_hi, enc_slope, enc_w, up_matrix(),
            mid_wide, mid_grad, state, dec_rows,
        ),
        2 << 30, 24, far_outs=1,
    )
    last_lo, last_hi = both_ways(face_lo, face_hi, "gx")

    axes = ("dp", "gx", "gy")
    count = lax.axis_size(axes)
    share = 1280 // count // 2
    pieces = lax.all_to_all(rows.reshape(count, share, 2, 128), axes, 0, 0)
    (shares,) = call(
        share_body,
        [sds(pieces.shape, BF16)],
        [
            pltpu.VMEM(pieces.shape, BF16),
            pltpu.VMEM((count // 8,) + pieces.shape[1:], BF16),
            pltpu.SemaphoreType.DMA((4,)),
            pltpu.SemaphoreType.DMA((8,)),
        ],
        (pieces,),
        1 << 20, 8, far=1, far_outs=1,
    )
    shares, last_lo, last_hi = lax.optimization_barrier((shares, last_lo, last_hi))
    rows = lax.all_to_all(shares, axes, 0, 0).reshape(1280, 128)
    col_lo, col_hi = call(
        corner_body, [sds((32, 128), BF16)] * 2, [], (edge_lo, edge_hi, last_lo, last_hi), 1 << 16, 4
    )
    end_lo, end_hi = both_ways(col_lo, col_hi, "gy")
    genc, gmid, gdec, ghead = call(
        functools.partial(unpack_body, grad_scale),
        [sds((3, 3, 3, 8, 32), F32), sds((3, 3, 3, 32, 64), F32), sds((3, 3, 3, 32, 96), F32), sds((8, 32), F32)],
        [],
        (rows,),
        1 << 20, 12,
    )
    genc, end_lo, end_hi = lax.optimization_barrier((genc, end_lo, end_hi))
    (state_grad,) = call(
        final_body,
        [sds((8, 4, 24, 128), BF16)],
        [],
        (cotangent, own, last_lo, last_hi, end_lo, end_hi),
        1 << 20, 8,
    )
    return (
        state_grad[None],
        genc.transpose(4, 3, 0, 1, 2),
        gmid.transpose(4, 3, 0, 1, 2),
        gdec.transpose(3, 4, 0, 1, 2),
        ghead,
    )


def solution(mesh):
    grid = P("dp", None, "gx", "gy", None)
    return jax.shard_map(
        on_device,
        mesh=mesh,
        in_specs=(grid,) * 5 + (P(),) * 4,
        out_specs=(grid, P(), P(), P(), P()),
        check_vma=False,
    )
```

```python
import functools
import math

import jax
import jax.numpy as jnp
import numpy as np
from jax import lax
from jax.experimental import pallas as pl
from jax.experimental.pallas import tpu as pltpu
from jax.sharding import PartitionSpec as P

F32 = jnp.float32
BF16 = jnp.bfloat16


VMEM = pl.BlockSpec(memory_space=pltpu.VMEM)
HBM = pl.BlockSpec(memory_space=pltpu.HBM)


def call(body, outs, scratch, args, flops, limit, far=0, far_outs=0):
    return pl.pallas_call(
        body,
        out_shape=outs,
        in_specs=[HBM] * far + [VMEM] * (len(args) - far),
        out_specs=[HBM] * far_outs + [VMEM] * (len(outs) - far_outs),
        scratch_shapes=scratch,
        compiler_params=pltpu.CompilerParams(vmem_limit_bytes=limit << 20),
        cost_estimate=pl.CostEstimate(flops=flops, bytes_accessed=4 << 20, transcendentals=0),
    )(*args)


def fetch(pairs, sems):
    copies = [pltpu.make_async_copy(src, dst, sems.at[i]) for i, (src, dst) in enumerate(pairs)]
    for copy in copies:
        copy.start()
    return [copy.wait for copy in copies]


def sds(shape, dtype):
    return jax.ShapeDtypeStruct(shape, dtype)


def dot(a, b):
    return lax.dot_general(a, b, (((1,), (0,)), ((), ())), preferred_element_type=F32)


def dot_tn(a, b):
    return lax.dot_general(a, b, (((0,), (0,)), ((), ())), preferred_element_type=F32)


def dot_nt(a, b):
    return lax.dot_general(a, b, (((1,), (1,)), ((), ())), preferred_element_type=F32)


def sigmoid(v):
    return 0.5 + 0.5 * jnp.tanh(0.5 * v)


def slope(v, s):
    return s * (1.0 + v * (1.0 - s))


def lane_ids(shape):
    return lax.broadcasted_iota(jnp.int32, shape, len(shape) - 1)


def shifts(v, period):
    lane = jnp.bitwise_and(lane_ids(v.shape), period - 1)
    axis = v.ndim - 1
    size = v.shape[-1]
    back = jnp.where(lane == period - 1, 0.0, pltpu.roll(v, size - 1, axis))
    ahead = jnp.where(lane == 0, 0.0, pltpu.roll(v, 1, axis))
    return back, v, ahead


def delta_plane(dec, cot, head):
    pre = jnp.swapaxes(dec.astype(F32), 0, 1)
    cot = jnp.swapaxes(cot.astype(F32), 0, 1)
    cot_lanes = jnp.concatenate([cot[y] for y in range(24)], axis=1).astype(BF16)
    back = dot_tn(head, cot_lanes)
    back = jnp.stack([back[:, y * 128 : y * 128 + 128] for y in range(24)], axis=0)
    s = sigmoid(pre)
    return (back * slope(pre, s)).astype(BF16), cot_lanes, pre * s


def face_body(dec_far, cot_far, head_far, low_far, high_far, dec_ref, cot_ref, head_ref, delta_ref, sems, out_sems):
    planes = (0, 3)
    pairs = [(head_far, head_ref)]
    for i, x in enumerate(planes):
        pairs += [(cot_far.at[:, x], cot_ref.at[i]), (dec_far.at[:, x], dec_ref.at[i])]
    waits = fetch(pairs, sems)
    waits[0]()
    writes = []
    for i, far in enumerate((low_far, high_far)):
        waits[2 * i + 1]()
        waits[2 * i + 2]()
        delta_ref[i] = delta_plane(dec_ref[i], cot_ref[i], head_ref[...])[0]
        writes += fetch([(delta_ref.at[i], far)], out_sems.at[i])
    for wait in writes:
        wait()


def forward_body(
    dec_ref, cot_ref, head_ref, enc_ref, state_ref, mid_ref, pool_ref,
    delta_ref, head_grad_ref, hid_ref, slope_ref, pooled_ref, hmid_ref, mslope_ref, st_ref, ylo_ref, yhi_ref, xlo_ref, xhi_ref,
):
    total = jnp.zeros((8, 32), F32)
    for x in range(4):
        delta, cot_lanes, decoded = delta_plane(dec_ref[:, x], cot_ref[:, x], head_ref[...])
        if x in (1, 2):
            delta_ref[x - 1] = delta
        decoded = jnp.concatenate([decoded[y] for y in range(24)], axis=1).astype(BF16)
        total = total + dot_nt(cot_lanes, decoded)
    head_grad_ref[...] = total
    low_rows, high_rows = [], []
    for x in range(4):
        pre = jnp.swapaxes(enc_ref[:, x].astype(F32), 0, 1)
        s = sigmoid(pre)
        hid_ref[x] = (pre * s).astype(BF16)
        slope_ref[x] = slope(pre, s)
        state = jnp.swapaxes(state_ref[:, x].astype(F32), 0, 1)
        st_ref[x] = state
        low_rows.append(state[0])
        high_rows.append(state[23])
    ylo_ref[64:96, :] = jnp.concatenate(low_rows, axis=0).astype(BF16)
    yhi_ref[64:96, :] = jnp.concatenate(high_rows, axis=0).astype(BF16)
    tilts = {}
    for bx in range(2):
        for m in range(6):
            acc = None
            for ex in range(2):
                for ey in range(2):
                    pair = jnp.concatenate(
                        [hid_ref[2 * bx + ex, 4 * m + ey], hid_ref[2 * bx + ex, 4 * m + 2 + ey]], axis=1
                    )
                    part = dot(pair, pool_ref[:, 128:256])
                    acc = part if acc is None else acc + part
            pooled = (acc * 0.125).astype(BF16)
            pooled_ref[bx, m] = pooled
            side_ref = xlo_ref if bx == 0 else xhi_ref
            side_ref[m * 32 : m * 32 + 32, :] = pooled
            pre = mid_ref[bx, m].astype(F32)
            s = sigmoid(pre)
            hmid_ref[bx, m] = (pre * s).astype(BF16)
            tilts[bx, m] = slope(pre, s)
            mslope_ref[bx, m] = tilts[bx, m]
    lower = lane_ids((64, 128)) < 64
    ylo_ref[0:64, :] = jnp.where(lower, tilts[0, 0], pltpu.roll(tilts[1, 0], 64, 1)).astype(BF16)
    yhi_ref[0:64, :] = jnp.where(lower, pltpu.roll(tilts[0, 5], 64, 1), tilts[1, 5]).astype(BF16)


def window_sums(rows_of, pool, put):
    got = dot(
        jnp.concatenate([jnp.concatenate([rows_of(x, j) for j in range(4)], axis=0) for x in range(6)], axis=0), pool
    )
    sums = []
    for x in range(6):
        at = [got[x * 128 + j * 32 : x * 128 + j * 32 + 32] for j in range(4)]
        sums.append([at[j] + at[j + 1] for j in (2, 1, 0)])
    for bx in range(2):
        for a, kx in enumerate((-1, 0, 1)):
            for b in range(3):
                both = (sums[2 * bx - kx + 1][b] + sums[2 * bx - kx + 2][b]).astype(BF16)
                for c in range(3):
                    put(bx, ((a * 3 + b) * 3 + c) * 32, both[:, c * 128 : c * 128 + 128])


def stack_of(row):
    return jnp.concatenate(
        [jnp.concatenate([row(x + 1 - kx) for x in range(4)], axis=1) for kx in (-1, 0, 1)], axis=0
    )


def skip_weights(w_ref):
    parts = [
        jnp.concatenate([w_ref[a, b].astype(F32).reshape(96, 96)[:, 64:96] for b in range(3)], axis=1)
        for a in range(3)
    ]
    return jnp.concatenate(parts, axis=0).T.astype(BF16)


def inner_body(xlo_ref, low_ref, delta_ref, high_ref, xhi_ref, pool_ref, w_ref, wmid_ref, acc_ref, wide_ref, win_ref, up_ref, wskip_ref, wm_ref, wup_ref):
    def put(x, v):
        parts = shifts(v.astype(F32).reshape(768, 128), 128)
        for a in range(3):
            wide_ref[x, :, a * 32 : a * 32 + 32, :] = parts[a].astype(BF16).reshape(24, 32, 128)

    for x, v in enumerate((xlo_ref[...], low_ref[...], delta_ref[0], delta_ref[1], high_ref[...], xhi_ref[...])):
        put(x, v)
    wskip_ref[...] = skip_weights(w_ref)
    acc_ref[...] = jnp.zeros(acc_ref.shape, F32)

    def step(i, carry):
        y = 4 * i
        out = dot(
            wskip_ref[...],
            jnp.concatenate([stack_of(lambda x, j=j: wide_ref[x, y + j]) for j in range(4)], axis=1),
        )
        for x in range(4):
            for r in range(6):
                parts = [
                    out[b * 32 : b * 32 + 32, ((r - b) * 4 + x) * 128 : ((r - b) * 4 + x) * 128 + 128]
                    for b in range(3)
                    if 0 <= r - b < 4
                ]
                acc_ref[x, y + r] += sum(parts[1:], parts[0])
        return carry

    lax.fori_loop(0, 6, step, 0)
    for m in range(1, 5):

        def rows_of(x, j):
            return jnp.concatenate(
                [wide_ref[x, 4 * m + j - 1, 32:64, :], wide_ref[x, 4 * m + j + 1, 32:64, :]], axis=1
            )

        def put_window(bx, row, v):
            lane = (bx * 4 + m - 1) * 128
            win_ref[row : row + 32, lane : lane + 128] = v

        window_sums(rows_of, pool_ref[...], put_window)
    wup_ref[...] = w_ref[...].reshape(864, 96).astype(F32).T[:64].astype(BF16)
    up_ref[...] = dot(wup_ref[...], win_ref[...])
    for a in range(3):
        for b in range(3):
            at = (a * 3 + b) * 32
            parts = [wmid_ref[a, b, c].astype(F32) for c in range(3)]
            wm_ref[at : at + 32, :] = jnp.concatenate(parts, axis=1).astype(BF16)


def outer_body(
    got_lo_ref, got_hi_ref, wide_ref, up_ref, mslope_ref, st_ref, pool_lo_ref, pool_hi_ref, pool_ref, wup_ref, wskip_ref, wm_ref,
    edge_ref, rim_ref, win_ref, mid_ref, back_ref, face_lo_ref, face_hi_ref,
    total_ref,
):
    wskip = wskip_ref[...]

    def row(x, y):
        if y < 0:
            at = (x * 3 + y + 3) * 32
            return got_lo_ref[at : at + 32, :]
        if y > 23:
            at = (x * 3 + y - 24) * 32
            return got_hi_ref[at : at + 32, :]
        return wide_ref[x, y, 32:64, :]

    for x in range(6):
        v = jnp.concatenate([row(x, -1), row(x, 24)], axis=0).astype(F32)
        parts = shifts(v, 128)
        for a in range(3):
            rim_ref[x, :, a * 32 : a * 32 + 32, :] = parts[a].astype(BF16).reshape(2, 32, 128)
    outs = [dot(wskip, stack_of(lambda x, r=r: rim_ref[x, r])) for r in range(2)]
    for x in range(4):
        at = slice(x * 128, x * 128 + 128)
        edge_ref[x, 0] = outs[0][64:96, at]
        edge_ref[x, 1] = outs[1][0:32, at]

    for i, (left, right) in enumerate(((-1, 1), (19, 21), (23, -3))):

        def rows_of(x, j):
            return jnp.concatenate([row(x, left + j), row(x, right + j)], axis=1)

        def put_window(bx, r, v):
            lane = (bx * 3 + i) * 128
            win_ref[r : r + 32, lane : lane + 128] = v

        window_sums(rows_of, pool_ref[...], put_window)
    rim_up = dot(wup_ref[...], win_ref[...])

    upper = lane_ids((64, 128)) >= 64
    before = got_lo_ref[576:640, :].astype(F32)
    after = got_hi_ref[576:640, :].astype(F32)
    rim_tilt = (
        jnp.where(upper, pltpu.roll(before, 64, 1), after),
        jnp.where(upper, before, pltpu.roll(after, 64, 1)),
    )
    for bx in range(2):
        for m in range(7):
            if 1 <= m <= 4:
                lane = (bx * 4 + m - 1) * 128
                v = up_ref[:, lane : lane + 128]
            else:
                lane = (bx * 3 + (0, 5, 6).index(m)) * 128
                v = rim_up[:, lane : lane + 128]
            tilt = rim_tilt[bx] if m == 6 else mslope_ref[bx, m]
            delta = (v * tilt).astype(BF16).astype(F32)
            lane = (bx * 7 + m) * 128
            for a, part in enumerate(shifts(delta, 64)):
                mid_ref[a * 64 : a * 64 + 64, lane : lane + 128] = part.astype(BF16)

    out = dot(wm_ref[...], mid_ref[...])
    upper = lane_ids((32, 128)) >= 64

    def term(a, b, x, m):
        if not 0 <= x - a < 2:
            return None
        col = ((x - a) * 7 + m) * 128
        return out[(a * 3 + b) * 32 : (a * 3 + b) * 32 + 32, col : col + 128]

    def tap_sum(b, x, m):
        parts = [v for v in (term(a, b, x, m) for a in range(3)) if v is not None]
        return sum(parts[1:], parts[0])

    for x in range(4):
        downs = [pltpu.roll(tap_sum(0, x, m), 64, 1) for m in range(7)]
        ups = [pltpu.roll(tap_sum(2, x, m), 64, 1) for m in range(7)]
        for m in range(6):
            low = ups[(m + 6) % 7] + downs[m]
            high = ups[m] + downs[m + 1]
            total_ref[x, m] = tap_sum(1, x, m) + jnp.where(upper, high, low)
    back_ref[...] = total_ref[1:3, 0:6]
    before = got_lo_ref[640:672, :].astype(F32)
    after = got_hi_ref[640:672, :].astype(F32)
    for x, face_ref, side_ref in ((0, face_lo_ref, pool_lo_ref), (3, face_hi_ref, pool_hi_ref)):
        face_ref[0:192, :] = total_ref[x, 0:6].astype(BF16).reshape(192, 128)
        face_ref[192:384, :] = side_ref[...]
        rows = (before[x * 8 : x * 8 + 8], st_ref[x].reshape(192, 128), after[x * 8 : x * 8 + 8])
        face_ref[384:592, :] = jnp.concatenate(rows, axis=0).astype(BF16)


def hidden_rows(hid_ref, ys):
    def tap(x, y):
        return hid_ref[x, y + 2]

    return jnp.concatenate(
        [jnp.concatenate([tap(x, y + b - 1) for y in ys for x in range(4)], axis=1) for b in range(3)], axis=0
    )


def pooled_taps(blocks):
    blocks = blocks + [jnp.zeros((32, 128), F32)]
    lower = lane_ids((32, 128)) < 64
    turned = [pltpu.roll(v, 64, 1) for v in blocks]
    taps = (
        [jnp.where(lower, turned[(m + 6) % 7], turned[m]) for m in range(7)],
        blocks,
        [jnp.where(lower, turned[m], turned[(m + 1) % 7]) for m in range(7)],
    )
    return jnp.concatenate([jnp.concatenate(v, axis=1) for v in taps], axis=0).astype(BF16)


def dec_grad_body(
    wide_ref, rim_ref, hid_ref, win_ref, rim_win_ref, hmid_ref, head_ref, pooled_ref, mid_ref,
    rows_ref, gmid_ref, hpad_ref, skip_ref,
):
    blank = jnp.zeros((2, 32, 128), BF16)
    for x in range(4):
        hpad_ref[x, 0:2] = blank
        hpad_ref[x, 26:28] = blank
        hpad_ref[x, 2:26] = hid_ref[x]
    rims = jnp.concatenate([stack_of(lambda x, r=r: rim_ref[x, r]) for r in (0, 1)], axis=1)
    skip_ref[...] = dot_nt(rims, hidden_rows(hpad_ref, (-1, 24)))

    def step(i, carry):
        y = 4 * i
        rows = jnp.concatenate([stack_of(lambda x, j=j: wide_ref[x, y + j]) for j in range(4)], axis=1)
        skip_ref[...] += dot_nt(rows, hidden_rows(hpad_ref, [y + j for j in range(4)]))
        return carry

    lax.fori_loop(0, 6, step, 0)
    rows_ref[0:288, :] = jnp.concatenate([skip_ref[...], jnp.zeros((288, 32), F32)], axis=1).astype(BF16)

    def side(bx, m):
        if 1 <= m <= 4:
            at = (bx * 4 + m - 1) * 128
            return win_ref[:, at : at + 128]
        at = (bx * 3 + (0 if m == 0 else 1)) * 128
        return rim_win_ref[:, at : at + 128]

    order = [(bx, m) for bx in range(2) for m in range(6)]
    windows = jnp.concatenate([side(bx, m) for bx, m in order], axis=1)
    hmid = jnp.concatenate([hmid_ref[bx, m] for bx, m in order], axis=1)
    lift = dot_nt(windows, hmid)
    rows_ref[288:720, :] = jnp.concatenate([lift[0:432], lift[432:864]], axis=1).astype(BF16)
    rows_ref[720:736, :] = jnp.concatenate(
        [jnp.concatenate([head_ref[...], jnp.zeros((8, 96), F32)], axis=1), jnp.zeros((8, 128), F32)], axis=0
    ).astype(BF16)
    taps = [pooled_taps([pooled_ref[bx, m].astype(F32) for m in range(6)]) for bx in range(2)]
    first, second = mid_ref[:, 0:896], mid_ref[:, 896:1792]
    gmid_ref[0:96, :] = dot_nt(taps[0], second)
    gmid_ref[96:192, :] = dot_nt(taps[0], first) + dot_nt(taps[1], second)
    gmid_ref[192:288, :] = dot_nt(taps[1], first)


def encoder_body(
    acc_ref, edge_ref, back_ref, rim_lo_ref, rim_hi_ref, got_lo_ref, got_hi_ref, slope_ref, w_ref, up_ref,
    mid_ref, gmid_ref, st_ref, dec_ref,
    rows_far, own_ref, face_lo_ref, face_hi_ref, edge_lo_ref, edge_hi_ref,
    enc_ref, wide_ref, total_ref, we_ref, rows_ref, sext_ref, sum_ref, sems,
):
    writes = fetch([(dec_ref, rows_far.at[0:736])], sems.at[0])

    def beyond(ref):
        side = ref[192:384, :].astype(F32)
        return pooled_taps([side[m * 32 : m * 32 + 32] for m in range(6)])

    gmid = jnp.concatenate(
        [
            gmid_ref[0:96, :] + dot_nt(beyond(got_lo_ref), mid_ref[:, 0:896]),
            gmid_ref[96:192, :],
            gmid_ref[192:288, :] + dot_nt(beyond(got_hi_ref), mid_ref[:, 896:1792]),
        ],
        axis=0,
    )
    rows_ref[0:288, :] = gmid[:, :128].astype(BF16)
    rows_ref[288:432, :] = jnp.concatenate([gmid[:144, 128:], gmid[144:, 128:]], axis=1).astype(BF16)
    writes += fetch([(rows_ref.at[0:432], rows_far.at[736:1168])], sems.at[1])

    sext_ref[1:5, 1:25] = st_ref[...]
    sext_ref[0] = got_lo_ref[384:592, :].astype(F32).reshape(26, 8, 128)
    sext_ref[5] = got_hi_ref[384:592, :].astype(F32).reshape(26, 8, 128)
    before = rim_lo_ref[640:672, :].astype(F32)
    after = rim_hi_ref[640:672, :].astype(F32)
    for x in range(4):
        sext_ref[x + 1, 0] = before[x * 8 : x * 8 + 8]
        sext_ref[x + 1, 25] = after[x * 8 : x * 8 + 8]

    whole = [back_ref[bx].reshape(192, 128) for bx in range(2)]
    whole = [v + ref[0:192, :].astype(F32) for v, ref in zip(whole, (got_lo_ref, got_hi_ref))]
    whole = jnp.concatenate(whole, axis=0) * 0.125
    high = whole.astype(BF16)
    low = (whole - high.astype(F32)).astype(BF16)
    wide_ref[...] = dot(jnp.concatenate([high, low], axis=1), up_ref[...])
    for bx in range(2):
        for m in range(6):
            at = (bx * 6 + m) * 32
            for half in range(2):
                fine = wide_ref[at : at + 32, half * 128 : half * 128 + 128]
                for ey in range(2):
                    y = 4 * m + 2 * half + ey
                    for ex in range(2):
                        x = 2 * bx + ex
                        sum_in = acc_ref[x, y + 1] + fine
                        if y in (0, 23):
                            sum_in = sum_in + edge_ref[x, (0, 23).index(y)]
                        delta = (sum_in * slope_ref[x, y]).astype(BF16).astype(F32)
                        lane = (y * 4 + x) * 128
                        for c, part in enumerate(shifts(delta, 128)):
                            enc_ref[c * 32 : c * 32 + 32, lane : lane + 128] = part.astype(BF16)

    for a in range(3):
        for b in range(3):
            at = (a * 3 + b) * 8
            we_ref[at : at + 8, :] = jnp.concatenate([w_ref[a, b, c].astype(F32) for c in range(3)], axis=1)
    w = we_ref[...].astype(BF16)
    total_ref[...] = jnp.zeros(total_ref.shape, F32)
    sum_ref[...] = jnp.zeros(sum_ref.shape, F32)

    def step(i, carry):
        y = 4 * i
        delta = enc_ref[:, pl.ds(pl.multiple_of(y * 512, 2048), 2048)]
        state = jnp.concatenate(
            [
                jnp.concatenate([sext_ref[x + a, y + j + b] for j in range(4) for x in range(4)], axis=1)
                for a in range(3)
                for b in range(3)
            ],
            axis=0,
        ).astype(BF16)
        sum_ref[...] += dot_nt(state, delta)
        out = dot(w, delta)
        for x in range(6):
            for r in range(6):
                parts = []
                for a in range(3):
                    for b in range(3):
                        j, own = r - b, x - a
                        if 0 <= j < 4 and 0 <= own < 4:
                            row, lane = (a * 3 + b) * 8, (j * 4 + own) * 128
                            parts.append(out[row : row + 8, lane : lane + 128])
                total_ref[x, y + r] += sum(parts[1:], parts[0])
        return carry

    lax.fori_loop(0, 6, step, 0, unroll=3)
    genc = jnp.concatenate([sum_ref[...], jnp.zeros((72, 32), F32)], axis=1)
    rows_ref[432:544, :] = jnp.concatenate([genc, jnp.zeros((40, 128), F32)], axis=0).astype(BF16)
    writes += fetch([(rows_ref.at[432:544], rows_far.at[1168:1280])], sems.at[2])
    own_ref[...] = total_ref[1:5, 1:25]
    face_lo_ref[...] = total_ref[0].reshape(208, 128).astype(BF16)
    face_hi_ref[...] = total_ref[5].reshape(208, 128).astype(BF16)
    edge_lo_ref[...] = total_ref[1:5, 0]
    edge_hi_ref[...] = total_ref[1:5, 25]
    for wait in writes:
        wait()


def corner_body(edge_lo_ref, edge_hi_ref, lo_ref, hi_ref, col_lo_ref, col_hi_ref):
    before = lo_ref[...].astype(F32)
    after = hi_ref[...].astype(F32)
    for edge_ref, at, col_ref in ((edge_lo_ref, 0, col_lo_ref), (edge_hi_ref, 200, col_hi_ref)):
        rows = [edge_ref[0] + before[at : at + 8], edge_ref[1], edge_ref[2], edge_ref[3] + after[at : at + 8]]
        col_ref[...] = jnp.concatenate(rows, axis=0).astype(BF16)


def final_body(cot_ref, own_ref, lo_ref, hi_ref, ylo_ref, yhi_ref, grad_ref):
    before = ylo_ref[...].astype(F32)
    after = yhi_ref[...].astype(F32)
    for x in range(4):
        total = own_ref[x]
        if x in (0, 3):
            side = (lo_ref if x == 0 else hi_ref)[...].astype(F32)
            total = total + side[8:200].reshape(24, 8, 128)
        at = slice(x * 8, x * 8 + 8)
        ends = [before[at][None], jnp.zeros((22, 8, 128), F32), after[at][None]]
        total = total + jnp.concatenate(ends, axis=0)
        grad_ref[:, x] = (cot_ref[:, x].astype(F32) + jnp.swapaxes(total, 0, 1)).astype(BF16)


def share_body(pieces_far, out_far, pieces_ref, copies_ref, sems, out_sems):
    count = pieces_ref.shape[0]
    part = count // 4
    spans = [pl.ds(i * part, part) for i in range(4)]
    waits = fetch([(pieces_far.at[span], pieces_ref.at[span]) for span in spans], sems)
    total = jnp.zeros(pieces_ref.shape[1:], F32)
    for i, wait in enumerate(waits):
        wait()
        for j in range(part):
            total = total + pieces_ref[i * part + j].astype(F32)
    total = total.astype(BF16)
    part = copies_ref.shape[0]
    for j in range(part):
        copies_ref[j] = total
    for wait in fetch([(copies_ref, out_far.at[pl.ds(i * part, part)]) for i in range(count // part)], out_sems):
        wait()


def unpack_body(scale, rows_ref, enc_ref, mid_ref, dec_ref, head_ref):
    def rows(at, count):
        return rows_ref[at : at + count, :].astype(F32) * scale

    skip = [rows(i * 32, 32) for i in range(9)]
    head_ref[...] = rows(720, 16)[:8, :32]
    mid_rest = [rows(1024 + i * 48, 48) for i in range(3)]
    mid_rest = jnp.concatenate(mid_rest, axis=0)
    mid_rest = jnp.concatenate([mid_rest[:, :64], mid_rest[:, 64:]], axis=0)
    enc = rows(1168, 80)
    lift = rows(288, 432)
    lift = jnp.concatenate([lift[:, :64], lift[:, 64:]], axis=0)
    for a in range(3):
        for b in range(3):
            tap = a * 3 + b
            pair = rows(736 + tap * 32, 32)
            mid_ref[a, b, 0] = pair[:, :64]
            mid_ref[a, b, 1] = pair[:, 64:]
            mid_ref[a, b, 2] = mid_rest[tap * 32 : tap * 32 + 32]
            for c in range(3):
                enc_ref[a, b, c] = enc[tap * 8 : tap * 8 + 8, c * 32 : c * 32 + 32]
                at = (tap * 3 + c) * 32
                dec_ref[a, b, c] = jnp.concatenate(
                    [lift[at : at + 32], skip[a * 3 + c][:, b * 32 : b * 32 + 32]], axis=1
                )


def pool_matrix():
    table = np.zeros((256, 3, 128), np.float32)
    for c, k in enumerate((-1, 0, 1)):
        for half in range(2):
            for q in range(64):
                for e in range(2):
                    z = 2 * q + e - k
                    if 0 <= z < 128:
                        table[half * 128 + z, c, half * 64 + q] = 1.0
    return jnp.asarray(table.reshape(256, 384), BF16)


def up_matrix():
    table = np.zeros((2, 128, 256), np.float32)
    for half in range(2):
        for z in range(128):
            table[:, half * 64 + z // 2, half * 128 + z] = 1.0
    return jnp.asarray(table.reshape(256, 256), BF16)


def both_ways(low, high, axis):
    ends = lax.axis_size(axis) - 1
    from_before = lax.ppermute(high, axis, [(i, i + 1) for i in range(ends)])
    from_after = lax.ppermute(low, axis, [(i + 1, i) for i in range(ends)])
    return from_before, from_after


def on_device(
    state_now, enc_pre, mid_pre, dec_pre, cotangent, enc_kernel, mid_kernel, dec_kernel, out_kernel
):
    state_now, enc_pre, mid_pre, dec_pre, cotangent = (
        v[0] for v in (state_now, enc_pre, mid_pre, dec_pre, cotangent)
    )
    cells = state_now[0].size * lax.axis_size("gx") * lax.axis_size("gy") * lax.axis_size("dp")
    grad_scale = 1.0 / math.sqrt(cells)
    pool = pool_matrix()
    dec_w = dec_kernel.transpose(2, 3, 4, 0, 1)
    mid_w = mid_kernel.transpose(2, 3, 4, 1, 0)
    enc_w = enc_kernel.transpose(2, 3, 4, 1, 0)

    plane = sds((24, 32, 128), BF16)
    delta_lo, delta_hi = call(
        face_body,
        [plane, plane],
        [
            pltpu.VMEM((2, 32, 24, 128), BF16),
            pltpu.VMEM((2, 8, 24, 128), BF16),
            pltpu.VMEM((8, 32), BF16),
            pltpu.VMEM((2, 24, 32, 128), BF16),
            pltpu.SemaphoreType.DMA((5,)),
            pltpu.SemaphoreType.DMA((2, 1)),
        ],
        (dec_pre, cotangent, out_kernel),
        200 << 20, 56, far=3, far_outs=2,
    )
    xlo, xhi = both_ways(delta_lo, delta_hi, "gx")
    mid_blocks = mid_pre.reshape(64, 2, 6, 2, 64).transpose(1, 2, 0, 3, 4).reshape(2, 6, 64, 128)
    (
        delta, head_grad, hidden, enc_slope, pooled, hidden_mid, mid_slope, state,
        tail_lo, tail_hi, pool_lo, pool_hi,
    ) = call(
        forward_body,
        [
            sds((2, 24, 32, 128), BF16),
            sds((8, 32), F32),
            sds((4, 24, 32, 128), BF16),
            sds((4, 24, 32, 128), F32),
            sds((2, 6, 32, 128), BF16),
            sds((2, 6, 64, 128), BF16),
            sds((2, 6, 64, 128), F32),
            sds((4, 24, 8, 128), F32),
            sds((96, 128), BF16),
            sds((96, 128), BF16),
            sds((192, 128), BF16),
            sds((192, 128), BF16),
        ],
        [],
        (dec_pre, cotangent, out_kernel, enc_pre, state_now, mid_blocks, pool),
        600 << 20, 16,
    )

    def column(at, tail):
        rows = (xlo[at], delta_lo[at], delta[0, at], delta[1, at], delta_hi[at], xhi[at], tail)
        return jnp.concatenate([v.reshape(-1, 128) for v in rows])

    ylo, yhi = both_ways(column(slice(0, 3), tail_lo), column(slice(21, 24), tail_hi), "gy")
    acc, wide, win, up, wskip, wmid, wup = call(
        inner_body,
        [
            sds((4, 26, 32, 128), F32),
            sds((6, 24, 96, 128), BF16),
            sds((864, 1024), BF16),
            sds((64, 1024), F32),
            sds((96, 288), BF16),
            sds((288, 192), BF16),
            sds((64, 864), BF16),
        ],
        [],
        (xlo, delta_lo, delta, delta_hi, xhi, pool, dec_w, mid_w),
        3 << 30, 24,
    )
    edge, rim_wide, rim_win, mid_wide, back, face_lo, face_hi = call(
        outer_body,
        [
            sds((4, 2, 32, 128), F32),
            sds((6, 2, 96, 128), BF16),
            sds((864, 768), BF16),
            sds((192, 1792), BF16),
            sds((2, 6, 32, 128), F32),
            sds((592, 128), BF16),
            sds((592, 128), BF16),
        ],
        [pltpu.VMEM((4, 6, 32, 128), F32)],
        (ylo, yhi, wide, up, mid_slope, state, pool_lo, pool_hi, pool, wup, wskip, wmid),
        1 << 30, 24,
    )
    got_lo, got_hi = both_ways(face_lo, face_hi, "gx")
    dec_rows, mid_grad = call(
        dec_grad_body,
        [sds((736, 128), BF16), sds((288, 192), F32)],
        [pltpu.VMEM((4, 28, 32, 128), BF16), pltpu.VMEM((288, 96), F32)],
        (wide, rim_wide, hidden, win, rim_win, hidden_mid, head_grad, pooled, mid_wide),
        3 << 30, 20,
    )
    dec_rows, mid_grad, got_lo, got_hi = lax.optimization_barrier((dec_rows, mid_grad, got_lo, got_hi))
    rows, own, face_lo, face_hi, edge_lo, edge_hi = call(
        encoder_body,
        [
            sds((1280, 128), BF16),
            sds((4, 24, 8, 128), F32),
            sds((208, 128), BF16),
            sds((208, 128), BF16),
            sds((4, 8, 128), F32),
            sds((4, 8, 128), F32),
        ],
        [
            pltpu.VMEM((96, 24 * 512), BF16),
            pltpu.VMEM((384, 256), F32),
            pltpu.VMEM((6, 26, 8, 128), F32),
            pltpu.VMEM((72, 96), F32),
            pltpu.VMEM((544, 128), BF16),
            pltpu.VMEM((6, 26, 8, 128), F32),
            pltpu.VMEM((72, 96), F32),
            pltpu.SemaphoreType.DMA((3, 1)),
        ],
        (
            acc, edge, back, ylo, yhi, got_lo, got_hi, enc_slope, enc_w, up_matrix(),
            mid_wide, mid_grad, state, dec_rows,
        ),
        2 << 30, 24, far_outs=1,
    )
    last_lo, last_hi = both_ways(face_lo, face_hi, "gx")

    axes = ("dp", "gx", "gy")
    count = lax.axis_size(axes)
    share = 1280 // count // 2
    pieces = lax.all_to_all(rows.reshape(count, share, 2, 128), axes, 0, 0)
    (shares,) = call(
        share_body,
        [sds(pieces.shape, BF16)],
        [
            pltpu.VMEM(pieces.shape, BF16),
            pltpu.VMEM((count // 8,) + pieces.shape[1:], BF16),
            pltpu.SemaphoreType.DMA((4,)),
            pltpu.SemaphoreType.DMA((8,)),
        ],
        (pieces,),
        1 << 20, 8, far=1, far_outs=1,
    )
    shares, last_lo, last_hi = lax.optimization_barrier((shares, last_lo, last_hi))
    rows = lax.all_to_all(shares, axes, 0, 0).reshape(1280, 128)
    col_lo, col_hi = call(
        corner_body, [sds((32, 128), BF16)] * 2, [], (edge_lo, edge_hi, last_lo, last_hi), 1 << 16, 4
    )
    end_lo, end_hi = both_ways(col_lo, col_hi, "gy")
    genc, gmid, gdec, ghead = call(
        functools.partial(unpack_body, grad_scale),
        [sds((3, 3, 3, 8, 32), F32), sds((3, 3, 3, 32, 64), F32), sds((3, 3, 3, 32, 96), F32), sds((8, 32), F32)],
        [],
        (rows,),
        1 << 20, 12,
    )
    genc, end_lo, end_hi = lax.optimization_barrier((genc, end_lo, end_hi))
    (state_grad,) = call(
        final_body,
        [sds((8, 4, 24, 128), BF16)],
        [],
        (cotangent, own, last_lo, last_hi, end_lo, end_hi),
        1 << 20, 8,
    )
    return (
        state_grad[None],
        genc.transpose(4, 3, 0, 1, 2),
        gmid.transpose(4, 3, 0, 1, 2),
        gdec.transpose(3, 4, 0, 1, 2),
        ghead,
    )


def solution(mesh):
    grid = P("dp", None, "gx", "gy", None)
    return jax.shard_map(
        on_device,
        mesh=mesh,
        in_specs=(grid,) * 5 + (P(),) * 4,
        out_specs=(grid, P(), P(), P(), P()),
        check_vma=False,
    )
```

```python
import functools
import math

import jax
import jax.numpy as jnp
import numpy as np
from jax import lax
from jax.experimental import pallas as pl
from jax.experimental.pallas import tpu as pltpu
from jax.sharding import PartitionSpec as P

F32 = jnp.float32
BF16 = jnp.bfloat16


VMEM = pl.BlockSpec(memory_space=pltpu.VMEM)
HBM = pl.BlockSpec(memory_space=pltpu.HBM)


def call(body, outs, scratch, args, flops, limit, far=0, far_outs=0):
    return pl.pallas_call(
        body,
        out_shape=outs,
        in_specs=[HBM] * far + [VMEM] * (len(args) - far),
        out_specs=[HBM] * far_outs + [VMEM] * (len(outs) - far_outs),
        scratch_shapes=scratch,
        compiler_params=pltpu.CompilerParams(vmem_limit_bytes=limit << 20),
        cost_estimate=pl.CostEstimate(flops=flops, bytes_accessed=4 << 20, transcendentals=0),
    )(*args)


def fetch(pairs, sems):
    copies = [pltpu.make_async_copy(src, dst, sems.at[i]) for i, (src, dst) in enumerate(pairs)]
    for copy in copies:
        copy.start()
    return [copy.wait for copy in copies]


def sds(shape, dtype):
    return jax.ShapeDtypeStruct(shape, dtype)


def dot(a, b):
    return lax.dot_general(a, b, (((1,), (0,)), ((), ())), preferred_element_type=F32)


def dot_tn(a, b):
    return lax.dot_general(a, b, (((0,), (0,)), ((), ())), preferred_element_type=F32)


def dot_nt(a, b):
    return lax.dot_general(a, b, (((1,), (1,)), ((), ())), preferred_element_type=F32)


def sigmoid(v):
    return 0.5 + 0.5 * jnp.tanh(0.5 * v)


def slope(v, s):
    return s * (1.0 + v * (1.0 - s))


def parity(axis):
    return jnp.bitwise_and(lax.axis_index(axis), 1)


def in_order(axis, first, second):
    odd = parity(axis) == 1
    return jnp.where(odd, first, second), jnp.where(odd, second, first)


def lane_ids(shape):
    return lax.broadcasted_iota(jnp.int32, shape, len(shape) - 1)


def shifts(v, period):
    lane = jnp.bitwise_and(lane_ids(v.shape), period - 1)
    axis = v.ndim - 1
    size = v.shape[-1]
    back = jnp.where(lane == period - 1, 0.0, pltpu.roll(v, size - 1, axis))
    ahead = jnp.where(lane == 0, 0.0, pltpu.roll(v, 1, axis))
    return back, v, ahead


def delta_plane(dec, cot, head):
    pre = jnp.swapaxes(dec.astype(F32), 0, 1)
    cot = jnp.swapaxes(cot.astype(F32), 0, 1)
    cot_lanes = jnp.concatenate([cot[y] for y in range(24)], axis=1).astype(BF16)
    back = dot_tn(head, cot_lanes)
    back = jnp.stack([back[:, y * 128 : y * 128 + 128] for y in range(24)], axis=0)
    s = sigmoid(pre)
    return (back * slope(pre, s)).astype(BF16), cot_lanes, pre * s


def face_body(dec_far, cot_far, head_far, first_far, second_far, dec_ref, cot_ref, head_ref, delta_ref, sems, out_sems):
    odd = parity("gx")
    planes = (3 - 3 * odd, 3 * odd)
    pairs = [(head_far, head_ref)]
    for i, x in enumerate(planes):
        pairs += [(cot_far.at[:, x], cot_ref.at[i]), (dec_far.at[:, x], dec_ref.at[i])]
    waits = fetch(pairs, sems)
    waits[0]()
    writes = []
    for i, far in enumerate((first_far, second_far)):
        waits[2 * i + 1]()
        waits[2 * i + 2]()
        delta_ref[i] = delta_plane(dec_ref[i], cot_ref[i], head_ref[...])[0]
        writes += fetch([(delta_ref.at[i], far)], out_sems.at[i])
    for wait in writes:
        wait()


def forward_body(
    dec_ref, cot_ref, head_ref, enc_ref, state_ref, mid_ref, pool_ref,
    delta_ref, head_grad_ref, hid_ref, slope_ref, pooled_ref, hmid_ref, mslope_ref, st_ref, ylo_ref, yhi_ref,
):
    total = jnp.zeros((8, 32), F32)
    for x in range(4):
        delta, cot_lanes, decoded = delta_plane(dec_ref[:, x], cot_ref[:, x], head_ref[...])
        if x in (1, 2):
            delta_ref[x - 1] = delta
        decoded = jnp.concatenate([decoded[y] for y in range(24)], axis=1).astype(BF16)
        total = total + dot_nt(cot_lanes, decoded)
    head_grad_ref[...] = total
    low_rows, high_rows = [], []
    for x in range(4):
        pre = jnp.swapaxes(enc_ref[:, x].astype(F32), 0, 1)
        s = sigmoid(pre)
        hid_ref[x] = (pre * s).astype(BF16)
        slope_ref[x] = slope(pre, s)
        state = jnp.swapaxes(state_ref[:, x].astype(F32), 0, 1)
        st_ref[x] = state
        low_rows.append(state[0])
        high_rows.append(state[23])
    ylo_ref[64:96, :] = jnp.concatenate(low_rows, axis=0).astype(BF16)
    yhi_ref[64:96, :] = jnp.concatenate(high_rows, axis=0).astype(BF16)
    tilts = {}
    for bx in range(2):
        for m in range(6):
            acc = None
            for ex in range(2):
                for ey in range(2):
                    pair = jnp.concatenate(
                        [hid_ref[2 * bx + ex, 4 * m + ey], hid_ref[2 * bx + ex, 4 * m + 2 + ey]], axis=1
                    )
                    part = dot(pair, pool_ref[:, 128:256])
                    acc = part if acc is None else acc + part
            pooled = (acc * 0.125).astype(BF16)
            pooled_ref[bx, m] = pooled
            pre = mid_ref[bx, m].astype(F32)
            s = sigmoid(pre)
            hmid_ref[bx, m] = (pre * s).astype(BF16)
            tilts[bx, m] = slope(pre, s)
            mslope_ref[bx, m] = tilts[bx, m]
    lower = lane_ids((64, 128)) < 64
    ylo_ref[0:64, :] = jnp.where(lower, tilts[0, 0], pltpu.roll(tilts[1, 0], 64, 1)).astype(BF16)
    yhi_ref[0:64, :] = jnp.where(lower, pltpu.roll(tilts[0, 5], 64, 1), tilts[1, 5]).astype(BF16)


def window_sums(rows_of, pool, put):
    got = dot(
        jnp.concatenate([jnp.concatenate([rows_of(x, j) for j in range(4)], axis=0) for x in range(6)], axis=0), pool
    )
    sums = []
    for x in range(6):
        at = [got[x * 128 + j * 32 : x * 128 + j * 32 + 32] for j in range(4)]
        sums.append([at[j] + at[j + 1] for j in (2, 1, 0)])
    for bx in range(2):
        for a, kx in enumerate((-1, 0, 1)):
            for b in range(3):
                both = (sums[2 * bx - kx + 1][b] + sums[2 * bx - kx + 2][b]).astype(BF16)
                for c in range(3):
                    put(bx, ((a * 3 + b) * 3 + c) * 32, both[:, c * 128 : c * 128 + 128])


def stack_of(row):
    return jnp.concatenate(
        [jnp.concatenate([row(x + 1 - kx) for x in range(4)], axis=1) for kx in (-1, 0, 1)], axis=0
    )


def skip_weights(w_ref):
    parts = [
        jnp.concatenate([w_ref[a, b].astype(F32).reshape(96, 96)[:, 64:96] for b in range(3)], axis=1)
        for a in range(3)
    ]
    return jnp.concatenate(parts, axis=0).T.astype(BF16)


def inner_body(got1_ref, face1_ref, delta_ref, face2_ref, got2_ref, pool_ref, w_ref, wmid_ref, acc_ref, wide_ref, win_ref, up_ref, wskip_ref, wm_ref, wup_ref):
    def put(x, v):
        parts = shifts(v.astype(F32).reshape(768, 128), 128)
        for a in range(3):
            wide_ref[x, :, a * 32 : a * 32 + 32, :] = parts[a].astype(BF16).reshape(24, 32, 128)

    odd = parity("gx")
    put(5 - 5 * odd, got1_ref[...])
    put(4 - 3 * odd, face1_ref[...])
    put(2, delta_ref[0])
    put(3, delta_ref[1])
    put(1 + 3 * odd, face2_ref[...])
    put(5 * odd, got2_ref[...])
    wskip_ref[...] = skip_weights(w_ref)
    acc_ref[...] = jnp.zeros(acc_ref.shape, F32)

    def step(i, carry):
        y = 4 * i
        out = dot(
            wskip_ref[...],
            jnp.concatenate([stack_of(lambda x, j=j: wide_ref[x, y + j]) for j in range(4)], axis=1),
        )
        for x in range(4):
            for r in range(6):
                parts = [
                    out[b * 32 : b * 32 + 32, ((r - b) * 4 + x) * 128 : ((r - b) * 4 + x) * 128 + 128]
                    for b in range(3)
                    if 0 <= r - b < 4
                ]
                acc_ref[x, y + r] += sum(parts[1:], parts[0])
        return carry

    lax.fori_loop(0, 6, step, 0)
    for m in range(1, 5):

        def rows_of(x, j):
            return jnp.concatenate(
                [wide_ref[x, 4 * m + j - 1, 32:64, :], wide_ref[x, 4 * m + j + 1, 32:64, :]], axis=1
            )

        def put_window(bx, row, v):
            lane = (bx * 4 + m - 1) * 128
            win_ref[row : row + 32, lane : lane + 128] = v

        window_sums(rows_of, pool_ref[...], put_window)
    wup_ref[...] = w_ref[...].reshape(864, 96).astype(F32).T[:64].astype(BF16)
    up_ref[...] = dot(wup_ref[...], win_ref[...])
    for a in range(3):
        for b in range(3):
            at = (a * 3 + b) * 32
            parts = [wmid_ref[a, b, c].astype(F32) for c in range(3)]
            wm_ref[at : at + 32, :] = jnp.concatenate(parts, axis=1).astype(BF16)


def outer_body(
    got1_ref, got2_ref, wide_ref, up_ref, mslope_ref, st_ref, pooled_ref, pool_ref, wup_ref, wskip_ref, wm_ref,
    edge_ref, rim_ref, win_ref, mid_ref, back_ref, face1_ref, face2_ref,
    total_ref, got_ref,
):
    wskip = wskip_ref[...]
    odd_x, odd_y = parity("gx"), parity("gy")
    got_ref[1 - odd_y] = got1_ref[...]
    got_ref[odd_y] = got2_ref[...]

    def row(x, y):
        if 0 <= y <= 23:
            return wide_ref[x, y, 32:64, :]
        slot = x + (1 - odd_x) * (5, 3, 0, 0, -3, -5)[x]
        at = (slot * 3 + (y + 3 if y < 0 else y - 24)) * 32
        return got_ref[0 if y < 0 else 1, pl.ds(pl.multiple_of(at, 32), 32), :]

    for x in range(6):
        v = jnp.concatenate([row(x, -1), row(x, 24)], axis=0).astype(F32)
        parts = shifts(v, 128)
        for a in range(3):
            rim_ref[x, :, a * 32 : a * 32 + 32, :] = parts[a].astype(BF16).reshape(2, 32, 128)
    outs = [dot(wskip, stack_of(lambda x, r=r: rim_ref[x, r])) for r in range(2)]
    for x in range(4):
        at = slice(x * 128, x * 128 + 128)
        edge_ref[x, 0] = outs[0][64:96, at]
        edge_ref[x, 1] = outs[1][0:32, at]

    for i, (left, right) in enumerate(((-1, 1), (19, 21), (23, -3))):

        def rows_of(x, j):
            return jnp.concatenate([row(x, left + j), row(x, right + j)], axis=1)

        def put_window(bx, r, v):
            lane = (bx * 3 + i) * 128
            win_ref[r : r + 32, lane : lane + 128] = v

        window_sums(rows_of, pool_ref[...], put_window)
    rim_up = dot(wup_ref[...], win_ref[...])

    upper = lane_ids((64, 128)) >= 64
    before = got_ref[0, 576:640, :].astype(F32)
    after = got_ref[1, 576:640, :].astype(F32)
    rim_tilt = (
        jnp.where(upper, pltpu.roll(before, 64, 1), after),
        jnp.where(upper, before, pltpu.roll(after, 64, 1)),
    )
    for bx in range(2):
        for m in range(7):
            if 1 <= m <= 4:
                lane = (bx * 4 + m - 1) * 128
                v = up_ref[:, lane : lane + 128]
            else:
                lane = (bx * 3 + (0, 5, 6).index(m)) * 128
                v = rim_up[:, lane : lane + 128]
            tilt = rim_tilt[bx] if m == 6 else mslope_ref[bx, m]
            delta = (v * tilt).astype(BF16).astype(F32)
            lane = (bx * 7 + m) * 128
            for a, part in enumerate(shifts(delta, 64)):
                mid_ref[a * 64 : a * 64 + 64, lane : lane + 128] = part.astype(BF16)

    out = dot(wm_ref[...], mid_ref[...])
    upper = lane_ids((32, 128)) >= 64

    def term(a, b, x, m):
        if not 0 <= x - a < 2:
            return None
        col = ((x - a) * 7 + m) * 128
        return out[(a * 3 + b) * 32 : (a * 3 + b) * 32 + 32, col : col + 128]

    def tap_sum(b, x, m):
        parts = [v for v in (term(a, b, x, m) for a in range(3)) if v is not None]
        return sum(parts[1:], parts[0])

    for x in range(4):
        downs = [pltpu.roll(tap_sum(0, x, m), 64, 1) for m in range(7)]
        ups = [pltpu.roll(tap_sum(2, x, m), 64, 1) for m in range(7)]
        for m in range(6):
            low = ups[(m + 6) % 7] + downs[m]
            high = ups[m] + downs[m + 1]
            total_ref[x, m] = tap_sum(1, x, m) + jnp.where(upper, high, low)
    back_ref[...] = total_ref[1:3, 0:6]
    before = got_ref[0, 640:672, :].astype(F32)
    after = got_ref[1, 640:672, :].astype(F32)
    for face_ref, last in ((face1_ref, 1 - odd_x), (face2_ref, odd_x)):
        face_ref[0:192, :] = total_ref[3 * last].astype(BF16).reshape(192, 128)
        face_ref[192:384, :] = pooled_ref[last].reshape(192, 128)
        rows = (
            jnp.where(last == 1, before[24:32], before[0:8]),
            st_ref[3 * last].reshape(192, 128),
            jnp.where(last == 1, after[24:32], after[0:8]),
        )
        face_ref[384:592, :] = jnp.concatenate(rows, axis=0).astype(BF16)


def hidden_rows(hid_ref, ys):
    def tap(x, y):
        return hid_ref[x, y + 2]

    return jnp.concatenate(
        [jnp.concatenate([tap(x, y + b - 1) for y in ys for x in range(4)], axis=1) for b in range(3)], axis=0
    )


def pooled_taps(blocks):
    blocks = blocks + [jnp.zeros((32, 128), F32)]
    lower = lane_ids((32, 128)) < 64
    turned = [pltpu.roll(v, 64, 1) for v in blocks]
    taps = (
        [jnp.where(lower, turned[(m + 6) % 7], turned[m]) for m in range(7)],
        blocks,
        [jnp.where(lower, turned[m], turned[(m + 1) % 7]) for m in range(7)],
    )
    return jnp.concatenate([jnp.concatenate(v, axis=1) for v in taps], axis=0).astype(BF16)


def dec_grad_body(
    wide_ref, rim_ref, hid_ref, win_ref, rim_win_ref, hmid_ref, head_ref, pooled_ref, mid_ref,
    rows_ref, gmid_ref, hpad_ref, skip_ref,
):
    blank = jnp.zeros((2, 32, 128), BF16)
    for x in range(4):
        hpad_ref[x, 0:2] = blank
        hpad_ref[x, 26:28] = blank
        hpad_ref[x, 2:26] = hid_ref[x]
    rims = jnp.concatenate([stack_of(lambda x, r=r: rim_ref[x, r]) for r in (0, 1)], axis=1)
    skip_ref[...] = dot_nt(rims, hidden_rows(hpad_ref, (-1, 24)))

    def step(i, carry):
        y = 4 * i
        rows = jnp.concatenate([stack_of(lambda x, j=j: wide_ref[x, y + j]) for j in range(4)], axis=1)
        skip_ref[...] += dot_nt(rows, hidden_rows(hpad_ref, [y + j for j in range(4)]))
        return carry

    lax.fori_loop(0, 6, step, 0)
    rows_ref[0:288, :] = jnp.concatenate([skip_ref[...], jnp.zeros((288, 32), F32)], axis=1).astype(BF16)

    def side(bx, m):
        if 1 <= m <= 4:
            at = (bx * 4 + m - 1) * 128
            return win_ref[:, at : at + 128]
        at = (bx * 3 + (0 if m == 0 else 1)) * 128
        return rim_win_ref[:, at : at + 128]

    order = [(bx, m) for bx in range(2) for m in range(6)]
    windows = jnp.concatenate([side(bx, m) for bx, m in order], axis=1)
    hmid = jnp.concatenate([hmid_ref[bx, m] for bx, m in order], axis=1)
    lift = dot_nt(windows, hmid)
    rows_ref[288:720, :] = jnp.concatenate([lift[0:432], lift[432:864]], axis=1).astype(BF16)
    rows_ref[720:736, :] = jnp.concatenate(
        [jnp.concatenate([head_ref[...], jnp.zeros((8, 96), F32)], axis=1), jnp.zeros((8, 128), F32)], axis=0
    ).astype(BF16)
    taps = [pooled_taps([pooled_ref[bx, m].astype(F32) for m in range(6)]) for bx in range(2)]
    first, second = mid_ref[:, 0:896], mid_ref[:, 896:1792]
    gmid_ref[0:96, :] = dot_nt(taps[0], second)
    gmid_ref[96:192, :] = dot_nt(taps[0], first) + dot_nt(taps[1], second)
    gmid_ref[192:288, :] = dot_nt(taps[1], first)


def encoder_body(
    acc_ref, edge_ref, back_ref, rim1_ref, rim2_ref, got1_ref, got2_ref, slope_ref, w_ref, up_ref,
    mid_ref, gmid_ref, st_ref, dec_ref,
    rows_far, own_ref, face1_ref, face2_ref, edge_lo_ref, edge_hi_ref,
    enc_ref, wide_ref, total_ref, we_ref, rows_ref, sext_ref, sum_ref, got_ref, sems,
):
    odd_x = parity("gx")
    got_ref[1 - odd_x] = got1_ref[...]
    got_ref[odd_x] = got2_ref[...]
    got_lo_ref, got_hi_ref = got_ref.at[0], got_ref.at[1]
    writes = fetch([(dec_ref, rows_far.at[0:736])], sems.at[0])

    def beyond(ref):
        side = ref[192:384, :].astype(F32)
        return pooled_taps([side[m * 32 : m * 32 + 32] for m in range(6)])

    gmid = jnp.concatenate(
        [
            gmid_ref[0:96, :] + dot_nt(beyond(got_lo_ref), mid_ref[:, 0:896]),
            gmid_ref[96:192, :],
            gmid_ref[192:288, :] + dot_nt(beyond(got_hi_ref), mid_ref[:, 896:1792]),
        ],
        axis=0,
    )
    rows_ref[0:288, :] = gmid[:, :128].astype(BF16)
    rows_ref[288:432, :] = jnp.concatenate([gmid[:144, 128:], gmid[144:, 128:]], axis=1).astype(BF16)
    writes += fetch([(rows_ref.at[0:432], rows_far.at[736:1168])], sems.at[1])

    sext_ref[1:5, 1:25] = st_ref[...]
    sext_ref[0] = got_lo_ref[384:592, :].astype(F32).reshape(26, 8, 128)
    sext_ref[5] = got_hi_ref[384:592, :].astype(F32).reshape(26, 8, 128)
    before, after = in_order("gy", rim1_ref[640:672, :].astype(F32), rim2_ref[640:672, :].astype(F32))
    for x in range(4):
        sext_ref[x + 1, 0] = before[x * 8 : x * 8 + 8]
        sext_ref[x + 1, 25] = after[x * 8 : x * 8 + 8]

    whole = [back_ref[bx].reshape(192, 128) for bx in range(2)]
    whole = [v + ref[0:192, :].astype(F32) for v, ref in zip(whole, (got_lo_ref, got_hi_ref))]
    whole = jnp.concatenate(whole, axis=0) * 0.125
    high = whole.astype(BF16)
    low = (whole - high.astype(F32)).astype(BF16)
    wide_ref[...] = dot(jnp.concatenate([high, low], axis=1), up_ref[...])
    for bx in range(2):
        for m in range(6):
            at = (bx * 6 + m) * 32
            for half in range(2):
                fine = wide_ref[at : at + 32, half * 128 : half * 128 + 128]
                for ey in range(2):
                    y = 4 * m + 2 * half + ey
                    for ex in range(2):
                        x = 2 * bx + ex
                        sum_in = acc_ref[x, y + 1] + fine
                        if y in (0, 23):
                            sum_in = sum_in + edge_ref[x, (0, 23).index(y)]
                        delta = (sum_in * slope_ref[x, y]).astype(BF16).astype(F32)
                        lane = (y * 4 + x) * 128
                        for c, part in enumerate(shifts(delta, 128)):
                            enc_ref[c * 32 : c * 32 + 32, lane : lane + 128] = part.astype(BF16)

    for a in range(3):
        for b in range(3):
            at = (a * 3 + b) * 8
            we_ref[at : at + 8, :] = jnp.concatenate([w_ref[a, b, c].astype(F32) for c in range(3)], axis=1)
    w = we_ref[...].astype(BF16)
    total_ref[...] = jnp.zeros(total_ref.shape, F32)
    sum_ref[...] = jnp.zeros(sum_ref.shape, F32)

    def step(i, carry):
        y = 4 * i
        delta = enc_ref[:, pl.ds(pl.multiple_of(y * 512, 2048), 2048)]
        state = jnp.concatenate(
            [
                jnp.concatenate([sext_ref[x + a, y + j + b] for j in range(4) for x in range(4)], axis=1)
                for a in range(3)
                for b in range(3)
            ],
            axis=0,
        ).astype(BF16)
        sum_ref[...] += dot_nt(state, delta)
        out = dot(w, delta)
        for x in range(6):
            for r in range(6):
                parts = []
                for a in range(3):
                    for b in range(3):
                        j, own = r - b, x - a
                        if 0 <= j < 4 and 0 <= own < 4:
                            row, lane = (a * 3 + b) * 8, (j * 4 + own) * 128
                            parts.append(out[row : row + 8, lane : lane + 128])
                total_ref[x, y + r] += sum(parts[1:], parts[0])
        return carry

    lax.fori_loop(0, 6, step, 0, unroll=3)
    genc = jnp.concatenate([sum_ref[...], jnp.zeros((72, 32), F32)], axis=1)
    rows_ref[432:544, :] = jnp.concatenate([genc, jnp.zeros((40, 128), F32)], axis=0).astype(BF16)
    writes += fetch([(rows_ref.at[432:544], rows_far.at[1168:1280])], sems.at[2])
    own_ref[...] = total_ref[1:5, 1:25]
    face1_ref[...] = total_ref[5 - 5 * odd_x].reshape(208, 128).astype(BF16)
    face2_ref[...] = total_ref[5 * odd_x].reshape(208, 128).astype(BF16)
    edge_lo_ref[...] = total_ref[1:5, 0]
    edge_hi_ref[...] = total_ref[1:5, 25]
    for wait in writes:
        wait()


def corner_body(edge_lo_ref, edge_hi_ref, got1_ref, got2_ref, col1_ref, col2_ref):
    before, after = in_order("gx", got1_ref[...].astype(F32), got2_ref[...].astype(F32))
    cols = []
    for edge_ref, at in ((edge_lo_ref, 0), (edge_hi_ref, 200)):
        rows = [edge_ref[0] + before[at : at + 8], edge_ref[1], edge_ref[2], edge_ref[3] + after[at : at + 8]]
        cols.append(jnp.concatenate(rows, axis=0))
    first, second = in_order("gy", *cols)
    col1_ref[...] = first.astype(BF16)
    col2_ref[...] = second.astype(BF16)


def final_body(cot_ref, own_ref, got1_ref, got2_ref, end1_ref, end2_ref, grad_ref):
    sides = in_order("gx", got1_ref[...].astype(F32), got2_ref[...].astype(F32))
    before, after = in_order("gy", end1_ref[...].astype(F32), end2_ref[...].astype(F32))
    for x in range(4):
        total = own_ref[x]
        if x in (0, 3):
            total = total + sides[x // 3][8:200].reshape(24, 8, 128)
        at = slice(x * 8, x * 8 + 8)
        ends = [before[at][None], jnp.zeros((22, 8, 128), F32), after[at][None]]
        total = total + jnp.concatenate(ends, axis=0)
        grad_ref[:, x] = (cot_ref[:, x].astype(F32) + jnp.swapaxes(total, 0, 1)).astype(BF16)


def share_body(pieces_far, out_far, pieces_ref, copies_ref, sems, out_sems):
    count = pieces_ref.shape[0]
    part = count // 4
    spans = [pl.ds(i * part, part) for i in range(4)]
    waits = fetch([(pieces_far.at[span], pieces_ref.at[span]) for span in spans], sems)
    total = jnp.zeros(pieces_ref.shape[1:], F32)
    for i, wait in enumerate(waits):
        wait()
        for j in range(part):
            total = total + pieces_ref[i * part + j].astype(F32)
    total = total.astype(BF16)
    part = copies_ref.shape[0]
    for j in range(part):
        copies_ref[j] = total
    for wait in fetch([(copies_ref, out_far.at[pl.ds(i * part, part)]) for i in range(count // part)], out_sems):
        wait()


def unpack_body(scale, rows_ref, enc_ref, mid_ref, dec_ref, head_ref):
    def rows(at, count):
        return rows_ref[at : at + count, :].astype(F32) * scale

    skip = [rows(i * 32, 32) for i in range(9)]
    head_ref[...] = rows(720, 16)[:8, :32]
    mid_rest = [rows(1024 + i * 48, 48) for i in range(3)]
    mid_rest = jnp.concatenate(mid_rest, axis=0)
    mid_rest = jnp.concatenate([mid_rest[:, :64], mid_rest[:, 64:]], axis=0)
    enc = rows(1168, 80)
    lift = rows(288, 432)
    lift = jnp.concatenate([lift[:, :64], lift[:, 64:]], axis=0)
    for a in range(3):
        for b in range(3):
            tap = a * 3 + b
            pair = rows(736 + tap * 32, 32)
            mid_ref[a, b, 0] = pair[:, :64]
            mid_ref[a, b, 1] = pair[:, 64:]
            mid_ref[a, b, 2] = mid_rest[tap * 32 : tap * 32 + 32]
            for c in range(3):
                enc_ref[a, b, c] = enc[tap * 8 : tap * 8 + 8, c * 32 : c * 32 + 32]
                at = (tap * 3 + c) * 32
                dec_ref[a, b, c] = jnp.concatenate(
                    [lift[at : at + 32], skip[a * 3 + c][:, b * 32 : b * 32 + 32]], axis=1
                )


def pool_matrix():
    table = np.zeros((256, 3, 128), np.float32)
    for c, k in enumerate((-1, 0, 1)):
        for half in range(2):
            for q in range(64):
                for e in range(2):
                    z = 2 * q + e - k
                    if 0 <= z < 128:
                        table[half * 128 + z, c, half * 64 + q] = 1.0
    return jnp.asarray(table.reshape(256, 384), BF16)


def up_matrix():
    table = np.zeros((2, 128, 256), np.float32)
    for half in range(2):
        for z in range(128):
            table[:, half * 64 + z // 2, half * 128 + z] = 1.0
    return jnp.asarray(table.reshape(256, 256), BF16)


def swaps(first, second, axis):
    count = lax.axis_size(axis)
    pairs = [(i, i + 1) for i in range(0, count - 1, 2)], [(i, i + 1) for i in range(1, count - 1, 2)]
    return tuple(
        lax.ppermute(v, axis, ahead + [(b, a) for a, b in ahead]) for v, ahead in zip((first, second), pairs)
    )


def on_device(
    state_now, enc_pre, mid_pre, dec_pre, cotangent, enc_kernel, mid_kernel, dec_kernel, out_kernel
):
    state_now, enc_pre, mid_pre, dec_pre, cotangent = (
        v[0] for v in (state_now, enc_pre, mid_pre, dec_pre, cotangent)
    )
    cells = state_now[0].size * lax.axis_size("gx") * lax.axis_size("gy") * lax.axis_size("dp")
    grad_scale = 1.0 / math.sqrt(cells)
    pool = pool_matrix()
    dec_w = dec_kernel.transpose(2, 3, 4, 0, 1)
    mid_w = mid_kernel.transpose(2, 3, 4, 1, 0)
    enc_w = enc_kernel.transpose(2, 3, 4, 1, 0)

    plane = sds((24, 32, 128), BF16)
    face1, face2 = call(
        face_body,
        [plane, plane],
        [
            pltpu.VMEM((2, 32, 24, 128), BF16),
            pltpu.VMEM((2, 8, 24, 128), BF16),
            pltpu.VMEM((8, 32), BF16),
            pltpu.VMEM((2, 24, 32, 128), BF16),
            pltpu.SemaphoreType.DMA((5,)),
            pltpu.SemaphoreType.DMA((2, 1)),
        ],
        (dec_pre, cotangent, out_kernel),
        200 << 20, 56, far=3, far_outs=2,
    )
    got1, got2 = swaps(face1, face2, "gx")
    mid_blocks = mid_pre.reshape(64, 2, 6, 2, 64).transpose(1, 2, 0, 3, 4).reshape(2, 6, 64, 128)
    (
        delta, head_grad, hidden, enc_slope, pooled, hidden_mid, mid_slope, state,
        tail_lo, tail_hi,
    ) = call(
        forward_body,
        [
            sds((2, 24, 32, 128), BF16),
            sds((8, 32), F32),
            sds((4, 24, 32, 128), BF16),
            sds((4, 24, 32, 128), F32),
            sds((2, 6, 32, 128), BF16),
            sds((2, 6, 64, 128), BF16),
            sds((2, 6, 64, 128), F32),
            sds((4, 24, 8, 128), F32),
            sds((96, 128), BF16),
            sds((96, 128), BF16),
        ],
        [],
        (dec_pre, cotangent, out_kernel, enc_pre, state_now, mid_blocks, pool),
        600 << 20, 16,
    )

    odd_y = parity("gy")

    def column(start, tail):
        planes = (got1, face1, delta[0], delta[1], face2, got2)
        rows = [lax.dynamic_slice_in_dim(v, start, 3, axis=0).reshape(96, 128) for v in planes]
        return jnp.concatenate(rows + [tail])

    tails = in_order("gy", tail_lo, tail_hi)
    rim1, rim2 = swaps(column(21 - 21 * odd_y, tails[0]), column(21 * odd_y, tails[1]), "gy")
    acc, wide, win, up, wskip, wmid, wup = call(
        inner_body,
        [
            sds((4, 26, 32, 128), F32),
            sds((6, 24, 96, 128), BF16),
            sds((864, 1024), BF16),
            sds((64, 1024), F32),
            sds((96, 288), BF16),
            sds((288, 192), BF16),
            sds((64, 864), BF16),
        ],
        [],
        (got1, face1, delta, face2, got2, pool, dec_w, mid_w),
        3 << 30, 24,
    )
    edge, rim_wide, rim_win, mid_wide, back, face1, face2 = call(
        outer_body,
        [
            sds((4, 2, 32, 128), F32),
            sds((6, 2, 96, 128), BF16),
            sds((864, 768), BF16),
            sds((192, 1792), BF16),
            sds((2, 6, 32, 128), F32),
            sds((592, 128), BF16),
            sds((592, 128), BF16),
        ],
        [pltpu.VMEM((4, 6, 32, 128), F32), pltpu.VMEM((2, 672, 128), BF16)],
        (rim1, rim2, wide, up, mid_slope, state, pooled, pool, wup, wskip, wmid),
        1 << 30, 24,
    )
    got1, got2 = swaps(face1, face2, "gx")
    dec_rows, mid_grad = call(
        dec_grad_body,
        [sds((736, 128), BF16), sds((288, 192), F32)],
        [pltpu.VMEM((4, 28, 32, 128), BF16), pltpu.VMEM((288, 96), F32)],
        (wide, rim_wide, hidden, win, rim_win, hidden_mid, head_grad, pooled, mid_wide),
        3 << 30, 20,
    )
    dec_rows, mid_grad, got1, got2 = lax.optimization_barrier((dec_rows, mid_grad, got1, got2))
    rows, own, face1, face2, edge_lo, edge_hi = call(
        encoder_body,
        [
            sds((1280, 128), BF16),
            sds((4, 24, 8, 128), F32),
            sds((208, 128), BF16),
            sds((208, 128), BF16),
            sds((4, 8, 128), F32),
            sds((4, 8, 128), F32),
        ],
        [
            pltpu.VMEM((96, 24 * 512), BF16),
            pltpu.VMEM((384, 256), F32),
            pltpu.VMEM((6, 26, 8, 128), F32),
            pltpu.VMEM((72, 96), F32),
            pltpu.VMEM((544, 128), BF16),
            pltpu.VMEM((6, 26, 8, 128), F32),
            pltpu.VMEM((72, 96), F32),
            pltpu.VMEM((2, 592, 128), BF16),
            pltpu.SemaphoreType.DMA((3, 1)),
        ],
        (
            acc, edge, back, rim1, rim2, got1, got2, enc_slope, enc_w, up_matrix(),
            mid_wide, mid_grad, state, dec_rows,
        ),
        2 << 30, 24, far_outs=1,
    )
    last1, last2 = swaps(face1, face2, "gx")

    axes = ("dp", "gx", "gy")
    count = lax.axis_size(axes)
    share = 1280 // count // 2
    pieces = lax.all_to_all(rows.reshape(count, share, 2, 128), axes, 0, 0)
    (shares,) = call(
        share_body,
        [sds(pieces.shape, BF16)],
        [
            pltpu.VMEM(pieces.shape, BF16),
            pltpu.VMEM((count // 8,) + pieces.shape[1:], BF16),
            pltpu.SemaphoreType.DMA((4,)),
            pltpu.SemaphoreType.DMA((8,)),
        ],
        (pieces,),
        1 << 20, 8, far=1, far_outs=1,
    )
    shares, last1, last2 = lax.optimization_barrier((shares, last1, last2))
    rows = lax.all_to_all(shares, axes, 0, 0).reshape(1280, 128)
    col1, col2 = call(
        corner_body, [sds((32, 128), BF16)] * 2, [], (edge_lo, edge_hi, last1, last2), 1 << 16, 4
    )
    end1, end2 = swaps(col1, col2, "gy")
    genc, gmid, gdec, ghead = call(
        functools.partial(unpack_body, grad_scale),
        [sds((3, 3, 3, 8, 32), F32), sds((3, 3, 3, 32, 64), F32), sds((3, 3, 3, 32, 96), F32), sds((8, 32), F32)],
        [],
        (rows,),
        1 << 20, 12,
    )
    genc, end1, end2 = lax.optimization_barrier((genc, end1, end2))
    (state_grad,) = call(
        final_body,
        [sds((8, 4, 24, 128), BF16)],
        [],
        (cotangent, own, last1, last2, end1, end2),
        1 << 20, 8,
    )
    return (
        state_grad[None],
        genc.transpose(4, 3, 0, 1, 2),
        gmid.transpose(4, 3, 0, 1, 2),
        gdec.transpose(3, 4, 0, 1, 2),
        ghead,
    )


def solution(mesh):
    grid = P("dp", None, "gx", "gy", None)
    return jax.shard_map(
        on_device,
        mesh=mesh,
        in_specs=(grid,) * 5 + (P(),) * 4,
        out_specs=(grid, P(), P(), P(), P()),
        check_vma=False,
    )
```

```python
import functools
import math

import jax
import jax.numpy as jnp
import numpy as np
from jax import lax
from jax.experimental import pallas as pl
from jax.experimental.pallas import tpu as pltpu
from jax.sharding import PartitionSpec as P

F32 = jnp.float32
BF16 = jnp.bfloat16


VMEM = pl.BlockSpec(memory_space=pltpu.VMEM)
HBM = pl.BlockSpec(memory_space=pltpu.HBM)


def call(body, outs, scratch, args, flops, limit, far=0, far_outs=0):
    return pl.pallas_call(
        body,
        out_shape=outs,
        in_specs=[HBM] * far + [VMEM] * (len(args) - far),
        out_specs=[HBM] * far_outs + [VMEM] * (len(outs) - far_outs),
        scratch_shapes=scratch,
        compiler_params=pltpu.CompilerParams(vmem_limit_bytes=limit << 20),
        cost_estimate=pl.CostEstimate(flops=flops, bytes_accessed=4 << 20, transcendentals=0),
    )(*args)


def fetch(pairs, sems):
    copies = [pltpu.make_async_copy(src, dst, sems.at[i]) for i, (src, dst) in enumerate(pairs)]
    for copy in copies:
        copy.start()
    return [copy.wait for copy in copies]


def sds(shape, dtype):
    return jax.ShapeDtypeStruct(shape, dtype)


def dot(a, b):
    return lax.dot_general(a, b, (((1,), (0,)), ((), ())), preferred_element_type=F32)


def dot_tn(a, b):
    return lax.dot_general(a, b, (((0,), (0,)), ((), ())), preferred_element_type=F32)


def dot_nt(a, b):
    return lax.dot_general(a, b, (((1,), (1,)), ((), ())), preferred_element_type=F32)


def sigmoid(v):
    return 0.5 + 0.5 * jnp.tanh(0.5 * v)


def slope(v, s):
    return s * (1.0 + v * (1.0 - s))


def parity(axis):
    return jnp.bitwise_and(lax.axis_index(axis), 1)


def in_order(axis, first, second):
    odd = parity(axis) == 1
    return jnp.where(odd, first, second), jnp.where(odd, second, first)


def lane_ids(shape):
    return lax.broadcasted_iota(jnp.int32, shape, len(shape) - 1)


def shifts(v, period):
    lane = jnp.bitwise_and(lane_ids(v.shape), period - 1)
    axis = v.ndim - 1
    size = v.shape[-1]
    back = jnp.where(lane == period - 1, 0.0, pltpu.roll(v, size - 1, axis))
    ahead = jnp.where(lane == 0, 0.0, pltpu.roll(v, 1, axis))
    return back, v, ahead


def delta_plane(dec, cot, head):
    pre = jnp.swapaxes(dec.astype(F32), 0, 1)
    cot = jnp.swapaxes(cot.astype(F32), 0, 1)
    cot_lanes = jnp.concatenate([cot[y] for y in range(24)], axis=1).astype(BF16)
    back = dot_tn(head, cot_lanes)
    back = jnp.stack([back[:, y * 128 : y * 128 + 128] for y in range(24)], axis=0)
    s = sigmoid(pre)
    return (back * slope(pre, s)).astype(BF16), cot_lanes, pre * s


def face_body(dec_far, cot_far, head_far, first_far, second_far, dec_ref, cot_ref, head_ref, delta_ref, sems, out_sems):
    odd = parity("gx")
    planes = (3 - 3 * odd, 3 * odd)
    pairs = [(head_far, head_ref)]
    for i, x in enumerate(planes):
        pairs += [(cot_far.at[:, x], cot_ref.at[i]), (dec_far.at[:, x], dec_ref.at[i])]
    waits = fetch(pairs, sems)
    waits[0]()
    writes = []
    for i, far in enumerate((first_far, second_far)):
        waits[2 * i + 1]()
        waits[2 * i + 2]()
        delta_ref[i] = delta_plane(dec_ref[i], cot_ref[i], head_ref[...])[0]
        writes += fetch([(delta_ref.at[i], far)], out_sems.at[i])
    for wait in writes:
        wait()


def forward_body(
    dec_ref, cot_ref, head_ref, enc_ref, state_ref, mid_ref, pool_ref,
    delta_ref, head_grad_ref, hid_ref, slope_ref, pooled_ref, hmid_ref, mslope_ref, st_ref, ylo_ref, yhi_ref,
):
    total = jnp.zeros((8, 32), F32)
    for x in range(4):
        delta, cot_lanes, decoded = delta_plane(dec_ref[:, x], cot_ref[:, x], head_ref[...])
        if x in (1, 2):
            delta_ref[x - 1] = delta
        decoded = jnp.concatenate([decoded[y] for y in range(24)], axis=1).astype(BF16)
        total = total + dot_nt(cot_lanes, decoded)
    head_grad_ref[...] = total
    low_rows, high_rows = [], []
    for x in range(4):
        pre = jnp.swapaxes(enc_ref[:, x].astype(F32), 0, 1)
        s = sigmoid(pre)
        hid_ref[x] = (pre * s).astype(BF16)
        slope_ref[x] = slope(pre, s)
        state = jnp.swapaxes(state_ref[:, x].astype(F32), 0, 1)
        st_ref[x] = state
        low_rows.append(state[0])
        high_rows.append(state[23])
    ylo_ref[64:96, :] = jnp.concatenate(low_rows, axis=0).astype(BF16)
    yhi_ref[64:96, :] = jnp.concatenate(high_rows, axis=0).astype(BF16)
    tilts = {}
    for bx in range(2):
        for m in range(6):
            acc = None
            for ex in range(2):
                for ey in range(2):
                    pair = jnp.concatenate(
                        [hid_ref[2 * bx + ex, 4 * m + ey], hid_ref[2 * bx + ex, 4 * m + 2 + ey]], axis=1
                    )
                    part = dot(pair, pool_ref[:, 128:256])
                    acc = part if acc is None else acc + part
            pooled = (acc * 0.125).astype(BF16)
            pooled_ref[bx, m] = pooled
            pre = mid_ref[bx, m].astype(F32)
            s = sigmoid(pre)
            hmid_ref[bx, m] = (pre * s).astype(BF16)
            tilts[bx, m] = slope(pre, s)
            mslope_ref[bx, m] = tilts[bx, m]
    lower = lane_ids((64, 128)) < 64
    ylo_ref[0:64, :] = jnp.where(lower, tilts[0, 0], pltpu.roll(tilts[1, 0], 64, 1)).astype(BF16)
    yhi_ref[0:64, :] = jnp.where(lower, pltpu.roll(tilts[0, 5], 64, 1), tilts[1, 5]).astype(BF16)


def window_sums(rows_of, pool, put):
    got = dot(
        jnp.concatenate([jnp.concatenate([rows_of(x, j) for j in range(4)], axis=0) for x in range(6)], axis=0), pool
    )
    sums = []
    for x in range(6):
        at = [got[x * 128 + j * 32 : x * 128 + j * 32 + 32] for j in range(4)]
        sums.append([at[j] + at[j + 1] for j in (2, 1, 0)])
    for bx in range(2):
        for a, kx in enumerate((-1, 0, 1)):
            for b in range(3):
                both = (sums[2 * bx - kx + 1][b] + sums[2 * bx - kx + 2][b]).astype(BF16)
                for c in range(3):
                    put(bx, ((a * 3 + b) * 3 + c) * 32, both[:, c * 128 : c * 128 + 128])


def stack_of(row):
    return jnp.concatenate(
        [jnp.concatenate([row(x + 1 - kx) for x in range(4)], axis=1) for kx in (-1, 0, 1)], axis=0
    )


def skip_weights(w_ref):
    parts = [
        jnp.concatenate([w_ref[a, b].astype(F32).reshape(96, 96)[:, 64:96] for b in range(3)], axis=1)
        for a in range(3)
    ]
    return jnp.concatenate(parts, axis=0).T.astype(BF16)


def inner_body(got1_ref, face1_ref, delta_ref, face2_ref, got2_ref, pool_ref, w_ref, wmid_ref, acc_ref, wide_ref, win_ref, up_ref, wskip_ref, wm_ref, wup_ref):
    def put(x, v):
        parts = shifts(v.astype(F32).reshape(768, 128), 128)
        for a in range(3):
            wide_ref[x, :, a * 32 : a * 32 + 32, :] = parts[a].astype(BF16).reshape(24, 32, 128)

    odd = parity("gx")
    put(5 - 5 * odd, got1_ref[...])
    put(4 - 3 * odd, face1_ref[...])
    put(2, delta_ref[0])
    put(3, delta_ref[1])
    put(1 + 3 * odd, face2_ref[...])
    put(5 * odd, got2_ref[...])
    wskip_ref[...] = skip_weights(w_ref)
    acc_ref[...] = jnp.zeros(acc_ref.shape, F32)

    def step(i, carry):
        y = 4 * i
        out = dot(
            wskip_ref[...],
            jnp.concatenate([stack_of(lambda x, j=j: wide_ref[x, y + j]) for j in range(4)], axis=1),
        )
        for x in range(4):
            for r in range(6):
                parts = [
                    out[b * 32 : b * 32 + 32, ((r - b) * 4 + x) * 128 : ((r - b) * 4 + x) * 128 + 128]
                    for b in range(3)
                    if 0 <= r - b < 4
                ]
                acc_ref[x, y + r] += sum(parts[1:], parts[0])
        return carry

    lax.fori_loop(0, 6, step, 0)
    for m in range(1, 5):

        def rows_of(x, j):
            return jnp.concatenate(
                [wide_ref[x, 4 * m + j - 1, 32:64, :], wide_ref[x, 4 * m + j + 1, 32:64, :]], axis=1
            )

        def put_window(bx, row, v):
            lane = (bx * 4 + m - 1) * 128
            win_ref[row : row + 32, lane : lane + 128] = v

        window_sums(rows_of, pool_ref[...], put_window)
    wup_ref[...] = w_ref[...].reshape(864, 96).astype(F32).T[:64].astype(BF16)
    up_ref[...] = dot(wup_ref[...], win_ref[...])
    for a in range(3):
        for b in range(3):
            at = (a * 3 + b) * 32
            parts = [wmid_ref[a, b, c].astype(F32) for c in range(3)]
            wm_ref[at : at + 32, :] = jnp.concatenate(parts, axis=1).astype(BF16)


def outer_body(
    got1_ref, got2_ref, wide_ref, up_ref, mslope_ref, st_ref, pooled_ref, pool_ref, wup_ref, wskip_ref, wm_ref,
    edge_ref, rim_ref, win_ref, mid_ref, back_ref, face1_ref, face2_ref,
    total_ref, got_ref,
):
    wskip = wskip_ref[...]
    odd_x, odd_y = parity("gx"), parity("gy")
    got_ref[1 - odd_y] = got1_ref[...]
    got_ref[odd_y] = got2_ref[...]

    def row(x, y):
        if 0 <= y <= 23:
            return wide_ref[x, y, 32:64, :]
        slot = x + (1 - odd_x) * (5, 3, 0, 0, -3, -5)[x]
        at = (slot * 3 + (y + 3 if y < 0 else y - 24)) * 32
        return got_ref[0 if y < 0 else 1, pl.ds(pl.multiple_of(at, 32), 32), :]

    for x in range(6):
        v = jnp.concatenate([row(x, -1), row(x, 24)], axis=0).astype(F32)
        parts = shifts(v, 128)
        for a in range(3):
            rim_ref[x, :, a * 32 : a * 32 + 32, :] = parts[a].astype(BF16).reshape(2, 32, 128)
    outs = [dot(wskip, stack_of(lambda x, r=r: rim_ref[x, r])) for r in range(2)]
    for x in range(4):
        at = slice(x * 128, x * 128 + 128)
        edge_ref[x, 0] = outs[0][64:96, at]
        edge_ref[x, 1] = outs[1][0:32, at]

    for i, (left, right) in enumerate(((-1, 1), (19, 21), (23, -3))):

        def rows_of(x, j):
            return jnp.concatenate([row(x, left + j), row(x, right + j)], axis=1)

        def put_window(bx, r, v):
            lane = (bx * 3 + i) * 128
            win_ref[r : r + 32, lane : lane + 128] = v

        window_sums(rows_of, pool_ref[...], put_window)
    rim_up = dot(wup_ref[...], win_ref[...])

    upper = lane_ids((64, 128)) >= 64
    before = got_ref[0, 576:640, :].astype(F32)
    after = got_ref[1, 576:640, :].astype(F32)
    rim_tilt = (
        jnp.where(upper, pltpu.roll(before, 64, 1), after),
        jnp.where(upper, before, pltpu.roll(after, 64, 1)),
    )
    for bx in range(2):
        for m in range(7):
            if 1 <= m <= 4:
                lane = (bx * 4 + m - 1) * 128
                v = up_ref[:, lane : lane + 128]
            else:
                lane = (bx * 3 + (0, 5, 6).index(m)) * 128
                v = rim_up[:, lane : lane + 128]
            tilt = rim_tilt[bx] if m == 6 else mslope_ref[bx, m]
            delta = (v * tilt).astype(BF16).astype(F32)
            lane = (bx * 7 + m) * 128
            for a, part in enumerate(shifts(delta, 64)):
                mid_ref[a * 64 : a * 64 + 64, lane : lane + 128] = part.astype(BF16)

    out = dot(wm_ref[...], mid_ref[...])
    upper = lane_ids((32, 128)) >= 64

    def term(a, b, x, m):
        if not 0 <= x - a < 2:
            return None
        col = ((x - a) * 7 + m) * 128
        return out[(a * 3 + b) * 32 : (a * 3 + b) * 32 + 32, col : col + 128]

    def tap_sum(b, x, m):
        parts = [v for v in (term(a, b, x, m) for a in range(3)) if v is not None]
        return sum(parts[1:], parts[0])

    for x in range(4):
        downs = [pltpu.roll(tap_sum(0, x, m), 64, 1) for m in range(7)]
        ups = [pltpu.roll(tap_sum(2, x, m), 64, 1) for m in range(7)]
        for m in range(6):
            low = ups[(m + 6) % 7] + downs[m]
            high = ups[m] + downs[m + 1]
            total_ref[x, m] = tap_sum(1, x, m) + jnp.where(upper, high, low)
    back_ref[...] = total_ref[1:3, 0:6]
    before = got_ref[0, 640:672, :].astype(F32)
    after = got_ref[1, 640:672, :].astype(F32)
    for face_ref, last in ((face1_ref, 1 - odd_x), (face2_ref, odd_x)):
        face_ref[0:192, :] = total_ref[3 * last].astype(BF16).reshape(192, 128)
        face_ref[192:384, :] = pooled_ref[last].reshape(192, 128)
        rows = (
            jnp.where(last == 1, before[24:32], before[0:8]),
            st_ref[3 * last].reshape(192, 128),
            jnp.where(last == 1, after[24:32], after[0:8]),
        )
        face_ref[384:592, :] = jnp.concatenate(rows, axis=0).astype(BF16)


def hidden_rows(hid_ref, ys):
    def tap(x, y):
        return hid_ref[x, y + 2]

    return jnp.concatenate(
        [jnp.concatenate([tap(x, y + b - 1) for y in ys for x in range(4)], axis=1) for b in range(3)], axis=0
    )


def pooled_taps(blocks):
    blocks = blocks + [jnp.zeros((32, 128), F32)]
    lower = lane_ids((32, 128)) < 64
    turned = [pltpu.roll(v, 64, 1) for v in blocks]
    taps = (
        [jnp.where(lower, turned[(m + 6) % 7], turned[m]) for m in range(7)],
        blocks,
        [jnp.where(lower, turned[m], turned[(m + 1) % 7]) for m in range(7)],
    )
    return jnp.concatenate([jnp.concatenate(v, axis=1) for v in taps], axis=0).astype(BF16)


def dec_grad_body(
    wide_ref, rim_ref, hid_ref, win_ref, rim_win_ref, hmid_ref, head_ref, pooled_ref, mid_ref,
    rows_ref, gmid_ref, hpad_ref, skip_ref,
):
    blank = jnp.zeros((2, 32, 128), BF16)
    for x in range(4):
        hpad_ref[x, 0:2] = blank
        hpad_ref[x, 26:28] = blank
        hpad_ref[x, 2:26] = hid_ref[x]
    rims = jnp.concatenate([stack_of(lambda x, r=r: rim_ref[x, r]) for r in (0, 1)], axis=1)
    skip_ref[...] = dot_nt(rims, hidden_rows(hpad_ref, (-1, 24)))

    def step(i, carry):
        y = 4 * i
        rows = jnp.concatenate([stack_of(lambda x, j=j: wide_ref[x, y + j]) for j in range(4)], axis=1)
        skip_ref[...] += dot_nt(rows, hidden_rows(hpad_ref, [y + j for j in range(4)]))
        return carry

    lax.fori_loop(0, 6, step, 0)
    rows_ref[0:288, :] = jnp.concatenate([skip_ref[...], jnp.zeros((288, 32), F32)], axis=1).astype(BF16)

    def side(bx, m):
        if 1 <= m <= 4:
            at = (bx * 4 + m - 1) * 128
            return win_ref[:, at : at + 128]
        at = (bx * 3 + (0 if m == 0 else 1)) * 128
        return rim_win_ref[:, at : at + 128]

    order = [(bx, m) for bx in range(2) for m in range(6)]
    windows = jnp.concatenate([side(bx, m) for bx, m in order], axis=1)
    hmid = jnp.concatenate([hmid_ref[bx, m] for bx, m in order], axis=1)
    lift = dot_nt(windows, hmid)
    rows_ref[288:720, :] = jnp.concatenate([lift[0:432], lift[432:864]], axis=1).astype(BF16)
    rows_ref[720:736, :] = jnp.concatenate(
        [jnp.concatenate([head_ref[...], jnp.zeros((8, 96), F32)], axis=1), jnp.zeros((8, 128), F32)], axis=0
    ).astype(BF16)
    taps = [pooled_taps([pooled_ref[bx, m].astype(F32) for m in range(6)]) for bx in range(2)]
    first, second = mid_ref[:, 0:896], mid_ref[:, 896:1792]
    gmid_ref[0:96, :] = dot_nt(taps[0], second)
    gmid_ref[96:192, :] = dot_nt(taps[0], first) + dot_nt(taps[1], second)
    gmid_ref[192:288, :] = dot_nt(taps[1], first)


def encoder_body(
    acc_ref, edge_ref, back_ref, rim1_ref, rim2_ref, got1_ref, got2_ref, slope_ref, w_ref, up_ref,
    mid_ref, gmid_ref, st_ref, dec_ref,
    rows_far, own_ref, face1_ref, face2_ref, edge_lo_ref, edge_hi_ref,
    enc_ref, wide_ref, total_ref, we_ref, rows_ref, sext_ref, sum_ref, got_ref, sems,
):
    odd_x = parity("gx")
    got_ref[1 - odd_x] = got1_ref[...]
    got_ref[odd_x] = got2_ref[...]
    got_lo_ref, got_hi_ref = got_ref.at[0], got_ref.at[1]
    writes = fetch([(dec_ref, rows_far.at[0:736])], sems.at[0])

    def beyond(ref):
        side = ref[192:384, :].astype(F32)
        return pooled_taps([side[m * 32 : m * 32 + 32] for m in range(6)])

    gmid = jnp.concatenate(
        [
            gmid_ref[0:96, :] + dot_nt(beyond(got_lo_ref), mid_ref[:, 0:896]),
            gmid_ref[96:192, :],
            gmid_ref[192:288, :] + dot_nt(beyond(got_hi_ref), mid_ref[:, 896:1792]),
        ],
        axis=0,
    )
    rows_ref[0:288, :] = gmid[:, :128].astype(BF16)
    rows_ref[288:432, :] = jnp.concatenate([gmid[:144, 128:], gmid[144:, 128:]], axis=1).astype(BF16)
    writes += fetch([(rows_ref.at[0:432], rows_far.at[736:1168])], sems.at[1])

    sext_ref[1:5, 1:25] = st_ref[...]
    sext_ref[0] = got_lo_ref[384:592, :].astype(F32).reshape(26, 8, 128)
    sext_ref[5] = got_hi_ref[384:592, :].astype(F32).reshape(26, 8, 128)
    before, after = in_order("gy", rim1_ref[640:672, :].astype(F32), rim2_ref[640:672, :].astype(F32))
    for x in range(4):
        sext_ref[x + 1, 0] = before[x * 8 : x * 8 + 8]
        sext_ref[x + 1, 25] = after[x * 8 : x * 8 + 8]

    whole = [back_ref[bx].reshape(192, 128) for bx in range(2)]
    whole = [v + ref[0:192, :].astype(F32) for v, ref in zip(whole, (got_lo_ref, got_hi_ref))]
    whole = jnp.concatenate(whole, axis=0) * 0.125
    high = whole.astype(BF16)
    low = (whole - high.astype(F32)).astype(BF16)
    wide_ref[...] = dot(jnp.concatenate([high, low], axis=1), up_ref[...])
    for bx in range(2):
        for m in range(6):
            at = (bx * 6 + m) * 32
            for half in range(2):
                fine = wide_ref[at : at + 32, half * 128 : half * 128 + 128]
                for ey in range(2):
                    y = 4 * m + 2 * half + ey
                    for ex in range(2):
                        x = 2 * bx + ex
                        sum_in = acc_ref[x, y + 1] + fine
                        if y in (0, 23):
                            sum_in = sum_in + edge_ref[x, (0, 23).index(y)]
                        delta = (sum_in * slope_ref[x, y]).astype(BF16).astype(F32)
                        lane = (y * 4 + x) * 128
                        for c, part in enumerate(shifts(delta, 128)):
                            enc_ref[c * 32 : c * 32 + 32, lane : lane + 128] = part.astype(BF16)

    for a in range(3):
        for b in range(3):
            at = (a * 3 + b) * 8
            we_ref[at : at + 8, :] = jnp.concatenate([w_ref[a, b, c].astype(F32) for c in range(3)], axis=1)
    w = we_ref[...].astype(BF16)
    total_ref[...] = jnp.zeros(total_ref.shape, F32)
    sum_ref[...] = jnp.zeros(sum_ref.shape, F32)

    def step(i, carry):
        y = 4 * i
        delta = enc_ref[:, pl.ds(pl.multiple_of(y * 512, 2048), 2048)]
        state = jnp.concatenate(
            [
                jnp.concatenate([sext_ref[x + a, y + j + b] for j in range(4) for x in range(4)], axis=1)
                for a in range(3)
                for b in range(3)
            ],
            axis=0,
        ).astype(BF16)
        sum_ref[...] += dot_nt(state, delta)
        out = dot(w, delta)
        for x in range(6):
            for r in range(6):
                parts = []
                for a in range(3):
                    for b in range(3):
                        j, own = r - b, x - a
                        if 0 <= j < 4 and 0 <= own < 4:
                            row, lane = (a * 3 + b) * 8, (j * 4 + own) * 128
                            parts.append(out[row : row + 8, lane : lane + 128])
                total_ref[x, y + r] += sum(parts[1:], parts[0])
        return carry

    lax.fori_loop(0, 6, step, 0, unroll=3)
    genc = jnp.concatenate([sum_ref[...], jnp.zeros((72, 32), F32)], axis=1)
    rows_ref[432:544, :] = jnp.concatenate([genc, jnp.zeros((40, 128), F32)], axis=0).astype(BF16)
    writes += fetch([(rows_ref.at[432:544], rows_far.at[1168:1280])], sems.at[2])
    own_ref[...] = total_ref[1:5, 1:25]
    face1_ref[...] = total_ref[5 - 5 * odd_x].reshape(208, 128).astype(BF16)
    face2_ref[...] = total_ref[5 * odd_x].reshape(208, 128).astype(BF16)
    edge_lo_ref[...] = total_ref[1:5, 0]
    edge_hi_ref[...] = total_ref[1:5, 25]
    for wait in writes:
        wait()


def corner_body(edge_lo_ref, edge_hi_ref, got1_ref, got2_ref, col1_ref, col2_ref):
    before, after = in_order("gx", got1_ref[...].astype(F32), got2_ref[...].astype(F32))
    cols = []
    for edge_ref, at in ((edge_lo_ref, 0), (edge_hi_ref, 200)):
        rows = [edge_ref[0] + before[at : at + 8], edge_ref[1], edge_ref[2], edge_ref[3] + after[at : at + 8]]
        cols.append(jnp.concatenate(rows, axis=0))
    first, second = in_order("gy", *cols)
    col1_ref[...] = first.astype(BF16)
    col2_ref[...] = second.astype(BF16)


def final_body(cot_ref, own_ref, got1_ref, got2_ref, end1_ref, end2_ref, grad_ref):
    sides = in_order("gx", got1_ref[...].astype(F32), got2_ref[...].astype(F32))
    before, after = in_order("gy", end1_ref[...].astype(F32), end2_ref[...].astype(F32))
    for x in range(4):
        total = own_ref[x]
        if x in (0, 3):
            total = total + sides[x // 3][8:200].reshape(24, 8, 128)
        at = slice(x * 8, x * 8 + 8)
        ends = [before[at][None], jnp.zeros((22, 8, 128), F32), after[at][None]]
        total = total + jnp.concatenate(ends, axis=0)
        grad_ref[:, x] = (cot_ref[:, x].astype(F32) + jnp.swapaxes(total, 0, 1)).astype(BF16)


def share_body(pieces_far, out_far, pieces_ref, copies_ref, sems, out_sems):
    count = pieces_ref.shape[0]
    part = count // 4
    spans = [pl.ds(i * part, part) for i in range(4)]
    waits = fetch([(pieces_far.at[span], pieces_ref.at[span]) for span in spans], sems)
    total = jnp.zeros(pieces_ref.shape[1:], F32)
    for i, wait in enumerate(waits):
        wait()
        for j in range(part):
            total = total + pieces_ref[i * part + j].astype(F32)
    total = total.astype(BF16)
    part = copies_ref.shape[0]
    for j in range(part):
        copies_ref[j] = total
    for wait in fetch([(copies_ref, out_far.at[pl.ds(i * part, part)]) for i in range(count // part)], out_sems):
        wait()


def unpack_body(scale, rows_ref, enc_ref, mid_ref, dec_ref, head_ref):
    def rows(at, count):
        return rows_ref[at : at + count, :].astype(F32) * scale

    skip = [rows(i * 32, 32) for i in range(9)]
    head_ref[...] = rows(720, 16)[:8, :32]
    mid_rest = [rows(1024 + i * 48, 48) for i in range(3)]
    mid_rest = jnp.concatenate(mid_rest, axis=0)
    mid_rest = jnp.concatenate([mid_rest[:, :64], mid_rest[:, 64:]], axis=0)
    enc = rows(1168, 80)
    lift = rows(288, 432)
    lift = jnp.concatenate([lift[:, :64], lift[:, 64:]], axis=0)
    for a in range(3):
        for b in range(3):
            tap = a * 3 + b
            pair = rows(736 + tap * 32, 32)
            mid_ref[a, b, 0] = pair[:, :64]
            mid_ref[a, b, 1] = pair[:, 64:]
            mid_ref[a, b, 2] = mid_rest[tap * 32 : tap * 32 + 32]
            for c in range(3):
                enc_ref[a, b, c] = enc[tap * 8 : tap * 8 + 8, c * 32 : c * 32 + 32]
                at = (tap * 3 + c) * 32
                dec_ref[a, b, c] = jnp.concatenate(
                    [lift[at : at + 32], skip[a * 3 + c][:, b * 32 : b * 32 + 32]], axis=1
                )


def pool_matrix():
    table = np.zeros((256, 3, 128), np.float32)
    for c, k in enumerate((-1, 0, 1)):
        for half in range(2):
            for q in range(64):
                for e in range(2):
                    z = 2 * q + e - k
                    if 0 <= z < 128:
                        table[half * 128 + z, c, half * 64 + q] = 1.0
    return jnp.asarray(table.reshape(256, 384), BF16)


def up_matrix():
    table = np.zeros((2, 128, 256), np.float32)
    for half in range(2):
        for z in range(128):
            table[:, half * 64 + z // 2, half * 128 + z] = 1.0
    return jnp.asarray(table.reshape(256, 256), BF16)


def swaps(first, second, axis):
    count = lax.axis_size(axis)
    pairs = [(i, i + 1) for i in range(0, count - 1, 2)], [(i, i + 1) for i in range(1, count - 1, 2)]
    return tuple(
        lax.ppermute(v, axis, ahead + [(b, a) for a, b in ahead]) for v, ahead in zip((first, second), pairs)
    )


def on_device(
    state_now, enc_pre, mid_pre, dec_pre, cotangent, enc_kernel, mid_kernel, dec_kernel, out_kernel
):
    state_now, enc_pre, mid_pre, dec_pre, cotangent = (
        v[0] for v in (state_now, enc_pre, mid_pre, dec_pre, cotangent)
    )
    cells = state_now[0].size * lax.axis_size("gx") * lax.axis_size("gy") * lax.axis_size("dp")
    grad_scale = 1.0 / math.sqrt(cells)
    pool = pool_matrix()
    dec_w = dec_kernel.transpose(2, 3, 4, 0, 1)
    mid_w = mid_kernel.transpose(2, 3, 4, 1, 0)
    enc_w = enc_kernel.transpose(2, 3, 4, 1, 0)

    plane = sds((24, 32, 128), BF16)
    face1, face2 = call(
        face_body,
        [plane, plane],
        [
            pltpu.VMEM((2, 32, 24, 128), BF16),
            pltpu.VMEM((2, 8, 24, 128), BF16),
            pltpu.VMEM((8, 32), BF16),
            pltpu.VMEM((2, 24, 32, 128), BF16),
            pltpu.SemaphoreType.DMA((5,)),
            pltpu.SemaphoreType.DMA((2, 1)),
        ],
        (dec_pre, cotangent, out_kernel),
        200 << 20, 56, far=3, far_outs=2,
    )
    got1, got2 = swaps(face1, face2, "gx")
    mid_blocks = mid_pre.reshape(64, 2, 6, 2, 64).transpose(1, 2, 0, 3, 4).reshape(2, 6, 64, 128)
    (
        delta, head_grad, hidden, enc_slope, pooled, hidden_mid, mid_slope, state,
        tail_lo, tail_hi,
    ) = call(
        forward_body,
        [
            sds((2, 24, 32, 128), BF16),
            sds((8, 32), F32),
            sds((4, 24, 32, 128), BF16),
            sds((4, 24, 32, 128), F32),
            sds((2, 6, 32, 128), BF16),
            sds((2, 6, 64, 128), BF16),
            sds((2, 6, 64, 128), F32),
            sds((4, 24, 8, 128), F32),
            sds((96, 128), BF16),
            sds((96, 128), BF16),
        ],
        [],
        (dec_pre, cotangent, out_kernel, enc_pre, state_now, mid_blocks, pool),
        600 << 20, 16,
    )


    def column(at, tail):
        rows = (got1[at], face1[at], delta[0, at], delta[1, at], face2[at], got2[at], tail)
        return jnp.concatenate([v.reshape(-1, 128) for v in rows])

    ends = column(slice(0, 3), tail_lo), column(slice(21, 24), tail_hi)
    rim1, rim2 = swaps(*in_order("gy", *ends), "gy")
    acc, wide, win, up, wskip, wmid, wup = call(
        inner_body,
        [
            sds((4, 26, 32, 128), F32),
            sds((6, 24, 96, 128), BF16),
            sds((864, 1024), BF16),
            sds((64, 1024), F32),
            sds((96, 288), BF16),
            sds((288, 192), BF16),
            sds((64, 864), BF16),
        ],
        [],
        (got1, face1, delta, face2, got2, pool, dec_w, mid_w),
        3 << 30, 24,
    )
    edge, rim_wide, rim_win, mid_wide, back, face1, face2 = call(
        outer_body,
        [
            sds((4, 2, 32, 128), F32),
            sds((6, 2, 96, 128), BF16),
            sds((864, 768), BF16),
            sds((192, 1792), BF16),
            sds((2, 6, 32, 128), F32),
            sds((592, 128), BF16),
            sds((592, 128), BF16),
        ],
        [pltpu.VMEM((4, 6, 32, 128), F32), pltpu.VMEM((2, 672, 128), BF16)],
        (rim1, rim2, wide, up, mid_slope, state, pooled, pool, wup, wskip, wmid),
        1 << 30, 24,
    )
    got1, got2 = swaps(face1, face2, "gx")
    dec_rows, mid_grad = call(
        dec_grad_body,
        [sds((736, 128), BF16), sds((288, 192), F32)],
        [pltpu.VMEM((4, 28, 32, 128), BF16), pltpu.VMEM((288, 96), F32)],
        (wide, rim_wide, hidden, win, rim_win, hidden_mid, head_grad, pooled, mid_wide),
        3 << 30, 20,
    )
    dec_rows, mid_grad, got1, got2 = lax.optimization_barrier((dec_rows, mid_grad, got1, got2))
    rows, own, face1, face2, edge_lo, edge_hi = call(
        encoder_body,
        [
            sds((1280, 128), BF16),
            sds((4, 24, 8, 128), F32),
            sds((208, 128), BF16),
            sds((208, 128), BF16),
            sds((4, 8, 128), F32),
            sds((4, 8, 128), F32),
        ],
        [
            pltpu.VMEM((96, 24 * 512), BF16),
            pltpu.VMEM((384, 256), F32),
            pltpu.VMEM((6, 26, 8, 128), F32),
            pltpu.VMEM((72, 96), F32),
            pltpu.VMEM((544, 128), BF16),
            pltpu.VMEM((6, 26, 8, 128), F32),
            pltpu.VMEM((72, 96), F32),
            pltpu.VMEM((2, 592, 128), BF16),
            pltpu.SemaphoreType.DMA((3, 1)),
        ],
        (
            acc, edge, back, rim1, rim2, got1, got2, enc_slope, enc_w, up_matrix(),
            mid_wide, mid_grad, state, dec_rows,
        ),
        2 << 30, 24, far_outs=1,
    )
    last1, last2 = swaps(face1, face2, "gx")

    axes = ("dp", "gx", "gy")
    count = lax.axis_size(axes)
    share = 1280 // count // 2
    pieces = lax.all_to_all(rows.reshape(count, share, 2, 128), axes, 0, 0)
    (shares,) = call(
        share_body,
        [sds(pieces.shape, BF16)],
        [
            pltpu.VMEM(pieces.shape, BF16),
            pltpu.VMEM((count // 8,) + pieces.shape[1:], BF16),
            pltpu.SemaphoreType.DMA((4,)),
            pltpu.SemaphoreType.DMA((8,)),
        ],
        (pieces,),
        1 << 20, 8, far=1, far_outs=1,
    )
    shares, last1, last2 = lax.optimization_barrier((shares, last1, last2))
    rows = lax.all_to_all(shares, axes, 0, 0).reshape(1280, 128)
    col1, col2 = call(
        corner_body, [sds((32, 128), BF16)] * 2, [], (edge_lo, edge_hi, last1, last2), 1 << 16, 4
    )
    end1, end2 = swaps(col1, col2, "gy")
    genc, gmid, gdec, ghead = call(
        functools.partial(unpack_body, grad_scale),
        [sds((3, 3, 3, 8, 32), F32), sds((3, 3, 3, 32, 64), F32), sds((3, 3, 3, 32, 96), F32), sds((8, 32), F32)],
        [],
        (rows,),
        1 << 20, 12,
    )
    genc, end1, end2 = lax.optimization_barrier((genc, end1, end2))
    (state_grad,) = call(
        final_body,
        [sds((8, 4, 24, 128), BF16)],
        [],
        (cotangent, own, last1, last2, end1, end2),
        1 << 20, 8,
    )
    return (
        state_grad[None],
        genc.transpose(4, 3, 0, 1, 2),
        gmid.transpose(4, 3, 0, 1, 2),
        gdec.transpose(3, 4, 0, 1, 2),
        ghead,
    )


def solution(mesh):
    grid = P("dp", None, "gx", "gy", None)
    return jax.shard_map(
        on_device,
        mesh=mesh,
        in_specs=(grid,) * 5 + (P(),) * 4,
        out_specs=(grid, P(), P(), P(), P()),
        check_vma=False,
    )
```

```python
import functools
import math

import jax
import jax.numpy as jnp
import numpy as np
from jax import lax
from jax.experimental import pallas as pl
from jax.experimental.pallas import tpu as pltpu
from jax.sharding import PartitionSpec as P

F32 = jnp.float32
BF16 = jnp.bfloat16


VMEM = pl.BlockSpec(memory_space=pltpu.VMEM)
HBM = pl.BlockSpec(memory_space=pltpu.HBM)


def call(body, outs, scratch, args, flops, limit, far=0, far_outs=0):
    return pl.pallas_call(
        body,
        out_shape=outs,
        in_specs=[HBM] * far + [VMEM] * (len(args) - far),
        out_specs=[HBM] * far_outs + [VMEM] * (len(outs) - far_outs),
        scratch_shapes=scratch,
        compiler_params=pltpu.CompilerParams(vmem_limit_bytes=limit << 20),
        cost_estimate=pl.CostEstimate(flops=flops, bytes_accessed=4 << 20, transcendentals=0),
    )(*args)


def fetch(pairs, sems):
    copies = [pltpu.make_async_copy(src, dst, sems.at[i]) for i, (src, dst) in enumerate(pairs)]
    for copy in copies:
        copy.start()
    return [copy.wait for copy in copies]


def sds(shape, dtype):
    return jax.ShapeDtypeStruct(shape, dtype)


def dot(a, b):
    return lax.dot_general(a, b, (((1,), (0,)), ((), ())), preferred_element_type=F32)


def dot_tn(a, b):
    return lax.dot_general(a, b, (((0,), (0,)), ((), ())), preferred_element_type=F32)


def dot_nt(a, b):
    return lax.dot_general(a, b, (((1,), (1,)), ((), ())), preferred_element_type=F32)


def sigmoid(v):
    return 0.5 + 0.5 * jnp.tanh(0.5 * v)


def slope(v, s):
    return s * (1.0 + v * (1.0 - s))


def parity(axis):
    return jnp.bitwise_and(lax.axis_index(axis), 1)


def in_order(axis, first, second):
    odd = parity(axis) == 1
    return jnp.where(odd, first, second), jnp.where(odd, second, first)


def lane_ids(shape):
    return lax.broadcasted_iota(jnp.int32, shape, len(shape) - 1)


def shifts(v, period):
    lane = jnp.bitwise_and(lane_ids(v.shape), period - 1)
    axis = v.ndim - 1
    size = v.shape[-1]
    back = jnp.where(lane == period - 1, 0.0, pltpu.roll(v, size - 1, axis))
    ahead = jnp.where(lane == 0, 0.0, pltpu.roll(v, 1, axis))
    return back, v, ahead


def delta_plane(dec, cot, head):
    pre = jnp.swapaxes(dec.astype(F32), 0, 1)
    cot = jnp.swapaxes(cot.astype(F32), 0, 1)
    cot_lanes = jnp.concatenate([cot[y] for y in range(24)], axis=1).astype(BF16)
    back = dot_tn(head, cot_lanes)
    back = jnp.stack([back[:, y * 128 : y * 128 + 128] for y in range(24)], axis=0)
    s = sigmoid(pre)
    return (back * slope(pre, s)).astype(BF16), cot_lanes, pre * s


def face_body(dec_far, cot_far, head_far, first_far, second_far, dec_ref, cot_ref, head_ref, delta_ref, sems, out_sems):
    odd = parity("gx")
    planes = (3 - 3 * odd, 3 * odd)
    pairs = [(head_far, head_ref)]
    for i, x in enumerate(planes):
        pairs += [(cot_far.at[:, x], cot_ref.at[i]), (dec_far.at[:, x], dec_ref.at[i])]
    waits = fetch(pairs, sems)
    waits[0]()
    writes = []
    for i, far in enumerate((first_far, second_far)):
        waits[2 * i + 1]()
        waits[2 * i + 2]()
        delta_ref[i] = delta_plane(dec_ref[i], cot_ref[i], head_ref[...])[0]
        writes += fetch([(delta_ref.at[i], far)], out_sems.at[i])
    for wait in writes:
        wait()


def forward_body(
    dec_ref, cot_ref, head_ref, enc_ref, state_ref, mid_ref, pool_ref,
    delta_ref, head_grad_ref, hid_ref, slope_ref, pooled_ref, hmid_ref, mslope_ref, st_ref, ylo_ref, yhi_ref,
):
    total = jnp.zeros((8, 32), F32)
    for x in range(4):
        delta, cot_lanes, decoded = delta_plane(dec_ref[:, x], cot_ref[:, x], head_ref[...])
        if x in (1, 2):
            delta_ref[x - 1] = delta
        decoded = jnp.concatenate([decoded[y] for y in range(24)], axis=1).astype(BF16)
        total = total + dot_nt(cot_lanes, decoded)
    head_grad_ref[...] = total
    low_rows, high_rows = [], []
    for x in range(4):
        pre = jnp.swapaxes(enc_ref[:, x].astype(F32), 0, 1)
        s = sigmoid(pre)
        hid_ref[x] = (pre * s).astype(BF16)
        slope_ref[x] = slope(pre, s)
        state = jnp.swapaxes(state_ref[:, x].astype(F32), 0, 1)
        st_ref[x] = state
        low_rows.append(state[0])
        high_rows.append(state[23])
    ylo_ref[64:96, :] = jnp.concatenate(low_rows, axis=0).astype(BF16)
    yhi_ref[64:96, :] = jnp.concatenate(high_rows, axis=0).astype(BF16)
    tilts = {}
    for bx in range(2):
        for m in range(6):
            acc = None
            for ex in range(2):
                for ey in range(2):
                    pair = jnp.concatenate(
                        [hid_ref[2 * bx + ex, 4 * m + ey], hid_ref[2 * bx + ex, 4 * m + 2 + ey]], axis=1
                    )
                    part = dot(pair, pool_ref[:, 128:256])
                    acc = part if acc is None else acc + part
            pooled = (acc * 0.125).astype(BF16)
            pooled_ref[bx, m] = pooled
            pre = mid_ref[bx, m].astype(F32)
            s = sigmoid(pre)
            hmid_ref[bx, m] = (pre * s).astype(BF16)
            tilts[bx, m] = slope(pre, s)
            mslope_ref[bx, m] = tilts[bx, m]
    lower = lane_ids((64, 128)) < 64
    ylo_ref[0:64, :] = jnp.where(lower, tilts[0, 0], pltpu.roll(tilts[1, 0], 64, 1)).astype(BF16)
    yhi_ref[0:64, :] = jnp.where(lower, pltpu.roll(tilts[0, 5], 64, 1), tilts[1, 5]).astype(BF16)


def window_sums(rows_of, pool, put):
    got = dot(
        jnp.concatenate([jnp.concatenate([rows_of(x, j) for j in range(4)], axis=0) for x in range(6)], axis=0), pool
    )
    sums = []
    for x in range(6):
        at = [got[x * 128 + j * 32 : x * 128 + j * 32 + 32] for j in range(4)]
        sums.append([at[j] + at[j + 1] for j in (2, 1, 0)])
    for bx in range(2):
        for a, kx in enumerate((-1, 0, 1)):
            for b in range(3):
                both = (sums[2 * bx - kx + 1][b] + sums[2 * bx - kx + 2][b]).astype(BF16)
                for c in range(3):
                    put(bx, ((a * 3 + b) * 3 + c) * 32, both[:, c * 128 : c * 128 + 128])


def stack_of(row):
    return jnp.concatenate(
        [jnp.concatenate([row(x + 1 - kx) for x in range(4)], axis=1) for kx in (-1, 0, 1)], axis=0
    )


def skip_weights(w_ref):
    parts = [
        jnp.concatenate([w_ref[a, b].astype(F32).reshape(96, 96)[:, 64:96] for b in range(3)], axis=1)
        for a in range(3)
    ]
    return jnp.concatenate(parts, axis=0).T.astype(BF16)


def inner_body(got1_ref, face1_ref, delta_ref, face2_ref, got2_ref, pool_ref, w_ref, wmid_ref, acc_ref, wide_ref, win_ref, up_ref, wskip_ref, wm_ref, wup_ref):
    def put(x, v):
        parts = shifts(v.astype(F32).reshape(768, 128), 128)
        for a in range(3):
            wide_ref[x, :, a * 32 : a * 32 + 32, :] = parts[a].astype(BF16).reshape(24, 32, 128)

    odd = parity("gx")
    put(5 - 5 * odd, got1_ref[...])
    put(4 - 3 * odd, face1_ref[...])
    put(2, delta_ref[0])
    put(3, delta_ref[1])
    put(1 + 3 * odd, face2_ref[...])
    put(5 * odd, got2_ref[...])
    wskip_ref[...] = skip_weights(w_ref)
    acc_ref[...] = jnp.zeros(acc_ref.shape, F32)

    def step(i, carry):
        y = 4 * i
        out = dot(
            wskip_ref[...],
            jnp.concatenate([stack_of(lambda x, j=j: wide_ref[x, y + j]) for j in range(4)], axis=1),
        )
        for x in range(4):
            for r in range(6):
                parts = [
                    out[b * 32 : b * 32 + 32, ((r - b) * 4 + x) * 128 : ((r - b) * 4 + x) * 128 + 128]
                    for b in range(3)
                    if 0 <= r - b < 4
                ]
                acc_ref[x, y + r] += sum(parts[1:], parts[0])
        return carry

    lax.fori_loop(0, 6, step, 0)
    for m in range(1, 5):

        def rows_of(x, j):
            return jnp.concatenate(
                [wide_ref[x, 4 * m + j - 1, 32:64, :], wide_ref[x, 4 * m + j + 1, 32:64, :]], axis=1
            )

        def put_window(bx, row, v):
            lane = (bx * 4 + m - 1) * 128
            win_ref[row : row + 32, lane : lane + 128] = v

        window_sums(rows_of, pool_ref[...], put_window)
    wup_ref[...] = w_ref[...].reshape(864, 96).astype(F32).T[:64].astype(BF16)
    up_ref[...] = dot(wup_ref[...], win_ref[...])
    for a in range(3):
        for b in range(3):
            at = (a * 3 + b) * 32
            parts = [wmid_ref[a, b, c].astype(F32) for c in range(3)]
            wm_ref[at : at + 32, :] = jnp.concatenate(parts, axis=1).astype(BF16)


def outer_body(
    got1_ref, got2_ref, wide_ref, up_ref, mslope_ref, st_ref, pooled_ref, pool_ref, wup_ref, wskip_ref, wm_ref,
    edge_ref, rim_ref, win_ref, mid_ref, back_ref, face1_ref, face2_ref,
    total_ref, got_ref,
):
    wskip = wskip_ref[...]
    odd_x, odd_y = parity("gx"), parity("gy")
    got_ref[1 - odd_y] = got1_ref[...]
    got_ref[odd_y] = got2_ref[...]

    def row(x, y):
        if 0 <= y <= 23:
            return wide_ref[x, y, 32:64, :]
        slot = x + (1 - odd_x) * (5, 3, 0, 0, -3, -5)[x]
        at = (slot * 3 + (y + 3 if y < 0 else y - 24)) * 32
        return got_ref[0 if y < 0 else 1, pl.ds(pl.multiple_of(at, 32), 32), :]

    for x in range(6):
        v = jnp.concatenate([row(x, -1), row(x, 24)], axis=0).astype(F32)
        parts = shifts(v, 128)
        for a in range(3):
            rim_ref[x, :, a * 32 : a * 32 + 32, :] = parts[a].astype(BF16).reshape(2, 32, 128)
    outs = [dot(wskip, stack_of(lambda x, r=r: rim_ref[x, r])) for r in range(2)]
    for x in range(4):
        at = slice(x * 128, x * 128 + 128)
        edge_ref[x, 0] = outs[0][64:96, at]
        edge_ref[x, 1] = outs[1][0:32, at]

    for i, (left, right) in enumerate(((-1, 1), (19, 21), (23, -3))):

        def rows_of(x, j):
            return jnp.concatenate([row(x, left + j), row(x, right + j)], axis=1)

        def put_window(bx, r, v):
            lane = (bx * 3 + i) * 128
            win_ref[r : r + 32, lane : lane + 128] = v

        window_sums(rows_of, pool_ref[...], put_window)
    rim_up = dot(wup_ref[...], win_ref[...])

    upper = lane_ids((64, 128)) >= 64
    before = got_ref[0, 576:640, :].astype(F32)
    after = got_ref[1, 576:640, :].astype(F32)
    rim_tilt = (
        jnp.where(upper, pltpu.roll(before, 64, 1), after),
        jnp.where(upper, before, pltpu.roll(after, 64, 1)),
    )
    for bx in range(2):
        for m in range(7):
            if 1 <= m <= 4:
                lane = (bx * 4 + m - 1) * 128
                v = up_ref[:, lane : lane + 128]
            else:
                lane = (bx * 3 + (0, 5, 6).index(m)) * 128
                v = rim_up[:, lane : lane + 128]
            tilt = rim_tilt[bx] if m == 6 else mslope_ref[bx, m]
            delta = (v * tilt).astype(BF16).astype(F32)
            lane = (bx * 7 + m) * 128
            for a, part in enumerate(shifts(delta, 64)):
                mid_ref[a * 64 : a * 64 + 64, lane : lane + 128] = part.astype(BF16)

    out = dot(wm_ref[...], mid_ref[...])
    upper = lane_ids((32, 128)) >= 64

    def term(a, b, x, m):
        if not 0 <= x - a < 2:
            return None
        col = ((x - a) * 7 + m) * 128
        return out[(a * 3 + b) * 32 : (a * 3 + b) * 32 + 32, col : col + 128]

    def tap_sum(b, x, m):
        parts = [v for v in (term(a, b, x, m) for a in range(3)) if v is not None]
        return sum(parts[1:], parts[0])

    for x in range(4):
        downs = [pltpu.roll(tap_sum(0, x, m), 64, 1) for m in range(7)]
        ups = [pltpu.roll(tap_sum(2, x, m), 64, 1) for m in range(7)]
        for m in range(6):
            low = ups[(m + 6) % 7] + downs[m]
            high = ups[m] + downs[m + 1]
            total_ref[x, m] = tap_sum(1, x, m) + jnp.where(upper, high, low)
    back_ref[...] = total_ref[1:3, 0:6]
    before = got_ref[0, 640:672, :].astype(F32)
    after = got_ref[1, 640:672, :].astype(F32)
    for face_ref, last in ((face1_ref, 1 - odd_x), (face2_ref, odd_x)):
        face_ref[0:192, :] = total_ref[3 * last].astype(BF16).reshape(192, 128)
        face_ref[192:384, :] = pooled_ref[last].reshape(192, 128)
        rows = (
            jnp.where(last == 1, before[24:32], before[0:8]),
            st_ref[3 * last].reshape(192, 128),
            jnp.where(last == 1, after[24:32], after[0:8]),
        )
        face_ref[384:592, :] = jnp.concatenate(rows, axis=0).astype(BF16)


def hidden_rows(hid_ref, ys):
    def tap(x, y):
        return hid_ref[x, y + 2]

    return jnp.concatenate(
        [jnp.concatenate([tap(x, y + b - 1) for y in ys for x in range(4)], axis=1) for b in range(3)], axis=0
    )


def pooled_taps(blocks):
    blocks = blocks + [jnp.zeros((32, 128), F32)]
    lower = lane_ids((32, 128)) < 64
    turned = [pltpu.roll(v, 64, 1) for v in blocks]
    taps = (
        [jnp.where(lower, turned[(m + 6) % 7], turned[m]) for m in range(7)],
        blocks,
        [jnp.where(lower, turned[m], turned[(m + 1) % 7]) for m in range(7)],
    )
    return jnp.concatenate([jnp.concatenate(v, axis=1) for v in taps], axis=0).astype(BF16)


def dec_grad_body(
    wide_ref, rim_ref, hid_ref, win_ref, rim_win_ref, hmid_ref, head_ref, pooled_ref, mid_ref,
    rows_ref, gmid_ref, hpad_ref, skip_ref,
):
    blank = jnp.zeros((2, 32, 128), BF16)
    for x in range(4):
        hpad_ref[x, 0:2] = blank
        hpad_ref[x, 26:28] = blank
        hpad_ref[x, 2:26] = hid_ref[x]
    rims = jnp.concatenate([stack_of(lambda x, r=r: rim_ref[x, r]) for r in (0, 1)], axis=1)
    skip_ref[...] = dot_nt(rims, hidden_rows(hpad_ref, (-1, 24)))

    def step(i, carry):
        y = 4 * i
        rows = jnp.concatenate([stack_of(lambda x, j=j: wide_ref[x, y + j]) for j in range(4)], axis=1)
        skip_ref[...] += dot_nt(rows, hidden_rows(hpad_ref, [y + j for j in range(4)]))
        return carry

    lax.fori_loop(0, 6, step, 0)
    rows_ref[0:288, :] = jnp.concatenate([skip_ref[...], jnp.zeros((288, 32), F32)], axis=1).astype(BF16)

    def side(bx, m):
        if 1 <= m <= 4:
            at = (bx * 4 + m - 1) * 128
            return win_ref[:, at : at + 128]
        at = (bx * 3 + (0 if m == 0 else 1)) * 128
        return rim_win_ref[:, at : at + 128]

    order = [(bx, m) for bx in range(2) for m in range(6)]
    windows = jnp.concatenate([side(bx, m) for bx, m in order], axis=1)
    hmid = jnp.concatenate([hmid_ref[bx, m] for bx, m in order], axis=1)
    lift = dot_nt(windows, hmid)
    rows_ref[288:720, :] = jnp.concatenate([lift[0:432], lift[432:864]], axis=1).astype(BF16)
    rows_ref[720:736, :] = jnp.concatenate(
        [jnp.concatenate([head_ref[...], jnp.zeros((8, 96), F32)], axis=1), jnp.zeros((8, 128), F32)], axis=0
    ).astype(BF16)
    taps = [pooled_taps([pooled_ref[bx, m].astype(F32) for m in range(6)]) for bx in range(2)]
    first, second = mid_ref[:, 0:896], mid_ref[:, 896:1792]
    gmid_ref[0:96, :] = dot_nt(taps[0], second)
    gmid_ref[96:192, :] = dot_nt(taps[0], first) + dot_nt(taps[1], second)
    gmid_ref[192:288, :] = dot_nt(taps[1], first)


def encoder_body(
    acc_ref, edge_ref, back_ref, rim1_ref, rim2_ref, got1_ref, got2_ref, slope_ref, w_ref, up_ref,
    mid_ref, gmid_ref, st_ref, dec_ref,
    rows_far, own_ref, face1_ref, face2_ref, edge_lo_ref, edge_hi_ref,
    enc_ref, wide_ref, total_ref, we_ref, rows_ref, sext_ref, sum_ref, got_ref, sems,
):
    odd_x = parity("gx")
    got_ref[1 - odd_x] = got1_ref[...]
    got_ref[odd_x] = got2_ref[...]
    got_lo_ref, got_hi_ref = got_ref.at[0], got_ref.at[1]
    writes = fetch([(dec_ref, rows_far.at[0:736])], sems.at[0])

    def beyond(ref):
        side = ref[192:384, :].astype(F32)
        return pooled_taps([side[m * 32 : m * 32 + 32] for m in range(6)])

    gmid = jnp.concatenate(
        [
            gmid_ref[0:96, :] + dot_nt(beyond(got_lo_ref), mid_ref[:, 0:896]),
            gmid_ref[96:192, :],
            gmid_ref[192:288, :] + dot_nt(beyond(got_hi_ref), mid_ref[:, 896:1792]),
        ],
        axis=0,
    )
    rows_ref[0:288, :] = gmid[:, :128].astype(BF16)
    rows_ref[288:432, :] = jnp.concatenate([gmid[:144, 128:], gmid[144:, 128:]], axis=1).astype(BF16)
    writes += fetch([(rows_ref.at[0:432], rows_far.at[736:1168])], sems.at[1])

    sext_ref[1:5, 1:25] = st_ref[...]
    sext_ref[0] = got_lo_ref[384:592, :].astype(F32).reshape(26, 8, 128)
    sext_ref[5] = got_hi_ref[384:592, :].astype(F32).reshape(26, 8, 128)
    before, after = in_order("gy", rim1_ref[640:672, :].astype(F32), rim2_ref[640:672, :].astype(F32))
    for x in range(4):
        sext_ref[x + 1, 0] = before[x * 8 : x * 8 + 8]
        sext_ref[x + 1, 25] = after[x * 8 : x * 8 + 8]

    whole = [back_ref[bx].reshape(192, 128) for bx in range(2)]
    whole = [v + ref[0:192, :].astype(F32) for v, ref in zip(whole, (got_lo_ref, got_hi_ref))]
    whole = jnp.concatenate(whole, axis=0) * 0.125
    high = whole.astype(BF16)
    low = (whole - high.astype(F32)).astype(BF16)
    wide_ref[...] = dot(jnp.concatenate([high, low], axis=1), up_ref[...])
    for bx in range(2):
        for m in range(6):
            at = (bx * 6 + m) * 32
            for half in range(2):
                fine = wide_ref[at : at + 32, half * 128 : half * 128 + 128]
                for ey in range(2):
                    y = 4 * m + 2 * half + ey
                    for ex in range(2):
                        x = 2 * bx + ex
                        sum_in = acc_ref[x, y + 1] + fine
                        if y in (0, 23):
                            sum_in = sum_in + edge_ref[x, (0, 23).index(y)]
                        delta = (sum_in * slope_ref[x, y]).astype(BF16).astype(F32)
                        lane = (y * 4 + x) * 128
                        for c, part in enumerate(shifts(delta, 128)):
                            enc_ref[c * 32 : c * 32 + 32, lane : lane + 128] = part.astype(BF16)

    for a in range(3):
        for b in range(3):
            at = (a * 3 + b) * 8
            we_ref[at : at + 8, :] = jnp.concatenate([w_ref[a, b, c].astype(F32) for c in range(3)], axis=1)
    w = we_ref[...].astype(BF16)
    total_ref[...] = jnp.zeros(total_ref.shape, F32)
    sum_ref[...] = jnp.zeros(sum_ref.shape, F32)

    def step(i, carry):
        y = 4 * i
        delta = enc_ref[:, pl.ds(pl.multiple_of(y * 512, 2048), 2048)]
        state = jnp.concatenate(
            [
                jnp.concatenate([sext_ref[x + a, y + j + b] for j in range(4) for x in range(4)], axis=1)
                for a in range(3)
                for b in range(3)
            ],
            axis=0,
        ).astype(BF16)
        sum_ref[...] += dot_nt(state, delta)
        out = dot(w, delta)
        for x in range(6):
            for r in range(6):
                parts = []
                for a in range(3):
                    for b in range(3):
                        j, own = r - b, x - a
                        if 0 <= j < 4 and 0 <= own < 4:
                            row, lane = (a * 3 + b) * 8, (j * 4 + own) * 128
                            parts.append(out[row : row + 8, lane : lane + 128])
                total_ref[x, y + r] += sum(parts[1:], parts[0])
        return carry

    lax.fori_loop(0, 6, step, 0, unroll=6)
    genc = jnp.concatenate([sum_ref[...], jnp.zeros((72, 32), F32)], axis=1)
    rows_ref[432:544, :] = jnp.concatenate([genc, jnp.zeros((40, 128), F32)], axis=0).astype(BF16)
    writes += fetch([(rows_ref.at[432:544], rows_far.at[1168:1280])], sems.at[2])
    own_ref[...] = total_ref[1:5, 1:25]
    face1_ref[...] = total_ref[5 - 5 * odd_x].reshape(208, 128).astype(BF16)
    face2_ref[...] = total_ref[5 * odd_x].reshape(208, 128).astype(BF16)
    edge_lo_ref[...] = total_ref[1:5, 0]
    edge_hi_ref[...] = total_ref[1:5, 25]
    for wait in writes:
        wait()


def corner_body(edge_lo_ref, edge_hi_ref, got1_ref, got2_ref, col1_ref, col2_ref):
    before, after = in_order("gx", got1_ref[...].astype(F32), got2_ref[...].astype(F32))
    cols = []
    for edge_ref, at in ((edge_lo_ref, 0), (edge_hi_ref, 200)):
        rows = [edge_ref[0] + before[at : at + 8], edge_ref[1], edge_ref[2], edge_ref[3] + after[at : at + 8]]
        cols.append(jnp.concatenate(rows, axis=0))
    first, second = in_order("gy", *cols)
    col1_ref[...] = first.astype(BF16)
    col2_ref[...] = second.astype(BF16)


def final_body(cot_ref, own_ref, got1_ref, got2_ref, end1_ref, end2_ref, grad_ref):
    sides = in_order("gx", got1_ref[...].astype(F32), got2_ref[...].astype(F32))
    before, after = in_order("gy", end1_ref[...].astype(F32), end2_ref[...].astype(F32))
    for x in range(4):
        total = own_ref[x]
        if x in (0, 3):
            total = total + sides[x // 3][8:200].reshape(24, 8, 128)
        at = slice(x * 8, x * 8 + 8)
        ends = [before[at][None], jnp.zeros((22, 8, 128), F32), after[at][None]]
        total = total + jnp.concatenate(ends, axis=0)
        grad_ref[:, x] = (cot_ref[:, x].astype(F32) + jnp.swapaxes(total, 0, 1)).astype(BF16)


def share_body(share, pieces_ref, out_ref):
    size = -(-share // 16) * 16
    rows = pieces_ref.shape[0]
    place = lax.broadcasted_iota(jnp.int32, (size, rows), 1)
    piece = ((place.astype(F32) + 0.5) * (1.0 / share)).astype(jnp.int32)
    same = place - piece * share == lax.broadcasted_iota(jnp.int32, (size, rows), 0)
    pick = jnp.where(same, 1.0, 0.0).astype(BF16)
    total = dot(pick, pieces_ref[...]).astype(BF16)
    out_ref[...] = dot_tn(pick, total).astype(BF16)


def unpack_body(scale, rows_ref, enc_ref, mid_ref, dec_ref, head_ref):
    def rows(at, count):
        return rows_ref[at : at + count, :].astype(F32) * scale

    skip = [rows(i * 32, 32) for i in range(9)]
    head_ref[...] = rows(720, 16)[:8, :32]
    mid_rest = [rows(1024 + i * 48, 48) for i in range(3)]
    mid_rest = jnp.concatenate(mid_rest, axis=0)
    mid_rest = jnp.concatenate([mid_rest[:, :64], mid_rest[:, 64:]], axis=0)
    enc = rows(1168, 80)
    lift = rows(288, 432)
    lift = jnp.concatenate([lift[:, :64], lift[:, 64:]], axis=0)
    for a in range(3):
        for b in range(3):
            tap = a * 3 + b
            pair = rows(736 + tap * 32, 32)
            mid_ref[a, b, 0] = pair[:, :64]
            mid_ref[a, b, 1] = pair[:, 64:]
            mid_ref[a, b, 2] = mid_rest[tap * 32 : tap * 32 + 32]
            for c in range(3):
                enc_ref[a, b, c] = enc[tap * 8 : tap * 8 + 8, c * 32 : c * 32 + 32]
                at = (tap * 3 + c) * 32
                dec_ref[a, b, c] = jnp.concatenate(
                    [lift[at : at + 32], skip[a * 3 + c][:, b * 32 : b * 32 + 32]], axis=1
                )


def pool_matrix():
    table = np.zeros((256, 3, 128), np.float32)
    for c, k in enumerate((-1, 0, 1)):
        for half in range(2):
            for q in range(64):
                for e in range(2):
                    z = 2 * q + e - k
                    if 0 <= z < 128:
                        table[half * 128 + z, c, half * 64 + q] = 1.0
    return jnp.asarray(table.reshape(256, 384), BF16)


def up_matrix():
    table = np.zeros((2, 128, 256), np.float32)
    for half in range(2):
        for z in range(128):
            table[:, half * 64 + z // 2, half * 128 + z] = 1.0
    return jnp.asarray(table.reshape(256, 256), BF16)


def swaps(first, second, axis):
    count = lax.axis_size(axis)
    pairs = [(i, i + 1) for i in range(0, count - 1, 2)], [(i, i + 1) for i in range(1, count - 1, 2)]
    return tuple(
        lax.ppermute(v, axis, ahead + [(b, a) for a, b in ahead]) for v, ahead in zip((first, second), pairs)
    )


def on_device(
    state_now, enc_pre, mid_pre, dec_pre, cotangent, enc_kernel, mid_kernel, dec_kernel, out_kernel
):
    state_now, enc_pre, mid_pre, dec_pre, cotangent = (
        v[0] for v in (state_now, enc_pre, mid_pre, dec_pre, cotangent)
    )
    cells = state_now[0].size * lax.axis_size("gx") * lax.axis_size("gy") * lax.axis_size("dp")
    grad_scale = 1.0 / math.sqrt(cells)
    pool = pool_matrix()
    dec_w = dec_kernel.transpose(2, 3, 4, 0, 1)
    mid_w = mid_kernel.transpose(2, 3, 4, 1, 0)
    enc_w = enc_kernel.transpose(2, 3, 4, 1, 0)

    plane = sds((24, 32, 128), BF16)
    face1, face2 = call(
        face_body,
        [plane, plane],
        [
            pltpu.VMEM((2, 32, 24, 128), BF16),
            pltpu.VMEM((2, 8, 24, 128), BF16),
            pltpu.VMEM((8, 32), BF16),
            pltpu.VMEM((2, 24, 32, 128), BF16),
            pltpu.SemaphoreType.DMA((5,)),
            pltpu.SemaphoreType.DMA((2, 1)),
        ],
        (dec_pre, cotangent, out_kernel),
        200 << 20, 56, far=3, far_outs=2,
    )
    got1, got2 = swaps(face1, face2, "gx")
    mid_blocks = mid_pre.reshape(64, 2, 6, 2, 64).transpose(1, 2, 0, 3, 4).reshape(2, 6, 64, 128)
    (
        delta, head_grad, hidden, enc_slope, pooled, hidden_mid, mid_slope, state,
        tail_lo, tail_hi,
    ) = call(
        forward_body,
        [
            sds((2, 24, 32, 128), BF16),
            sds((8, 32), F32),
            sds((4, 24, 32, 128), BF16),
            sds((4, 24, 32, 128), F32),
            sds((2, 6, 32, 128), BF16),
            sds((2, 6, 64, 128), BF16),
            sds((2, 6, 64, 128), F32),
            sds((4, 24, 8, 128), F32),
            sds((96, 128), BF16),
            sds((96, 128), BF16),
        ],
        [],
        (dec_pre, cotangent, out_kernel, enc_pre, state_now, mid_blocks, pool),
        600 << 20, 16,
    )


    def column(at, tail):
        rows = (got1[at], face1[at], delta[0, at], delta[1, at], face2[at], got2[at], tail)
        return jnp.concatenate([v.reshape(-1, 128) for v in rows])

    ends = column(slice(0, 3), tail_lo), column(slice(21, 24), tail_hi)
    rim1, rim2 = swaps(*in_order("gy", *ends), "gy")
    acc, wide, win, up, wskip, wmid, wup = call(
        inner_body,
        [
            sds((4, 26, 32, 128), F32),
            sds((6, 24, 96, 128), BF16),
            sds((864, 1024), BF16),
            sds((64, 1024), F32),
            sds((96, 288), BF16),
            sds((288, 192), BF16),
            sds((64, 864), BF16),
        ],
        [],
        (got1, face1, delta, face2, got2, pool, dec_w, mid_w),
        3 << 30, 24,
    )
    edge, rim_wide, rim_win, mid_wide, back, face1, face2 = call(
        outer_body,
        [
            sds((4, 2, 32, 128), F32),
            sds((6, 2, 96, 128), BF16),
            sds((864, 768), BF16),
            sds((192, 1792), BF16),
            sds((2, 6, 32, 128), F32),
            sds((592, 128), BF16),
            sds((592, 128), BF16),
        ],
        [pltpu.VMEM((4, 6, 32, 128), F32), pltpu.VMEM((2, 672, 128), BF16)],
        (rim1, rim2, wide, up, mid_slope, state, pooled, pool, wup, wskip, wmid),
        1 << 30, 24,
    )
    got1, got2 = swaps(face1, face2, "gx")
    dec_rows, mid_grad = call(
        dec_grad_body,
        [sds((736, 128), BF16), sds((288, 192), F32)],
        [pltpu.VMEM((4, 28, 32, 128), BF16), pltpu.VMEM((288, 96), F32)],
        (wide, rim_wide, hidden, win, rim_win, hidden_mid, head_grad, pooled, mid_wide),
        3 << 30, 20,
    )
    dec_rows, mid_grad, got1, got2 = lax.optimization_barrier((dec_rows, mid_grad, got1, got2))
    rows, own, face1, face2, edge_lo, edge_hi = call(
        encoder_body,
        [
            sds((1280, 128), BF16),
            sds((4, 24, 8, 128), F32),
            sds((208, 128), BF16),
            sds((208, 128), BF16),
            sds((4, 8, 128), F32),
            sds((4, 8, 128), F32),
        ],
        [
            pltpu.VMEM((96, 24 * 512), BF16),
            pltpu.VMEM((384, 256), F32),
            pltpu.VMEM((6, 26, 8, 128), F32),
            pltpu.VMEM((72, 96), F32),
            pltpu.VMEM((544, 128), BF16),
            pltpu.VMEM((6, 26, 8, 128), F32),
            pltpu.VMEM((72, 96), F32),
            pltpu.VMEM((2, 592, 128), BF16),
            pltpu.SemaphoreType.DMA((3, 1)),
        ],
        (
            acc, edge, back, rim1, rim2, got1, got2, enc_slope, enc_w, up_matrix(),
            mid_wide, mid_grad, state, dec_rows,
        ),
        2 << 30, 24, far_outs=1,
    )
    last1, last2 = swaps(face1, face2, "gx")

    axes = ("dp", "gx", "gy")
    count = lax.axis_size(axes)
    share = 1280 // count
    shape = (count, share // 2, 2, 128)
    pieces = lax.all_to_all(rows.reshape(shape), axes, 0, 0).reshape(1280, 128)
    (shares,) = call(
        functools.partial(share_body, share), [sds((1280, 128), BF16)], [], (pieces,), 1 << 20, 8
    )
    shares, last1, last2 = lax.optimization_barrier((shares, last1, last2))
    rows = lax.all_to_all(shares.reshape(shape), axes, 0, 0).reshape(1280, 128)
    col1, col2 = call(
        corner_body, [sds((32, 128), BF16)] * 2, [], (edge_lo, edge_hi, last1, last2), 1 << 16, 4
    )
    end1, end2 = swaps(col1, col2, "gy")
    genc, gmid, gdec, ghead = call(
        functools.partial(unpack_body, grad_scale),
        [sds((3, 3, 3, 8, 32), F32), sds((3, 3, 3, 32, 64), F32), sds((3, 3, 3, 32, 96), F32), sds((8, 32), F32)],
        [],
        (rows,),
        1 << 20, 12,
    )
    genc, end1, end2 = lax.optimization_barrier((genc, end1, end2))
    (state_grad,) = call(
        final_body,
        [sds((8, 4, 24, 128), BF16)],
        [],
        (cotangent, own, last1, last2, end1, end2),
        1 << 20, 8,
    )
    return (
        state_grad[None],
        genc.transpose(4, 3, 0, 1, 2),
        gmid.transpose(4, 3, 0, 1, 2),
        gdec.transpose(3, 4, 0, 1, 2),
        ghead,
    )


def solution(mesh):
    grid = P("dp", None, "gx", "gy", None)
    return jax.shard_map(
        on_device,
        mesh=mesh,
        in_specs=(grid,) * 5 + (P(),) * 4,
        out_specs=(grid, P(), P(), P(), P()),
        check_vma=False,
    )
```

```python
import functools
import math

import jax
import jax.numpy as jnp
import numpy as np
from jax import lax
from jax.experimental import pallas as pl
from jax.experimental.pallas import tpu as pltpu
from jax.sharding import PartitionSpec as P

F32 = jnp.float32
BF16 = jnp.bfloat16


VMEM = pl.BlockSpec(memory_space=pltpu.VMEM)
HBM = pl.BlockSpec(memory_space=pltpu.HBM)


def call(body, outs, scratch, args, flops, limit, far=0, far_outs=0):
    return pl.pallas_call(
        body,
        out_shape=outs,
        in_specs=[HBM] * far + [VMEM] * (len(args) - far),
        out_specs=[HBM] * far_outs + [VMEM] * (len(outs) - far_outs),
        scratch_shapes=scratch,
        compiler_params=pltpu.CompilerParams(vmem_limit_bytes=limit << 20),
        cost_estimate=pl.CostEstimate(flops=flops, bytes_accessed=4 << 20, transcendentals=0),
    )(*args)


def fetch(pairs, sems):
    copies = [pltpu.make_async_copy(src, dst, sems.at[i]) for i, (src, dst) in enumerate(pairs)]
    for copy in copies:
        copy.start()
    return [copy.wait for copy in copies]


def sds(shape, dtype):
    return jax.ShapeDtypeStruct(shape, dtype)


def dot(a, b):
    return lax.dot_general(a, b, (((1,), (0,)), ((), ())), preferred_element_type=F32)


def dot_tn(a, b):
    return lax.dot_general(a, b, (((0,), (0,)), ((), ())), preferred_element_type=F32)


def dot_nt(a, b):
    return lax.dot_general(a, b, (((1,), (1,)), ((), ())), preferred_element_type=F32)


def sigmoid(v):
    return 0.5 + 0.5 * jnp.tanh(0.5 * v)


def slope(v, s):
    return s * (1.0 + v * (1.0 - s))


def parity(axis):
    return jnp.bitwise_and(lax.axis_index(axis), 1)


def in_order(axis, first, second):
    odd = parity(axis) == 1
    return jnp.where(odd, first, second), jnp.where(odd, second, first)


def lane_ids(shape):
    return lax.broadcasted_iota(jnp.int32, shape, len(shape) - 1)


def shifts(v, period):
    lane = jnp.bitwise_and(lane_ids(v.shape), period - 1)
    axis = v.ndim - 1
    size = v.shape[-1]
    back = jnp.where(lane == period - 1, 0.0, pltpu.roll(v, size - 1, axis))
    ahead = jnp.where(lane == 0, 0.0, pltpu.roll(v, 1, axis))
    return back, v, ahead


def delta_plane(dec, cot, head):
    pre = jnp.swapaxes(dec.astype(F32), 0, 1)
    cot = jnp.swapaxes(cot.astype(F32), 0, 1)
    cot_lanes = jnp.concatenate([cot[y] for y in range(24)], axis=1).astype(BF16)
    back = dot_tn(head, cot_lanes)
    back = jnp.stack([back[:, y * 128 : y * 128 + 128] for y in range(24)], axis=0)
    s = sigmoid(pre)
    return (back * slope(pre, s)).astype(BF16), cot_lanes, pre * s


def face_body(dec_far, cot_far, head_far, first_far, second_far, dec_ref, cot_ref, head_ref, delta_ref, sems, out_sems):
    odd = parity("gx")
    planes = (3 - 3 * odd, 3 * odd)
    pairs = [(head_far, head_ref)]
    for i, x in enumerate(planes):
        pairs += [(cot_far.at[:, x], cot_ref.at[i]), (dec_far.at[:, x], dec_ref.at[i])]
    waits = fetch(pairs, sems)
    waits[0]()
    writes = []
    for i, far in enumerate((first_far, second_far)):
        waits[2 * i + 1]()
        waits[2 * i + 2]()
        delta_ref[i] = delta_plane(dec_ref[i], cot_ref[i], head_ref[...])[0]
        writes += fetch([(delta_ref.at[i], far)], out_sems.at[i])
    for wait in writes:
        wait()


def forward_body(
    dec_ref, cot_ref, head_ref, enc_ref, state_ref, mid_ref, pool_ref,
    delta_ref, head_grad_ref, hid_ref, slope_ref, pooled_ref, hmid_ref, mslope_ref, st_ref, ylo_ref, yhi_ref,
):
    total = jnp.zeros((8, 32), F32)
    for x in range(4):
        delta, cot_lanes, decoded = delta_plane(dec_ref[:, x], cot_ref[:, x], head_ref[...])
        if x in (1, 2):
            delta_ref[x - 1] = delta
        decoded = jnp.concatenate([decoded[y] for y in range(24)], axis=1).astype(BF16)
        total = total + dot_nt(cot_lanes, decoded)
    head_grad_ref[...] = total
    low_rows, high_rows = [], []
    for x in range(4):
        pre = jnp.swapaxes(enc_ref[:, x].astype(F32), 0, 1)
        s = sigmoid(pre)
        hid_ref[x] = (pre * s).astype(BF16)
        slope_ref[x] = slope(pre, s)
        state = jnp.swapaxes(state_ref[:, x].astype(F32), 0, 1)
        st_ref[x] = state
        low_rows.append(state[0])
        high_rows.append(state[23])
    ylo_ref[64:96, :] = jnp.concatenate(low_rows, axis=0).astype(BF16)
    yhi_ref[64:96, :] = jnp.concatenate(high_rows, axis=0).astype(BF16)
    tilts = {}
    for bx in range(2):
        for m in range(6):
            acc = None
            for ex in range(2):
                for ey in range(2):
                    pair = jnp.concatenate(
                        [hid_ref[2 * bx + ex, 4 * m + ey], hid_ref[2 * bx + ex, 4 * m + 2 + ey]], axis=1
                    )
                    part = dot(pair, pool_ref[:, 128:256])
                    acc = part if acc is None else acc + part
            pooled = (acc * 0.125).astype(BF16)
            pooled_ref[bx, m] = pooled
            pre = mid_ref[bx, m].astype(F32)
            s = sigmoid(pre)
            hmid_ref[bx, m] = (pre * s).astype(BF16)
            tilts[bx, m] = slope(pre, s)
            mslope_ref[bx, m] = tilts[bx, m]
    lower = lane_ids((64, 128)) < 64
    ylo_ref[0:64, :] = jnp.where(lower, tilts[0, 0], pltpu.roll(tilts[1, 0], 64, 1)).astype(BF16)
    yhi_ref[0:64, :] = jnp.where(lower, pltpu.roll(tilts[0, 5], 64, 1), tilts[1, 5]).astype(BF16)


def window_sums(rows_of, pool, put):
    got = dot(
        jnp.concatenate([jnp.concatenate([rows_of(x, j) for j in range(4)], axis=0) for x in range(6)], axis=0), pool
    )
    sums = []
    for x in range(6):
        at = [got[x * 128 + j * 32 : x * 128 + j * 32 + 32] for j in range(4)]
        sums.append([at[j] + at[j + 1] for j in (2, 1, 0)])
    for bx in range(2):
        for a, kx in enumerate((-1, 0, 1)):
            for b in range(3):
                both = (sums[2 * bx - kx + 1][b] + sums[2 * bx - kx + 2][b]).astype(BF16)
                for c in range(3):
                    put(bx, ((a * 3 + b) * 3 + c) * 32, both[:, c * 128 : c * 128 + 128])


def stack_of(row):
    return jnp.concatenate(
        [jnp.concatenate([row(x + 1 - kx) for x in range(4)], axis=1) for kx in (-1, 0, 1)], axis=0
    )


def skip_weights(w_ref):
    parts = [
        jnp.concatenate([w_ref[a, b].astype(F32).reshape(96, 96)[:, 64:96] for b in range(3)], axis=1)
        for a in range(3)
    ]
    return jnp.concatenate(parts, axis=0).T.astype(BF16)


def inner_body(got1_ref, face1_ref, delta_ref, face2_ref, got2_ref, pool_ref, w_ref, wmid_ref, acc_ref, wide_ref, win_ref, up_ref, wskip_ref, wm_ref, wup_ref):
    def put(x, v):
        parts = shifts(v.astype(F32).reshape(768, 128), 128)
        for a in range(3):
            wide_ref[x, :, a * 32 : a * 32 + 32, :] = parts[a].astype(BF16).reshape(24, 32, 128)

    odd = parity("gx")
    put(5 - 5 * odd, got1_ref[...])
    put(4 - 3 * odd, face1_ref[...])
    put(2, delta_ref[0])
    put(3, delta_ref[1])
    put(1 + 3 * odd, face2_ref[...])
    put(5 * odd, got2_ref[...])
    wskip_ref[...] = skip_weights(w_ref)
    acc_ref[...] = jnp.zeros(acc_ref.shape, F32)

    def step(i, carry):
        y = 4 * i
        out = dot(
            wskip_ref[...],
            jnp.concatenate([stack_of(lambda x, j=j: wide_ref[x, y + j]) for j in range(4)], axis=1),
        )
        for x in range(4):
            for r in range(6):
                parts = [
                    out[b * 32 : b * 32 + 32, ((r - b) * 4 + x) * 128 : ((r - b) * 4 + x) * 128 + 128]
                    for b in range(3)
                    if 0 <= r - b < 4
                ]
                acc_ref[x, y + r] += sum(parts[1:], parts[0])
        return carry

    lax.fori_loop(0, 6, step, 0, unroll=2)
    for m in range(1, 5):

        def rows_of(x, j):
            return jnp.concatenate(
                [wide_ref[x, 4 * m + j - 1, 32:64, :], wide_ref[x, 4 * m + j + 1, 32:64, :]], axis=1
            )

        def put_window(bx, row, v):
            lane = (bx * 4 + m - 1) * 128
            win_ref[row : row + 32, lane : lane + 128] = v

        window_sums(rows_of, pool_ref[...], put_window)
    wup_ref[...] = w_ref[...].reshape(864, 96).astype(F32).T[:64].astype(BF16)
    up_ref[...] = dot(wup_ref[...], win_ref[...])
    for a in range(3):
        for b in range(3):
            at = (a * 3 + b) * 32
            parts = [wmid_ref[a, b, c].astype(F32) for c in range(3)]
            wm_ref[at : at + 32, :] = jnp.concatenate(parts, axis=1).astype(BF16)


def outer_body(
    got1_ref, got2_ref, wide_ref, up_ref, mslope_ref, st_ref, pooled_ref, pool_ref, wup_ref, wskip_ref, wm_ref,
    edge_ref, rim_ref, win_ref, mid_ref, back_ref, face1_ref, face2_ref,
    total_ref, got_ref,
):
    wskip = wskip_ref[...]
    odd_x, odd_y = parity("gx"), parity("gy")
    got_ref[1 - odd_y] = got1_ref[...]
    got_ref[odd_y] = got2_ref[...]

    def row(x, y):
        if 0 <= y <= 23:
            return wide_ref[x, y, 32:64, :]
        slot = x + (1 - odd_x) * (5, 3, 0, 0, -3, -5)[x]
        at = (slot * 3 + (y + 3 if y < 0 else y - 24)) * 32
        return got_ref[0 if y < 0 else 1, pl.ds(pl.multiple_of(at, 32), 32), :]

    for x in range(6):
        v = jnp.concatenate([row(x, -1), row(x, 24)], axis=0).astype(F32)
        parts = shifts(v, 128)
        for a in range(3):
            rim_ref[x, :, a * 32 : a * 32 + 32, :] = parts[a].astype(BF16).reshape(2, 32, 128)
    outs = [dot(wskip, stack_of(lambda x, r=r: rim_ref[x, r])) for r in range(2)]
    for x in range(4):
        at = slice(x * 128, x * 128 + 128)
        edge_ref[x, 0] = outs[0][64:96, at]
        edge_ref[x, 1] = outs[1][0:32, at]

    for i, (left, right) in enumerate(((-1, 1), (19, 21), (23, -3))):

        def rows_of(x, j):
            return jnp.concatenate([row(x, left + j), row(x, right + j)], axis=1)

        def put_window(bx, r, v):
            lane = (bx * 3 + i) * 128
            win_ref[r : r + 32, lane : lane + 128] = v

        window_sums(rows_of, pool_ref[...], put_window)
    rim_up = dot(wup_ref[...], win_ref[...])

    upper = lane_ids((64, 128)) >= 64
    before = got_ref[0, 576:640, :].astype(F32)
    after = got_ref[1, 576:640, :].astype(F32)
    rim_tilt = (
        jnp.where(upper, pltpu.roll(before, 64, 1), after),
        jnp.where(upper, before, pltpu.roll(after, 64, 1)),
    )
    for bx in range(2):
        for m in range(7):
            if 1 <= m <= 4:
                lane = (bx * 4 + m - 1) * 128
                v = up_ref[:, lane : lane + 128]
            else:
                lane = (bx * 3 + (0, 5, 6).index(m)) * 128
                v = rim_up[:, lane : lane + 128]
            tilt = rim_tilt[bx] if m == 6 else mslope_ref[bx, m]
            delta = (v * tilt).astype(BF16).astype(F32)
            lane = (bx * 7 + m) * 128
            for a, part in enumerate(shifts(delta, 64)):
                mid_ref[a * 64 : a * 64 + 64, lane : lane + 128] = part.astype(BF16)

    out = dot(wm_ref[...], mid_ref[...])
    upper = lane_ids((32, 128)) >= 64

    def term(a, b, x, m):
        if not 0 <= x - a < 2:
            return None
        col = ((x - a) * 7 + m) * 128
        return out[(a * 3 + b) * 32 : (a * 3 + b) * 32 + 32, col : col + 128]

    def tap_sum(b, x, m):
        parts = [v for v in (term(a, b, x, m) for a in range(3)) if v is not None]
        return sum(parts[1:], parts[0])

    for x in range(4):
        downs = [pltpu.roll(tap_sum(0, x, m), 64, 1) for m in range(7)]
        ups = [pltpu.roll(tap_sum(2, x, m), 64, 1) for m in range(7)]
        for m in range(6):
            low = ups[(m + 6) % 7] + downs[m]
            high = ups[m] + downs[m + 1]
            total_ref[x, m] = tap_sum(1, x, m) + jnp.where(upper, high, low)
    back_ref[...] = total_ref[1:3, 0:6]
    before = got_ref[0, 640:672, :].astype(F32)
    after = got_ref[1, 640:672, :].astype(F32)
    for face_ref, last in ((face1_ref, 1 - odd_x), (face2_ref, odd_x)):
        face_ref[0:192, :] = total_ref[3 * last].astype(BF16).reshape(192, 128)
        face_ref[192:384, :] = pooled_ref[last].reshape(192, 128)
        rows = (
            jnp.where(last == 1, before[24:32], before[0:8]),
            st_ref[3 * last].reshape(192, 128),
            jnp.where(last == 1, after[24:32], after[0:8]),
        )
        face_ref[384:592, :] = jnp.concatenate(rows, axis=0).astype(BF16)


def hidden_rows(hid_ref, ys):
    def tap(x, y):
        return hid_ref[x, y + 2]

    return jnp.concatenate(
        [jnp.concatenate([tap(x, y + b - 1) for y in ys for x in range(4)], axis=1) for b in range(3)], axis=0
    )


def pooled_taps(blocks):
    blocks = blocks + [jnp.zeros((32, 128), F32)]
    lower = lane_ids((32, 128)) < 64
    turned = [pltpu.roll(v, 64, 1) for v in blocks]
    taps = (
        [jnp.where(lower, turned[(m + 6) % 7], turned[m]) for m in range(7)],
        blocks,
        [jnp.where(lower, turned[m], turned[(m + 1) % 7]) for m in range(7)],
    )
    return jnp.concatenate([jnp.concatenate(v, axis=1) for v in taps], axis=0).astype(BF16)


def dec_grad_body(
    wide_ref, rim_ref, hid_ref, win_ref, rim_win_ref, hmid_ref, head_ref, pooled_ref, mid_ref,
    rows_ref, gmid_ref, hpad_ref, skip_ref,
):
    blank = jnp.zeros((2, 32, 128), BF16)
    for x in range(4):
        hpad_ref[x, 0:2] = blank
        hpad_ref[x, 26:28] = blank
        hpad_ref[x, 2:26] = hid_ref[x]
    rims = jnp.concatenate([stack_of(lambda x, r=r: rim_ref[x, r]) for r in (0, 1)], axis=1)
    skip_ref[...] = dot_nt(rims, hidden_rows(hpad_ref, (-1, 24)))

    def step(i, carry):
        y = 4 * i
        rows = jnp.concatenate([stack_of(lambda x, j=j: wide_ref[x, y + j]) for j in range(4)], axis=1)
        skip_ref[...] += dot_nt(rows, hidden_rows(hpad_ref, [y + j for j in range(4)]))
        return carry

    lax.fori_loop(0, 6, step, 0, unroll=2)
    rows_ref[0:288, :] = jnp.concatenate([skip_ref[...], jnp.zeros((288, 32), F32)], axis=1).astype(BF16)

    def side(bx, m):
        if 1 <= m <= 4:
            at = (bx * 4 + m - 1) * 128
            return win_ref[:, at : at + 128]
        at = (bx * 3 + (0 if m == 0 else 1)) * 128
        return rim_win_ref[:, at : at + 128]

    order = [(bx, m) for bx in range(2) for m in range(6)]
    windows = jnp.concatenate([side(bx, m) for bx, m in order], axis=1)
    hmid = jnp.concatenate([hmid_ref[bx, m] for bx, m in order], axis=1)
    lift = dot_nt(windows, hmid)
    rows_ref[288:720, :] = jnp.concatenate([lift[0:432], lift[432:864]], axis=1).astype(BF16)
    rows_ref[720:736, :] = jnp.concatenate(
        [jnp.concatenate([head_ref[...], jnp.zeros((8, 96), F32)], axis=1), jnp.zeros((8, 128), F32)], axis=0
    ).astype(BF16)
    taps = [pooled_taps([pooled_ref[bx, m].astype(F32) for m in range(6)]) for bx in range(2)]
    first, second = mid_ref[:, 0:896], mid_ref[:, 896:1792]
    gmid_ref[0:96, :] = dot_nt(taps[0], second)
    gmid_ref[96:192, :] = dot_nt(taps[0], first) + dot_nt(taps[1], second)
    gmid_ref[192:288, :] = dot_nt(taps[1], first)


def encoder_body(
    acc_ref, edge_ref, back_ref, rim1_ref, rim2_ref, got1_ref, got2_ref, slope_ref, w_ref, up_ref,
    mid_ref, gmid_ref, st_ref, dec_ref,
    rows_far, own_ref, face1_ref, face2_ref, edge_lo_ref, edge_hi_ref,
    enc_ref, wide_ref, total_ref, we_ref, rows_ref, sext_ref, sum_ref, got_ref, sems,
):
    odd_x = parity("gx")
    got_ref[1 - odd_x] = got1_ref[...]
    got_ref[odd_x] = got2_ref[...]
    got_lo_ref, got_hi_ref = got_ref.at[0], got_ref.at[1]
    writes = fetch([(dec_ref, rows_far.at[0:736])], sems.at[0])

    def beyond(ref):
        side = ref[192:384, :].astype(F32)
        return pooled_taps([side[m * 32 : m * 32 + 32] for m in range(6)])

    gmid = jnp.concatenate(
        [
            gmid_ref[0:96, :] + dot_nt(beyond(got_lo_ref), mid_ref[:, 0:896]),
            gmid_ref[96:192, :],
            gmid_ref[192:288, :] + dot_nt(beyond(got_hi_ref), mid_ref[:, 896:1792]),
        ],
        axis=0,
    )
    rows_ref[0:288, :] = gmid[:, :128].astype(BF16)
    rows_ref[288:432, :] = jnp.concatenate([gmid[:144, 128:], gmid[144:, 128:]], axis=1).astype(BF16)
    writes += fetch([(rows_ref.at[0:432], rows_far.at[736:1168])], sems.at[1])

    sext_ref[1:5, 1:25] = st_ref[...]
    sext_ref[0] = got_lo_ref[384:592, :].astype(F32).reshape(26, 8, 128)
    sext_ref[5] = got_hi_ref[384:592, :].astype(F32).reshape(26, 8, 128)
    before, after = in_order("gy", rim1_ref[640:672, :].astype(F32), rim2_ref[640:672, :].astype(F32))
    for x in range(4):
        sext_ref[x + 1, 0] = before[x * 8 : x * 8 + 8]
        sext_ref[x + 1, 25] = after[x * 8 : x * 8 + 8]

    whole = [back_ref[bx].reshape(192, 128) for bx in range(2)]
    whole = [v + ref[0:192, :].astype(F32) for v, ref in zip(whole, (got_lo_ref, got_hi_ref))]
    whole = jnp.concatenate(whole, axis=0) * 0.125
    high = whole.astype(BF16)
    low = (whole - high.astype(F32)).astype(BF16)
    wide_ref[...] = dot(jnp.concatenate([high, low], axis=1), up_ref[...])
    for bx in range(2):
        for m in range(6):
            at = (bx * 6 + m) * 32
            for half in range(2):
                fine = wide_ref[at : at + 32, half * 128 : half * 128 + 128]
                for ey in range(2):
                    y = 4 * m + 2 * half + ey
                    for ex in range(2):
                        x = 2 * bx + ex
                        sum_in = acc_ref[x, y + 1] + fine
                        if y in (0, 23):
                            sum_in = sum_in + edge_ref[x, (0, 23).index(y)]
                        delta = (sum_in * slope_ref[x, y]).astype(BF16).astype(F32)
                        lane = (y * 4 + x) * 128
                        for c, part in enumerate(shifts(delta, 128)):
                            enc_ref[c * 32 : c * 32 + 32, lane : lane + 128] = part.astype(BF16)

    for a in range(3):
        for b in range(3):
            at = (a * 3 + b) * 8
            we_ref[at : at + 8, :] = jnp.concatenate([w_ref[a, b, c].astype(F32) for c in range(3)], axis=1)
    w = we_ref[...].astype(BF16)
    total_ref[...] = jnp.zeros(total_ref.shape, F32)
    sum_ref[...] = jnp.zeros(sum_ref.shape, F32)

    def step(i, carry):
        y = 4 * i
        delta = enc_ref[:, pl.ds(pl.multiple_of(y * 512, 2048), 2048)]
        state = jnp.concatenate(
            [
                jnp.concatenate([sext_ref[x + a, y + j + b] for j in range(4) for x in range(4)], axis=1)
                for a in range(3)
                for b in range(3)
            ],
            axis=0,
        ).astype(BF16)
        sum_ref[...] += dot_nt(state, delta)
        out = dot(w, delta)
        for x in range(6):
            for r in range(6):
                parts = []
                for a in range(3):
                    for b in range(3):
                        j, own = r - b, x - a
                        if 0 <= j < 4 and 0 <= own < 4:
                            row, lane = (a * 3 + b) * 8, (j * 4 + own) * 128
                            parts.append(out[row : row + 8, lane : lane + 128])
                total_ref[x, y + r] += sum(parts[1:], parts[0])
        return carry

    lax.fori_loop(0, 6, step, 0, unroll=6)
    genc = jnp.concatenate([sum_ref[...], jnp.zeros((72, 32), F32)], axis=1)
    rows_ref[432:544, :] = jnp.concatenate([genc, jnp.zeros((40, 128), F32)], axis=0).astype(BF16)
    writes += fetch([(rows_ref.at[432:544], rows_far.at[1168:1280])], sems.at[2])
    own_ref[...] = total_ref[1:5, 1:25]
    face1_ref[...] = total_ref[5 - 5 * odd_x].reshape(208, 128).astype(BF16)
    face2_ref[...] = total_ref[5 * odd_x].reshape(208, 128).astype(BF16)
    edge_lo_ref[...] = total_ref[1:5, 0]
    edge_hi_ref[...] = total_ref[1:5, 25]
    for wait in writes:
        wait()


def corner_body(edge_lo_ref, edge_hi_ref, got1_ref, got2_ref, col1_ref, col2_ref):
    before, after = in_order("gx", got1_ref[...].astype(F32), got2_ref[...].astype(F32))
    cols = []
    for edge_ref, at in ((edge_lo_ref, 0), (edge_hi_ref, 200)):
        rows = [edge_ref[0] + before[at : at + 8], edge_ref[1], edge_ref[2], edge_ref[3] + after[at : at + 8]]
        cols.append(jnp.concatenate(rows, axis=0))
    first, second = in_order("gy", *cols)
    col1_ref[...] = first.astype(BF16)
    col2_ref[...] = second.astype(BF16)


def final_body(cot_ref, own_ref, got1_ref, got2_ref, end1_ref, end2_ref, grad_ref):
    sides = in_order("gx", got1_ref[...].astype(F32), got2_ref[...].astype(F32))
    before, after = in_order("gy", end1_ref[...].astype(F32), end2_ref[...].astype(F32))
    for x in range(4):
        total = own_ref[x]
        if x in (0, 3):
            total = total + sides[x // 3][8:200].reshape(24, 8, 128)
        at = slice(x * 8, x * 8 + 8)
        ends = [before[at][None], jnp.zeros((22, 8, 128), F32), after[at][None]]
        total = total + jnp.concatenate(ends, axis=0)
        grad_ref[:, x] = (cot_ref[:, x].astype(F32) + jnp.swapaxes(total, 0, 1)).astype(BF16)


def share_body(share, pieces_ref, out_ref):
    size = -(-share // 16) * 16
    rows = pieces_ref.shape[0]
    place = lax.broadcasted_iota(jnp.int32, (size, rows), 1)
    piece = ((place.astype(F32) + 0.5) * (1.0 / share)).astype(jnp.int32)
    same = place - piece * share == lax.broadcasted_iota(jnp.int32, (size, rows), 0)
    pick = jnp.where(same, 1.0, 0.0).astype(BF16)
    total = dot(pick, pieces_ref[...]).astype(BF16)
    out_ref[...] = dot_tn(pick, total).astype(BF16)


def unpack_body(
    scale, rows_ref, enc_far, mid_far, dec_far, head_far, enc_ref, mid_ref, dec_ref, head_ref, sems
):
    def rows(at, count):
        return rows_ref[at : at + count, :].astype(F32) * scale

    mid_rest = rows(1024, 144)
    mid_rest = jnp.concatenate([mid_rest[:, :64], mid_rest[:, 64:]], axis=0)
    for a in range(3):
        for b in range(3):
            tap = a * 3 + b
            pair = rows(736 + tap * 32, 32)
            mid_ref[a, b, 0] = pair[:, :64]
            mid_ref[a, b, 1] = pair[:, 64:]
            mid_ref[a, b, 2] = mid_rest[tap * 32 : tap * 32 + 32]
    writes = fetch([(mid_ref, mid_far)], sems.at[0])
    lift = rows(288, 432)
    lift = jnp.concatenate([lift[:, :64], lift[:, 64:]], axis=0)
    for a in range(3):
        skip = [rows((a * 3 + c) * 32, 32) for c in range(3)]
        for b in range(3):
            for c in range(3):
                at = ((a * 3 + b) * 3 + c) * 32
                dec_ref[a, b, c] = jnp.concatenate([lift[at : at + 32], skip[c][:, b * 32 : b * 32 + 32]], axis=1)
        writes += fetch([(dec_ref.at[a], dec_far.at[a])], sems.at[1 + a])
    enc = rows(1168, 80)
    for a in range(3):
        for b in range(3):
            for c in range(3):
                tap = a * 3 + b
                enc_ref[a, b, c] = enc[tap * 8 : tap * 8 + 8, c * 32 : c * 32 + 32]
    head_ref[...] = rows(720, 16)[:8, :32]
    writes += fetch([(enc_ref, enc_far), (head_ref, head_far)], sems.at[4])
    for wait in writes:
        wait()


def pool_matrix():
    table = np.zeros((256, 3, 128), np.float32)
    for c, k in enumerate((-1, 0, 1)):
        for half in range(2):
            for q in range(64):
                for e in range(2):
                    z = 2 * q + e - k
                    if 0 <= z < 128:
                        table[half * 128 + z, c, half * 64 + q] = 1.0
    return jnp.asarray(table.reshape(256, 384), BF16)


def up_matrix():
    table = np.zeros((2, 128, 256), np.float32)
    for half in range(2):
        for z in range(128):
            table[:, half * 64 + z // 2, half * 128 + z] = 1.0
    return jnp.asarray(table.reshape(256, 256), BF16)


def swaps(first, second, axis):
    count = lax.axis_size(axis)
    pairs = [(i, i + 1) for i in range(0, count - 1, 2)], [(i, i + 1) for i in range(1, count - 1, 2)]
    return tuple(
        lax.ppermute(v, axis, ahead + [(b, a) for a, b in ahead]) for v, ahead in zip((first, second), pairs)
    )


def on_device(
    state_now, enc_pre, mid_pre, dec_pre, cotangent, enc_kernel, mid_kernel, dec_kernel, out_kernel
):
    state_now, enc_pre, mid_pre, dec_pre, cotangent = (
        v[0] for v in (state_now, enc_pre, mid_pre, dec_pre, cotangent)
    )
    cells = state_now[0].size * lax.axis_size("gx") * lax.axis_size("gy") * lax.axis_size("dp")
    grad_scale = 1.0 / math.sqrt(cells)
    pool = pool_matrix()
    dec_w = dec_kernel.transpose(2, 3, 4, 0, 1)
    mid_w = mid_kernel.transpose(2, 3, 4, 1, 0)
    enc_w = enc_kernel.transpose(2, 3, 4, 1, 0)

    plane = sds((24, 32, 128), BF16)
    face1, face2 = call(
        face_body,
        [plane, plane],
        [
            pltpu.VMEM((2, 32, 24, 128), BF16),
            pltpu.VMEM((2, 8, 24, 128), BF16),
            pltpu.VMEM((8, 32), BF16),
            pltpu.VMEM((2, 24, 32, 128), BF16),
            pltpu.SemaphoreType.DMA((5,)),
            pltpu.SemaphoreType.DMA((2, 1)),
        ],
        (dec_pre, cotangent, out_kernel),
        200 << 20, 56, far=3, far_outs=2,
    )
    got1, got2 = swaps(face1, face2, "gx")
    mid_blocks = mid_pre.reshape(64, 2, 6, 2, 64).transpose(1, 2, 0, 3, 4).reshape(2, 6, 64, 128)
    (
        delta, head_grad, hidden, enc_slope, pooled, hidden_mid, mid_slope, state,
        tail_lo, tail_hi,
    ) = call(
        forward_body,
        [
            sds((2, 24, 32, 128), BF16),
            sds((8, 32), F32),
            sds((4, 24, 32, 128), BF16),
            sds((4, 24, 32, 128), F32),
            sds((2, 6, 32, 128), BF16),
            sds((2, 6, 64, 128), BF16),
            sds((2, 6, 64, 128), F32),
            sds((4, 24, 8, 128), F32),
            sds((96, 128), BF16),
            sds((96, 128), BF16),
        ],
        [],
        (dec_pre, cotangent, out_kernel, enc_pre, state_now, mid_blocks, pool),
        600 << 20, 16,
    )


    def column(at, tail):
        rows = (got1[at], face1[at], delta[0, at], delta[1, at], face2[at], got2[at], tail)
        return jnp.concatenate([v.reshape(-1, 128) for v in rows])

    ends = column(slice(0, 3), tail_lo), column(slice(21, 24), tail_hi)
    rim1, rim2 = swaps(*in_order("gy", *ends), "gy")
    acc, wide, win, up, wskip, wmid, wup = call(
        inner_body,
        [
            sds((4, 26, 32, 128), F32),
            sds((6, 24, 96, 128), BF16),
            sds((864, 1024), BF16),
            sds((64, 1024), F32),
            sds((96, 288), BF16),
            sds((288, 192), BF16),
            sds((64, 864), BF16),
        ],
        [],
        (got1, face1, delta, face2, got2, pool, dec_w, mid_w),
        3 << 30, 24,
    )
    edge, rim_wide, rim_win, mid_wide, back, face1, face2 = call(
        outer_body,
        [
            sds((4, 2, 32, 128), F32),
            sds((6, 2, 96, 128), BF16),
            sds((864, 768), BF16),
            sds((192, 1792), BF16),
            sds((2, 6, 32, 128), F32),
            sds((592, 128), BF16),
            sds((592, 128), BF16),
        ],
        [pltpu.VMEM((4, 6, 32, 128), F32), pltpu.VMEM((2, 672, 128), BF16)],
        (rim1, rim2, wide, up, mid_slope, state, pooled, pool, wup, wskip, wmid),
        1 << 30, 24,
    )
    got1, got2 = swaps(face1, face2, "gx")
    dec_rows, mid_grad = call(
        dec_grad_body,
        [sds((736, 128), BF16), sds((288, 192), F32)],
        [pltpu.VMEM((4, 28, 32, 128), BF16), pltpu.VMEM((288, 96), F32)],
        (wide, rim_wide, hidden, win, rim_win, hidden_mid, head_grad, pooled, mid_wide),
        3 << 30, 20,
    )
    dec_rows, mid_grad, got1, got2 = lax.optimization_barrier((dec_rows, mid_grad, got1, got2))
    rows, own, face1, face2, edge_lo, edge_hi = call(
        encoder_body,
        [
            sds((1280, 128), BF16),
            sds((4, 24, 8, 128), F32),
            sds((208, 128), BF16),
            sds((208, 128), BF16),
            sds((4, 8, 128), F32),
            sds((4, 8, 128), F32),
        ],
        [
            pltpu.VMEM((96, 24 * 512), BF16),
            pltpu.VMEM((384, 256), F32),
            pltpu.VMEM((6, 26, 8, 128), F32),
            pltpu.VMEM((72, 96), F32),
            pltpu.VMEM((544, 128), BF16),
            pltpu.VMEM((6, 26, 8, 128), F32),
            pltpu.VMEM((72, 96), F32),
            pltpu.VMEM((2, 592, 128), BF16),
            pltpu.SemaphoreType.DMA((3, 1)),
        ],
        (
            acc, edge, back, rim1, rim2, got1, got2, enc_slope, enc_w, up_matrix(),
            mid_wide, mid_grad, state, dec_rows,
        ),
        2 << 30, 24, far_outs=1,
    )
    last1, last2 = swaps(face1, face2, "gx")

    axes = ("dp", "gx", "gy")
    count = lax.axis_size(axes)
    share = 1280 // count
    shape = (count, share // 2, 2, 128)
    pieces = lax.all_to_all(rows.reshape(shape), axes, 0, 0).reshape(1280, 128)
    (shares,) = call(
        functools.partial(share_body, share), [sds((1280, 128), BF16)], [], (pieces,), 1 << 20, 8
    )
    shares, last1, last2 = lax.optimization_barrier((shares, last1, last2))
    rows = lax.all_to_all(shares.reshape(shape), axes, 0, 0).reshape(1280, 128)
    col1, col2 = call(
        corner_body, [sds((32, 128), BF16)] * 2, [], (edge_lo, edge_hi, last1, last2), 1 << 16, 4
    )
    end1, end2 = swaps(col1, col2, "gy")
    genc, gmid, gdec, ghead = call(
        functools.partial(unpack_body, grad_scale),
        [sds((3, 3, 3, 8, 32), F32), sds((3, 3, 3, 32, 64), F32), sds((3, 3, 3, 32, 96), F32), sds((8, 32), F32)],
        [
            pltpu.VMEM((3, 3, 3, 8, 32), F32),
            pltpu.VMEM((3, 3, 3, 32, 64), F32),
            pltpu.VMEM((3, 3, 3, 32, 96), F32),
            pltpu.VMEM((8, 32), F32),
            pltpu.SemaphoreType.DMA((5, 2)),
        ],
        (rows,),
        1 << 20, 12, far_outs=4,
    )
    genc, end1, end2 = lax.optimization_barrier((genc, end1, end2))
    (state_grad,) = call(
        final_body,
        [sds((8, 4, 24, 128), BF16)],
        [],
        (cotangent, own, last1, last2, end1, end2),
        1 << 20, 8,
    )
    return (
        state_grad[None],
        genc.transpose(4, 3, 0, 1, 2),
        gmid.transpose(4, 3, 0, 1, 2),
        gdec.transpose(3, 4, 0, 1, 2),
        ghead,
    )


def solution(mesh):
    grid = P("dp", None, "gx", "gy", None)
    return jax.shard_map(
        on_device,
        mesh=mesh,
        in_specs=(grid,) * 5 + (P(),) * 4,
        out_specs=(grid, P(), P(), P(), P()),
        check_vma=False,
    )
```

```python
import functools
import math

import jax
import jax.numpy as jnp
import numpy as np
from jax import lax
from jax.experimental import pallas as pl
from jax.experimental.pallas import tpu as pltpu
from jax.sharding import PartitionSpec as P

F32 = jnp.float32
BF16 = jnp.bfloat16


VMEM = pl.BlockSpec(memory_space=pltpu.VMEM)
HBM = pl.BlockSpec(memory_space=pltpu.HBM)


def call(body, outs, scratch, args, flops, limit, far=0, far_outs=0):
    return pl.pallas_call(
        body,
        out_shape=outs,
        in_specs=[HBM] * far + [VMEM] * (len(args) - far),
        out_specs=[HBM] * far_outs + [VMEM] * (len(outs) - far_outs),
        scratch_shapes=scratch,
        compiler_params=pltpu.CompilerParams(vmem_limit_bytes=limit << 20),
        cost_estimate=pl.CostEstimate(flops=flops, bytes_accessed=4 << 20, transcendentals=0),
    )(*args)


def fetch(pairs, sems):
    copies = [pltpu.make_async_copy(src, dst, sems.at[i]) for i, (src, dst) in enumerate(pairs)]
    for copy in copies:
        copy.start()
    return [copy.wait for copy in copies]


def sds(shape, dtype):
    return jax.ShapeDtypeStruct(shape, dtype)


def dot(a, b):
    return lax.dot_general(a, b, (((1,), (0,)), ((), ())), preferred_element_type=F32)


def dot_tn(a, b):
    return lax.dot_general(a, b, (((0,), (0,)), ((), ())), preferred_element_type=F32)


def dot_nt(a, b):
    return lax.dot_general(a, b, (((1,), (1,)), ((), ())), preferred_element_type=F32)


def sigmoid(v):
    return 0.5 + 0.5 * jnp.tanh(0.5 * v)


def slope(v, s):
    return s * (1.0 + v * (1.0 - s))


def parity(axis):
    return jnp.bitwise_and(lax.axis_index(axis), 1)


def in_order(axis, first, second):
    odd = parity(axis) == 1
    return jnp.where(odd, first, second), jnp.where(odd, second, first)


def lane_ids(shape):
    return lax.broadcasted_iota(jnp.int32, shape, len(shape) - 1)


def shifts(v, period):
    lane = jnp.bitwise_and(lane_ids(v.shape), period - 1)
    axis = v.ndim - 1
    size = v.shape[-1]
    back = jnp.where(lane == period - 1, 0.0, pltpu.roll(v, size - 1, axis))
    ahead = jnp.where(lane == 0, 0.0, pltpu.roll(v, 1, axis))
    return back, v, ahead


def delta_plane(dec, cot, head):
    pre = jnp.swapaxes(dec.astype(F32), 0, 1)
    cot = jnp.swapaxes(cot.astype(F32), 0, 1)
    cot_lanes = jnp.concatenate([cot[y] for y in range(24)], axis=1).astype(BF16)
    back = dot_tn(head, cot_lanes)
    back = jnp.stack([back[:, y * 128 : y * 128 + 128] for y in range(24)], axis=0)
    s = sigmoid(pre)
    return (back * slope(pre, s)).astype(BF16), cot_lanes, pre * s


def face_body(dec_far, cot_far, head_far, first_far, second_far, dec_ref, cot_ref, head_ref, delta_ref, sems, out_sems):
    odd = parity("gx")
    planes = (3 - 3 * odd, 3 * odd)
    pairs = [(head_far, head_ref)]
    for i, x in enumerate(planes):
        pairs += [(cot_far.at[:, x], cot_ref.at[i]), (dec_far.at[:, x], dec_ref.at[i])]
    waits = fetch(pairs, sems)
    waits[0]()
    writes = []
    for i, far in enumerate((first_far, second_far)):
        waits[2 * i + 1]()
        waits[2 * i + 2]()
        delta_ref[i] = delta_plane(dec_ref[i], cot_ref[i], head_ref[...])[0]
        writes += fetch([(delta_ref.at[i], far)], out_sems.at[i])
    for wait in writes:
        wait()


def forward_body(
    dec_ref, cot_ref, head_ref, enc_ref, state_ref, mid_ref, pool_ref,
    delta_ref, head_grad_ref, hid_ref, slope_ref, pooled_ref, hmid_ref, mslope_ref, st_ref, ylo_ref, yhi_ref,
):
    total = jnp.zeros((8, 32), F32)
    for x in range(4):
        delta, cot_lanes, decoded = delta_plane(dec_ref[:, x], cot_ref[:, x], head_ref[...])
        if x in (1, 2):
            delta_ref[x - 1] = delta
        decoded = jnp.concatenate([decoded[y] for y in range(24)], axis=1).astype(BF16)
        total = total + dot_nt(cot_lanes, decoded)
    head_grad_ref[...] = total
    low_rows, high_rows = [], []
    for x in range(4):
        pre = jnp.swapaxes(enc_ref[:, x].astype(F32), 0, 1)
        s = sigmoid(pre)
        hid_ref[x] = (pre * s).astype(BF16)
        slope_ref[x] = slope(pre, s)
        state = jnp.swapaxes(state_ref[:, x].astype(F32), 0, 1)
        st_ref[x] = state
        low_rows.append(state[0])
        high_rows.append(state[23])
    ylo_ref[64:96, :] = jnp.concatenate(low_rows, axis=0).astype(BF16)
    yhi_ref[64:96, :] = jnp.concatenate(high_rows, axis=0).astype(BF16)
    tilts = {}
    for bx in range(2):
        for m in range(6):
            acc = None
            for ex in range(2):
                for ey in range(2):
                    pair = jnp.concatenate(
                        [hid_ref[2 * bx + ex, 4 * m + ey], hid_ref[2 * bx + ex, 4 * m + 2 + ey]], axis=1
                    )
                    part = dot(pair, pool_ref[:, 128:256])
                    acc = part if acc is None else acc + part
            pooled = (acc * 0.125).astype(BF16)
            pooled_ref[bx, m] = pooled
            pre = mid_ref[bx, m].astype(F32)
            s = sigmoid(pre)
            hmid_ref[bx, m] = (pre * s).astype(BF16)
            tilts[bx, m] = slope(pre, s)
            mslope_ref[bx, m] = tilts[bx, m]
    lower = lane_ids((64, 128)) < 64
    ylo_ref[0:64, :] = jnp.where(lower, tilts[0, 0], pltpu.roll(tilts[1, 0], 64, 1)).astype(BF16)
    yhi_ref[0:64, :] = jnp.where(lower, pltpu.roll(tilts[0, 5], 64, 1), tilts[1, 5]).astype(BF16)


def window_sums(rows_of, pool, put):
    got = dot(
        jnp.concatenate([jnp.concatenate([rows_of(x, j) for j in range(4)], axis=0) for x in range(6)], axis=0), pool
    )
    sums = []
    for x in range(6):
        at = [got[x * 128 + j * 32 : x * 128 + j * 32 + 32] for j in range(4)]
        sums.append([at[j] + at[j + 1] for j in (2, 1, 0)])
    for bx in range(2):
        for a, kx in enumerate((-1, 0, 1)):
            for b in range(3):
                both = (sums[2 * bx - kx + 1][b] + sums[2 * bx - kx + 2][b]).astype(BF16)
                for c in range(3):
                    put(bx, ((a * 3 + b) * 3 + c) * 32, both[:, c * 128 : c * 128 + 128])


def stack_of(row):
    return jnp.concatenate(
        [jnp.concatenate([row(x + 1 - kx) for x in range(4)], axis=1) for kx in (-1, 0, 1)], axis=0
    )


def skip_weights(w_ref):
    parts = [
        jnp.concatenate([w_ref[a, b].astype(F32).reshape(96, 96)[:, 64:96] for b in range(3)], axis=1)
        for a in range(3)
    ]
    return jnp.concatenate(parts, axis=0).T.astype(BF16)


def inner_body(got1_ref, face1_ref, delta_ref, face2_ref, got2_ref, pool_ref, w_ref, wmid_ref, acc_ref, wide_ref, win_ref, up_ref, wskip_ref, wm_ref, wup_ref):
    def put(x, v):
        parts = shifts(v.astype(F32).reshape(768, 128), 128)
        for a in range(3):
            wide_ref[x, :, a * 32 : a * 32 + 32, :] = parts[a].astype(BF16).reshape(24, 32, 128)

    odd = parity("gx")
    put(5 - 5 * odd, got1_ref[...])
    put(4 - 3 * odd, face1_ref[...])
    put(2, delta_ref[0])
    put(3, delta_ref[1])
    put(1 + 3 * odd, face2_ref[...])
    put(5 * odd, got2_ref[...])
    wskip_ref[...] = skip_weights(w_ref)
    acc_ref[...] = jnp.zeros(acc_ref.shape, F32)

    def step(i, carry):
        y = 4 * i
        out = dot(
            wskip_ref[...],
            jnp.concatenate([stack_of(lambda x, j=j: wide_ref[x, y + j]) for j in range(4)], axis=1),
        )
        for x in range(4):
            for r in range(6):
                parts = [
                    out[b * 32 : b * 32 + 32, ((r - b) * 4 + x) * 128 : ((r - b) * 4 + x) * 128 + 128]
                    for b in range(3)
                    if 0 <= r - b < 4
                ]
                acc_ref[x, y + r] += sum(parts[1:], parts[0])
        return carry

    lax.fori_loop(0, 6, step, 0, unroll=2)
    for m in range(1, 5):

        def rows_of(x, j):
            return jnp.concatenate(
                [wide_ref[x, 4 * m + j - 1, 32:64, :], wide_ref[x, 4 * m + j + 1, 32:64, :]], axis=1
            )

        def put_window(bx, row, v):
            lane = (bx * 4 + m - 1) * 128
            win_ref[row : row + 32, lane : lane + 128] = v

        window_sums(rows_of, pool_ref[...], put_window)
    wup_ref[...] = w_ref[...].reshape(864, 96).astype(F32).T[:64].astype(BF16)
    up_ref[...] = dot(wup_ref[...], win_ref[...])
    for a in range(3):
        for b in range(3):
            at = (a * 3 + b) * 32
            parts = [wmid_ref[a, b, c].astype(F32) for c in range(3)]
            wm_ref[at : at + 32, :] = jnp.concatenate(parts, axis=1).astype(BF16)


def outer_body(
    got1_ref, got2_ref, wide_ref, up_ref, mslope_ref, st_ref, pooled_ref, pool_ref, wup_ref, wm_ref,
    win_ref, mid_ref, back_ref, face1_ref, face2_ref,
    total_ref, got_ref,
):
    odd_x, odd_y = parity("gx"), parity("gy")
    got_ref[1 - odd_y] = got1_ref[...]
    got_ref[odd_y] = got2_ref[...]

    def row(x, y):
        if 0 <= y <= 23:
            return wide_ref[x, y, 32:64, :]
        slot = x + (1 - odd_x) * (5, 3, 0, 0, -3, -5)[x]
        at = (slot * 3 + (y + 3 if y < 0 else y - 24)) * 32
        return got_ref[0 if y < 0 else 1, pl.ds(pl.multiple_of(at, 32), 32), :]

    for i, (left, right) in enumerate(((-1, 1), (19, 21), (23, -3))):

        def rows_of(x, j):
            return jnp.concatenate([row(x, left + j), row(x, right + j)], axis=1)

        def put_window(bx, r, v):
            lane = (bx * 3 + i) * 128
            win_ref[r : r + 32, lane : lane + 128] = v

        window_sums(rows_of, pool_ref[...], put_window)
    rim_up = dot(wup_ref[...], win_ref[...])

    upper = lane_ids((64, 128)) >= 64
    before = got_ref[0, 576:640, :].astype(F32)
    after = got_ref[1, 576:640, :].astype(F32)
    rim_tilt = (
        jnp.where(upper, pltpu.roll(before, 64, 1), after),
        jnp.where(upper, before, pltpu.roll(after, 64, 1)),
    )
    for bx in range(2):
        for m in range(7):
            if 1 <= m <= 4:
                lane = (bx * 4 + m - 1) * 128
                v = up_ref[:, lane : lane + 128]
            else:
                lane = (bx * 3 + (0, 5, 6).index(m)) * 128
                v = rim_up[:, lane : lane + 128]
            tilt = rim_tilt[bx] if m == 6 else mslope_ref[bx, m]
            delta = (v * tilt).astype(BF16).astype(F32)
            lane = (bx * 7 + m) * 128
            for a, part in enumerate(shifts(delta, 64)):
                mid_ref[a * 64 : a * 64 + 64, lane : lane + 128] = part.astype(BF16)

    out = dot(wm_ref[...], mid_ref[...])
    upper = lane_ids((32, 128)) >= 64

    def term(a, b, x, m):
        if not 0 <= x - a < 2:
            return None
        col = ((x - a) * 7 + m) * 128
        return out[(a * 3 + b) * 32 : (a * 3 + b) * 32 + 32, col : col + 128]

    def tap_sum(b, x, m):
        parts = [v for v in (term(a, b, x, m) for a in range(3)) if v is not None]
        return sum(parts[1:], parts[0])

    for x in range(4):
        downs = [pltpu.roll(tap_sum(0, x, m), 64, 1) for m in range(7)]
        ups = [pltpu.roll(tap_sum(2, x, m), 64, 1) for m in range(7)]
        for m in range(6):
            low = ups[(m + 6) % 7] + downs[m]
            high = ups[m] + downs[m + 1]
            total_ref[x, m] = tap_sum(1, x, m) + jnp.where(upper, high, low)
    back_ref[...] = total_ref[1:3, 0:6]
    before = got_ref[0, 640:672, :].astype(F32)
    after = got_ref[1, 640:672, :].astype(F32)
    for face_ref, last in ((face1_ref, 1 - odd_x), (face2_ref, odd_x)):
        face_ref[0:192, :] = total_ref[3 * last].astype(BF16).reshape(192, 128)
        face_ref[192:384, :] = pooled_ref[last].reshape(192, 128)
        rows = (
            jnp.where(last == 1, before[24:32], before[0:8]),
            st_ref[3 * last].reshape(192, 128),
            jnp.where(last == 1, after[24:32], after[0:8]),
        )
        face_ref[384:592, :] = jnp.concatenate(rows, axis=0).astype(BF16)


def hidden_rows(hid_ref, ys):
    def tap(x, y):
        return hid_ref[x, y + 2]

    return jnp.concatenate(
        [jnp.concatenate([tap(x, y + b - 1) for y in ys for x in range(4)], axis=1) for b in range(3)], axis=0
    )


def pooled_taps(blocks):
    blocks = blocks + [jnp.zeros((32, 128), F32)]
    lower = lane_ids((32, 128)) < 64
    turned = [pltpu.roll(v, 64, 1) for v in blocks]
    taps = (
        [jnp.where(lower, turned[(m + 6) % 7], turned[m]) for m in range(7)],
        blocks,
        [jnp.where(lower, turned[m], turned[(m + 1) % 7]) for m in range(7)],
    )
    return jnp.concatenate([jnp.concatenate(v, axis=1) for v in taps], axis=0).astype(BF16)


def dec_grad_body(
    got1_ref, got2_ref, wskip_ref, wide_ref, hid_ref, win_ref, rim_win_ref, hmid_ref, head_ref, pooled_ref, mid_ref,
    edge_ref, rows_ref, gmid_ref, hpad_ref, skip_ref, rim_ref, got_ref,
):
    odd_x, odd_y = parity("gx"), parity("gy")
    got_ref[1 - odd_y] = got1_ref[...]
    got_ref[odd_y] = got2_ref[...]

    def row(x, y):
        slot = x + (1 - odd_x) * (5, 3, 0, 0, -3, -5)[x]
        at = (slot * 3 + (2 if y < 0 else 0)) * 32
        return got_ref[0 if y < 0 else 1, pl.ds(pl.multiple_of(at, 32), 32), :]

    for x in range(6):
        v = jnp.concatenate([row(x, -1), row(x, 24)], axis=0).astype(F32)
        parts = shifts(v, 128)
        for a in range(3):
            rim_ref[x, :, a * 32 : a * 32 + 32, :] = parts[a].astype(BF16).reshape(2, 32, 128)
    outs = [dot(wskip_ref[...], stack_of(lambda x, r=r: rim_ref[x, r])) for r in range(2)]
    for x in range(4):
        at = slice(x * 128, x * 128 + 128)
        edge_ref[x, 0] = outs[0][64:96, at]
        edge_ref[x, 1] = outs[1][0:32, at]

    blank = jnp.zeros((2, 32, 128), BF16)
    for x in range(4):
        hpad_ref[x, 0:2] = blank
        hpad_ref[x, 26:28] = blank
        hpad_ref[x, 2:26] = hid_ref[x]
    rims = jnp.concatenate([stack_of(lambda x, r=r: rim_ref[x, r]) for r in (0, 1)], axis=1)
    skip_ref[...] = dot_nt(rims, hidden_rows(hpad_ref, (-1, 24)))

    def step(i, carry):
        y = 4 * i
        rows = jnp.concatenate([stack_of(lambda x, j=j: wide_ref[x, y + j]) for j in range(4)], axis=1)
        skip_ref[...] += dot_nt(rows, hidden_rows(hpad_ref, [y + j for j in range(4)]))
        return carry

    lax.fori_loop(0, 6, step, 0, unroll=2)
    rows_ref[0:288, :] = jnp.concatenate([skip_ref[...], jnp.zeros((288, 32), F32)], axis=1).astype(BF16)

    def side(bx, m):
        if 1 <= m <= 4:
            at = (bx * 4 + m - 1) * 128
            return win_ref[:, at : at + 128]
        at = (bx * 3 + (0 if m == 0 else 1)) * 128
        return rim_win_ref[:, at : at + 128]

    order = [(bx, m) for bx in range(2) for m in range(6)]
    windows = jnp.concatenate([side(bx, m) for bx, m in order], axis=1)
    hmid = jnp.concatenate([hmid_ref[bx, m] for bx, m in order], axis=1)
    lift = dot_nt(windows, hmid)
    rows_ref[288:720, :] = jnp.concatenate([lift[0:432], lift[432:864]], axis=1).astype(BF16)
    rows_ref[720:736, :] = jnp.concatenate(
        [jnp.concatenate([head_ref[...], jnp.zeros((8, 96), F32)], axis=1), jnp.zeros((8, 128), F32)], axis=0
    ).astype(BF16)
    taps = [pooled_taps([pooled_ref[bx, m].astype(F32) for m in range(6)]) for bx in range(2)]
    first, second = mid_ref[:, 0:896], mid_ref[:, 896:1792]
    gmid_ref[0:96, :] = dot_nt(taps[0], second)
    gmid_ref[96:192, :] = dot_nt(taps[0], first) + dot_nt(taps[1], second)
    gmid_ref[192:288, :] = dot_nt(taps[1], first)


def encoder_body(
    acc_ref, edge_ref, back_ref, rim1_ref, rim2_ref, got1_ref, got2_ref, slope_ref, w_ref, up_ref,
    mid_ref, gmid_ref, st_ref, dec_ref,
    rows_far, own_ref, face1_ref, face2_ref, edge_lo_ref, edge_hi_ref,
    enc_ref, wide_ref, total_ref, we_ref, rows_ref, sext_ref, sum_ref, got_ref, sems,
):
    odd_x = parity("gx")
    got_ref[1 - odd_x] = got1_ref[...]
    got_ref[odd_x] = got2_ref[...]
    got_lo_ref, got_hi_ref = got_ref.at[0], got_ref.at[1]
    writes = fetch([(dec_ref, rows_far.at[0:736])], sems.at[0])

    def beyond(ref):
        side = ref[192:384, :].astype(F32)
        return pooled_taps([side[m * 32 : m * 32 + 32] for m in range(6)])

    gmid = jnp.concatenate(
        [
            gmid_ref[0:96, :] + dot_nt(beyond(got_lo_ref), mid_ref[:, 0:896]),
            gmid_ref[96:192, :],
            gmid_ref[192:288, :] + dot_nt(beyond(got_hi_ref), mid_ref[:, 896:1792]),
        ],
        axis=0,
    )
    rows_ref[0:288, :] = gmid[:, :128].astype(BF16)
    rows_ref[288:432, :] = jnp.concatenate([gmid[:144, 128:], gmid[144:, 128:]], axis=1).astype(BF16)
    writes += fetch([(rows_ref.at[0:432], rows_far.at[736:1168])], sems.at[1])

    sext_ref[1:5, 1:25] = st_ref[...]
    sext_ref[0] = got_lo_ref[384:592, :].astype(F32).reshape(26, 8, 128)
    sext_ref[5] = got_hi_ref[384:592, :].astype(F32).reshape(26, 8, 128)
    before, after = in_order("gy", rim1_ref[640:672, :].astype(F32), rim2_ref[640:672, :].astype(F32))
    for x in range(4):
        sext_ref[x + 1, 0] = before[x * 8 : x * 8 + 8]
        sext_ref[x + 1, 25] = after[x * 8 : x * 8 + 8]

    whole = [back_ref[bx].reshape(192, 128) for bx in range(2)]
    whole = [v + ref[0:192, :].astype(F32) for v, ref in zip(whole, (got_lo_ref, got_hi_ref))]
    whole = jnp.concatenate(whole, axis=0) * 0.125
    high = whole.astype(BF16)
    low = (whole - high.astype(F32)).astype(BF16)
    wide_ref[...] = dot(jnp.concatenate([high, low], axis=1), up_ref[...])
    for bx in range(2):
        for m in range(6):
            at = (bx * 6 + m) * 32
            for half in range(2):
                fine = wide_ref[at : at + 32, half * 128 : half * 128 + 128]
                for ey in range(2):
                    y = 4 * m + 2 * half + ey
                    for ex in range(2):
                        x = 2 * bx + ex
                        sum_in = acc_ref[x, y + 1] + fine
                        if y in (0, 23):
                            sum_in = sum_in + edge_ref[x, (0, 23).index(y)]
                        delta = (sum_in * slope_ref[x, y]).astype(BF16).astype(F32)
                        lane = (y * 4 + x) * 128
                        for c, part in enumerate(shifts(delta, 128)):
                            enc_ref[c * 32 : c * 32 + 32, lane : lane + 128] = part.astype(BF16)

    for a in range(3):
        for b in range(3):
            at = (a * 3 + b) * 8
            we_ref[at : at + 8, :] = jnp.concatenate([w_ref[a, b, c].astype(F32) for c in range(3)], axis=1)
    w = we_ref[...].astype(BF16)
    total_ref[...] = jnp.zeros(total_ref.shape, F32)
    sum_ref[...] = jnp.zeros(sum_ref.shape, F32)

    def step(i, carry):
        y = 4 * i
        delta = enc_ref[:, pl.ds(pl.multiple_of(y * 512, 2048), 2048)]
        state = jnp.concatenate(
            [
                jnp.concatenate([sext_ref[x + a, y + j + b] for j in range(4) for x in range(4)], axis=1)
                for a in range(3)
                for b in range(3)
            ],
            axis=0,
        ).astype(BF16)
        sum_ref[...] += dot_nt(state, delta)
        out = dot(w, delta)
        for x in range(6):
            for r in range(6):
                parts = []
                for a in range(3):
                    for b in range(3):
                        j, own = r - b, x - a
                        if 0 <= j < 4 and 0 <= own < 4:
                            row, lane = (a * 3 + b) * 8, (j * 4 + own) * 128
                            parts.append(out[row : row + 8, lane : lane + 128])
                total_ref[x, y + r] += sum(parts[1:], parts[0])
        return carry

    lax.fori_loop(0, 6, step, 0, unroll=6)
    genc = jnp.concatenate([sum_ref[...], jnp.zeros((72, 32), F32)], axis=1)
    rows_ref[432:544, :] = jnp.concatenate([genc, jnp.zeros((40, 128), F32)], axis=0).astype(BF16)
    writes += fetch([(rows_ref.at[432:544], rows_far.at[1168:1280])], sems.at[2])
    own_ref[...] = total_ref[1:5, 1:25]
    face1_ref[...] = total_ref[5 - 5 * odd_x].reshape(208, 128).astype(BF16)
    face2_ref[...] = total_ref[5 * odd_x].reshape(208, 128).astype(BF16)
    edge_lo_ref[...] = total_ref[1:5, 0]
    edge_hi_ref[...] = total_ref[1:5, 25]
    for wait in writes:
        wait()


def corner_body(edge_lo_ref, edge_hi_ref, got1_ref, got2_ref, col1_ref, col2_ref):
    before, after = in_order("gx", got1_ref[...].astype(F32), got2_ref[...].astype(F32))
    cols = []
    for edge_ref, at in ((edge_lo_ref, 0), (edge_hi_ref, 200)):
        rows = [edge_ref[0] + before[at : at + 8], edge_ref[1], edge_ref[2], edge_ref[3] + after[at : at + 8]]
        cols.append(jnp.concatenate(rows, axis=0))
    first, second = in_order("gy", *cols)
    col1_ref[...] = first.astype(BF16)
    col2_ref[...] = second.astype(BF16)


def final_body(cot_ref, own_ref, got1_ref, got2_ref, end1_ref, end2_ref, grad_ref):
    sides = in_order("gx", got1_ref[...].astype(F32), got2_ref[...].astype(F32))
    before, after = in_order("gy", end1_ref[...].astype(F32), end2_ref[...].astype(F32))
    for x in range(4):
        total = own_ref[x]
        if x in (0, 3):
            total = total + sides[x // 3][8:200].reshape(24, 8, 128)
        at = slice(x * 8, x * 8 + 8)
        ends = [before[at][None], jnp.zeros((22, 8, 128), F32), after[at][None]]
        total = total + jnp.concatenate(ends, axis=0)
        grad_ref[:, x] = (cot_ref[:, x].astype(F32) + jnp.swapaxes(total, 0, 1)).astype(BF16)


def share_body(share, pieces_ref, out_ref):
    size = -(-share // 16) * 16
    rows = pieces_ref.shape[0]
    place = lax.broadcasted_iota(jnp.int32, (size, rows), 1)
    piece = ((place.astype(F32) + 0.5) * (1.0 / share)).astype(jnp.int32)
    same = place - piece * share == lax.broadcasted_iota(jnp.int32, (size, rows), 0)
    pick = jnp.where(same, 1.0, 0.0).astype(BF16)
    total = dot(pick, pieces_ref[...]).astype(BF16)
    out_ref[...] = dot_tn(pick, total).astype(BF16)


def unpack_body(
    scale, rows_ref, enc_far, mid_far, dec_far, head_far, enc_ref, mid_ref, dec_ref, head_ref, sems
):
    def rows(at, count):
        return rows_ref[at : at + count, :].astype(F32) * scale

    mid_rest = rows(1024, 144)
    mid_rest = jnp.concatenate([mid_rest[:, :64], mid_rest[:, 64:]], axis=0)
    for a in range(3):
        for b in range(3):
            tap = a * 3 + b
            pair = rows(736 + tap * 32, 32)
            mid_ref[a, b, 0] = pair[:, :64]
            mid_ref[a, b, 1] = pair[:, 64:]
            mid_ref[a, b, 2] = mid_rest[tap * 32 : tap * 32 + 32]
    writes = fetch([(mid_ref, mid_far)], sems.at[0])
    lift = rows(288, 432)
    lift = jnp.concatenate([lift[:, :64], lift[:, 64:]], axis=0)
    for a in range(3):
        skip = [rows((a * 3 + c) * 32, 32) for c in range(3)]
        for b in range(3):
            for c in range(3):
                at = ((a * 3 + b) * 3 + c) * 32
                dec_ref[a, b, c] = jnp.concatenate([lift[at : at + 32], skip[c][:, b * 32 : b * 32 + 32]], axis=1)
        writes += fetch([(dec_ref.at[a], dec_far.at[a])], sems.at[1 + a])
    enc = rows(1168, 80)
    for a in range(3):
        for b in range(3):
            for c in range(3):
                tap = a * 3 + b
                enc_ref[a, b, c] = enc[tap * 8 : tap * 8 + 8, c * 32 : c * 32 + 32]
    head_ref[...] = rows(720, 16)[:8, :32]
    writes += fetch([(enc_ref, enc_far), (head_ref, head_far)], sems.at[4])
    for wait in writes:
        wait()


def pool_matrix():
    table = np.zeros((256, 3, 128), np.float32)
    for c, k in enumerate((-1, 0, 1)):
        for half in range(2):
            for q in range(64):
                for e in range(2):
                    z = 2 * q + e - k
                    if 0 <= z < 128:
                        table[half * 128 + z, c, half * 64 + q] = 1.0
    return jnp.asarray(table.reshape(256, 384), BF16)


def up_matrix():
    table = np.zeros((2, 128, 256), np.float32)
    for half in range(2):
        for z in range(128):
            table[:, half * 64 + z // 2, half * 128 + z] = 1.0
    return jnp.asarray(table.reshape(256, 256), BF16)


def swaps(first, second, axis):
    count = lax.axis_size(axis)
    pairs = [(i, i + 1) for i in range(0, count - 1, 2)], [(i, i + 1) for i in range(1, count - 1, 2)]
    return tuple(
        lax.ppermute(v, axis, ahead + [(b, a) for a, b in ahead]) for v, ahead in zip((first, second), pairs)
    )


def on_device(
    state_now, enc_pre, mid_pre, dec_pre, cotangent, enc_kernel, mid_kernel, dec_kernel, out_kernel
):
    state_now, enc_pre, mid_pre, dec_pre, cotangent = (
        v[0] for v in (state_now, enc_pre, mid_pre, dec_pre, cotangent)
    )
    cells = state_now[0].size * lax.axis_size("gx") * lax.axis_size("gy") * lax.axis_size("dp")
    grad_scale = 1.0 / math.sqrt(cells)
    pool = pool_matrix()
    dec_w = dec_kernel.transpose(2, 3, 4, 0, 1)
    mid_w = mid_kernel.transpose(2, 3, 4, 1, 0)
    enc_w = enc_kernel.transpose(2, 3, 4, 1, 0)

    plane = sds((24, 32, 128), BF16)
    face1, face2 = call(
        face_body,
        [plane, plane],
        [
            pltpu.VMEM((2, 32, 24, 128), BF16),
            pltpu.VMEM((2, 8, 24, 128), BF16),
            pltpu.VMEM((8, 32), BF16),
            pltpu.VMEM((2, 24, 32, 128), BF16),
            pltpu.SemaphoreType.DMA((5,)),
            pltpu.SemaphoreType.DMA((2, 1)),
        ],
        (dec_pre, cotangent, out_kernel),
        200 << 20, 56, far=3, far_outs=2,
    )
    got1, got2 = swaps(face1, face2, "gx")
    mid_blocks = mid_pre.reshape(64, 2, 6, 2, 64).transpose(1, 2, 0, 3, 4).reshape(2, 6, 64, 128)
    (
        delta, head_grad, hidden, enc_slope, pooled, hidden_mid, mid_slope, state,
        tail_lo, tail_hi,
    ) = call(
        forward_body,
        [
            sds((2, 24, 32, 128), BF16),
            sds((8, 32), F32),
            sds((4, 24, 32, 128), BF16),
            sds((4, 24, 32, 128), F32),
            sds((2, 6, 32, 128), BF16),
            sds((2, 6, 64, 128), BF16),
            sds((2, 6, 64, 128), F32),
            sds((4, 24, 8, 128), F32),
            sds((96, 128), BF16),
            sds((96, 128), BF16),
        ],
        [],
        (dec_pre, cotangent, out_kernel, enc_pre, state_now, mid_blocks, pool),
        600 << 20, 16,
    )


    def column(at, tail):
        rows = (got1[at], face1[at], delta[0, at], delta[1, at], face2[at], got2[at], tail)
        return jnp.concatenate([v.reshape(-1, 128) for v in rows])

    ends = column(slice(0, 3), tail_lo), column(slice(21, 24), tail_hi)
    rim1, rim2 = swaps(*in_order("gy", *ends), "gy")
    acc, wide, win, up, wskip, wmid, wup = call(
        inner_body,
        [
            sds((4, 26, 32, 128), F32),
            sds((6, 24, 96, 128), BF16),
            sds((864, 1024), BF16),
            sds((64, 1024), F32),
            sds((96, 288), BF16),
            sds((288, 192), BF16),
            sds((64, 864), BF16),
        ],
        [],
        (got1, face1, delta, face2, got2, pool, dec_w, mid_w),
        3 << 30, 24,
    )
    rim_win, mid_wide, back, face1, face2 = call(
        outer_body,
        [
            sds((864, 768), BF16),
            sds((192, 1792), BF16),
            sds((2, 6, 32, 128), F32),
            sds((592, 128), BF16),
            sds((592, 128), BF16),
        ],
        [pltpu.VMEM((4, 6, 32, 128), F32), pltpu.VMEM((2, 672, 128), BF16)],
        (rim1, rim2, wide, up, mid_slope, state, pooled, pool, wup, wmid),
        1 << 30, 24,
    )
    got1, got2 = swaps(face1, face2, "gx")
    edge, dec_rows, mid_grad = call(
        dec_grad_body,
        [sds((4, 2, 32, 128), F32), sds((736, 128), BF16), sds((288, 192), F32)],
        [
            pltpu.VMEM((4, 28, 32, 128), BF16),
            pltpu.VMEM((288, 96), F32),
            pltpu.VMEM((6, 2, 96, 128), BF16),
            pltpu.VMEM((2, 672, 128), BF16),
        ],
        (rim1, rim2, wskip, wide, hidden, win, rim_win, hidden_mid, head_grad, pooled, mid_wide),
        3 << 30, 20,
    )
    dec_rows, mid_grad, got1, got2 = lax.optimization_barrier((dec_rows, mid_grad, got1, got2))
    rows, own, face1, face2, edge_lo, edge_hi = call(
        encoder_body,
        [
            sds((1280, 128), BF16),
            sds((4, 24, 8, 128), F32),
            sds((208, 128), BF16),
            sds((208, 128), BF16),
            sds((4, 8, 128), F32),
            sds((4, 8, 128), F32),
        ],
        [
            pltpu.VMEM((96, 24 * 512), BF16),
            pltpu.VMEM((384, 256), F32),
            pltpu.VMEM((6, 26, 8, 128), F32),
            pltpu.VMEM((72, 96), F32),
            pltpu.VMEM((544, 128), BF16),
            pltpu.VMEM((6, 26, 8, 128), F32),
            pltpu.VMEM((72, 96), F32),
            pltpu.VMEM((2, 592, 128), BF16),
            pltpu.SemaphoreType.DMA((3, 1)),
        ],
        (
            acc, edge, back, rim1, rim2, got1, got2, enc_slope, enc_w, up_matrix(),
            mid_wide, mid_grad, state, dec_rows,
        ),
        2 << 30, 24, far_outs=1,
    )
    last1, last2 = swaps(face1, face2, "gx")

    axes = ("dp", "gx", "gy")
    count = lax.axis_size(axes)
    share = 1280 // count
    shape = (count, share // 2, 2, 128)
    pieces = lax.all_to_all(rows.reshape(shape), axes, 0, 0).reshape(1280, 128)
    (shares,) = call(
        functools.partial(share_body, share), [sds((1280, 128), BF16)], [], (pieces,), 1 << 20, 8
    )
    shares, last1, last2 = lax.optimization_barrier((shares, last1, last2))
    rows = lax.all_to_all(shares.reshape(shape), axes, 0, 0).reshape(1280, 128)
    col1, col2 = call(
        corner_body, [sds((32, 128), BF16)] * 2, [], (edge_lo, edge_hi, last1, last2), 1 << 16, 4
    )
    end1, end2 = swaps(col1, col2, "gy")
    genc, gmid, gdec, ghead = call(
        functools.partial(unpack_body, grad_scale),
        [sds((3, 3, 3, 8, 32), F32), sds((3, 3, 3, 32, 64), F32), sds((3, 3, 3, 32, 96), F32), sds((8, 32), F32)],
        [
            pltpu.VMEM((3, 3, 3, 8, 32), F32),
            pltpu.VMEM((3, 3, 3, 32, 64), F32),
            pltpu.VMEM((3, 3, 3, 32, 96), F32),
            pltpu.VMEM((8, 32), F32),
            pltpu.SemaphoreType.DMA((5, 2)),
        ],
        (rows,),
        1 << 20, 12, far_outs=4,
    )
    genc, end1, end2 = lax.optimization_barrier((genc, end1, end2))
    (state_grad,) = call(
        final_body,
        [sds((8, 4, 24, 128), BF16)],
        [],
        (cotangent, own, last1, last2, end1, end2),
        1 << 20, 8,
    )
    return (
        state_grad[None],
        genc.transpose(4, 3, 0, 1, 2),
        gmid.transpose(4, 3, 0, 1, 2),
        gdec.transpose(3, 4, 0, 1, 2),
        ghead,
    )


def solution(mesh):
    grid = P("dp", None, "gx", "gy", None)
    return jax.shard_map(
        on_device,
        mesh=mesh,
        in_specs=(grid,) * 5 + (P(),) * 4,
        out_specs=(grid, P(), P(), P(), P()),
        check_vma=False,
    )
```
